256 devices in a mesh: gx: 8 (over z), gy: 8 (over x, core), gz: 4 (over y).
Axes of the slice: x: 4, y: 4, z: 8, core: 2. Of those that a mesh axis runs over, the one named last changes fastest.
Arguments:
- adjoint: bfloat16 [4, 16384, 512], P(None, ('gx', 'gy', 'gz')), may hold values from -6 to 6
- load: bfloat16 [4, 16384, 512], P(None, ('gx', 'gy', 'gz')), may hold values from -4 to 4
- displace: bfloat16 [3, 16384, 512], P(None, ('gx', 'gy', 'gz')), may hold values from -4 to 4
- damage: bfloat16 [16384, 512], P(('gx', 'gy', 'gz')), may hold values from 0 to 0.8984375
- history: bfloat16 [16384, 512], P(('gx', 'gy', 'gz')), may hold values from 0 to 20
- frozen: int32 [16384], P(('gx', 'gy', 'gz')), may hold values 0 or 1
- order: int32 [256, 64], P(('gx', 'gy', 'gz')), may hold values from 0 to 63, each once within a row
Outputs:
- residual: float32 [4, 16384, 512], P(None, ('gx', 'gy', 'gz'))
The draws below stay inside these ranges and needn't reach their ends.
Inputs may be any that keep to these rules, and one draw needn't show every extreme that they name: `order`: each device's row of 64 entries holds every local place once.
All inputs are finite; a program needn't handle non-finite values. No bound on the sum of `frozen` on one device may be relied on, other than what follows from the above.
Results may differ from the reference program's by a relative error of at most 0.00035.
Values sent between devices are 32-bit elements; how exact they have to be, the bound alone decides.
A program may use at most 64 MiB of HBM per device.

```python
import jax
import jax.numpy as jnp
import numpy as np
from jax import lax

P_SIZE = 8
NODES = 512
BX = 1
BY = 4
BZ = 16
EL_DEV = 64
ELEMS = 16384
GRID_X = 64
GRID_Y = 256
GRID_Z = 512
N_GX = 8
N_GY = 8
N_GZ = 4
DEVICES = 256


def touch_ends(values, stream_key, low, largest):
    longest = values.shape.index(max(values.shape))
    spots = []
    for shift in (0, 1):
        where = [jax.random.randint(jax.random.fold_in(stream_key, axis), (), 0, length) for axis, length in enumerate(values.shape)]
        where[longest] = (where[longest] + shift) % values.shape[longest]
        spots.append(tuple(where))
    return values.at[spots[0]].set(low).at[spots[1]].set(largest)


def steps_of(rng, extent, split, smallest, largest):
    def one(dim, shards_of):
        steps = jax.random.uniform(jax.random.fold_in(jax.random.fold_in(rng, 6), dim), (shards_of,), jnp.float32, smallest / len(split), largest / len(split))
        return jnp.repeat(jnp.exp(steps), extent[dim] // shards_of).reshape((-1,) + (1,) * (len(extent) - dim - 1))

    loudness = one(*split[0])
    for cut in split[1:]:
        loudness = loudness * one(*cut)
    return loudness


def bell_draw(own_key, shape, spread, bound, shards=(), kind=jnp.bfloat16):
    entries = jax.random.normal(own_key, shape, jnp.float32) * spread
    if len(shards) > 0:
        entries = steps_of(own_key, shape, shards, -0.22, 0.18) * entries
    return jnp.clip(entries, min=-bound, max=bound).astype(kind)


def setup_inputs(seed: int = 0) -> dict:
    seeds = jax.random.split(jax.random.key(seed), 8)
    adjoint = bell_draw(seeds[0], (4, ELEMS, NODES), 1.0, 6.0, ((1, 256),))
    load = bell_draw(seeds[1], (4, ELEMS, NODES), 0.5, 4.0, ((1, 256),))
    displace = bell_draw(seeds[2], (3, ELEMS, NODES), 0.5, 4.0, ((1, 256),))
    damage = jnp.clip(0.8984375 * jax.random.uniform(seeds[3], (ELEMS, NODES), jnp.float32) ** steps_of(seeds[3], (ELEMS, NODES), ((0, 256),), -0.2, 0.2), 0.0, 0.8984375).astype(jnp.bfloat16)
    history = jnp.clip(20.0 * jax.random.uniform(seeds[4], (ELEMS, NODES), jnp.float32) ** steps_of(seeds[4], (ELEMS, NODES), ((0, 256),), -0.2, 0.2), 0.0, 20.0).astype(jnp.bfloat16)
    frozen = touch_ends((jax.random.randint(seeds[5], (ELEMS,), 0, 2) < 1).astype(jnp.int32), jax.random.fold_in(seeds[5], 1), 0, 1)
    order = jax.vmap(lambda own: jax.random.permutation(own, EL_DEV))(jax.random.split(seeds[6], DEVICES)).reshape((DEVICES, EL_DEV)).astype(jnp.int32)
    return {"adjoint": adjoint, "load": load, "displace": displace, "damage": damage, "history": history, "frozen": frozen, "order": order}


lame_lambda = 0.15
lame_mu = 0.1
gc_length = 0.3
gc_inverse = 40.0
residual_stiff = 0.001
relaxation = 0.5
sym_pairs = ((0, 0), (1, 1), (2, 2), (0, 1), (0, 2), (1, 2))
tensor_slot = ((0, 3, 4), (3, 1, 5), (4, 5, 2))
gll_points = (-1.0, -0.8717401485096066, -0.5917001814331423, -0.2092992179024789, 0.2092992179024789, 0.5917001814331423, 0.8717401485096066, 1.0)


def legendre_at(points, degree):
    values = []
    for point in points:
        previous = 1.0
        current = point
        for level in range(1, degree):
            following = ((2 * level + 1) * point * current - level * previous) / (level + 1)
            previous = current
            current = following
        values.append(current)
    return values


def gll_tables():
    degree = 7
    points = list(gll_points)
    legendre_vals = legendre_at(points, degree)
    weights = [2.0 / (degree * (degree + 1) * entry * entry) for entry in legendre_vals]
    derivative = []
    for row_index in range(degree + 1):
        row_vals = []
        for col_index in range(degree + 1):
            if row_index != col_index:
                row_vals.append(legendre_vals[row_index] / (legendre_vals[col_index] * (points[row_index] - points[col_index])))
            else:
                row_vals.append(0.0)
        derivative.append(row_vals)
    derivative[0][0] = -degree * (degree + 1) / 4.0
    derivative[degree][degree] = degree * (degree + 1) / 4.0
    return np.array(weights), np.array(derivative)


def along_axis(source, small, spatial_axis):
    fields_n, size_x, size_y, size_z = source.shape
    if spatial_axis == 0:
        shaped = source.reshape(fields_n, size_x // 8, 8, size_y, size_z)
        result = jnp.einsum("ab,fubyz->fuayz", small, shaped, precision=lax.Precision.HIGHEST)
    elif spatial_axis == 1:
        shaped = source.reshape(fields_n, size_x, size_y // 8, 8, size_z)
        result = jnp.einsum("ab,fxubz->fxuaz", small, shaped, precision=lax.Precision.HIGHEST)
    else:
        shaped = source.reshape(fields_n, size_x, size_y, size_z // 8, 8)
        result = jnp.einsum("ab,fxyub->fxyua", small, shaped, precision=lax.Precision.HIGHEST)
    return result.reshape(source.shape)


def sym_strain(grads):
    return [0.5 * (grads[second][first] + grads[first][second]) for first, second in sym_pairs]


def stress_of(strain):
    trace_sum = strain[0] + strain[1] + strain[2]
    normal_part = [lame_lambda * trace_sum + 2.0 * lame_mu * strain[slot_index] for slot_index in range(3)]
    shear_part = [2.0 * lame_mu * strain[slot_index] for slot_index in range(3, 6)]
    return normal_part + shear_part


def contract(left_side, right_side):
    diagonal_sum = left_side[0] * right_side[0] + left_side[1] * right_side[1] + left_side[2] * right_side[2]
    return diagonal_sum + 2.0 * (left_side[3] * right_side[3] + left_side[4] * right_side[4] + left_side[5] * right_side[5])


def state_terms(displace, damage, history, frozen, weight_brick, small):
    grads = [along_axis(displace, small, spatial_axis) for spatial_axis in range(3)]
    strain = sym_strain(grads)
    stress = stress_of(strain)
    energy = 0.5 * contract(stress, strain)
    loading = 1.0 - frozen
    driving = frozen * history + loading * energy
    intact = 1.0 - damage
    weighted_g = weight_brick * (intact * intact + residual_stiff)
    slope_weight = -2.0 * intact * weight_brick
    scaled = [slope_weight * entry for entry in stress]
    coupled = [loading * entry for entry in scaled]
    reaction = weight_brick * (gc_inverse + 2.0 * driving)
    return weighted_g, scaled, coupled, reaction


def apply_transposed(adjoint, state, weight_brick, small):
    weighted_g, scaled, coupled, reaction = state
    grads = [along_axis(adjoint, small, spatial_axis) for spatial_axis in range(3)]
    strain = sym_strain(grads)
    stress = stress_of(strain)
    damage_adj = adjoint[3]
    tensor = [weighted_g * stress[slot_index] + coupled[slot_index] * damage_adj for slot_index in range(6)]
    result = None
    for spatial_axis in range(3):
        stacked = jnp.stack([tensor[tensor_slot[0][spatial_axis]], tensor[tensor_slot[1][spatial_axis]], tensor[tensor_slot[2][spatial_axis]], gc_length * weight_brick * grads[spatial_axis][3]])
        term_part = along_axis(stacked, small.T, spatial_axis)
        result = term_part if result is None else result + term_part
    nodal_term = contract(scaled, strain) + reaction * damage_adj
    return jnp.concatenate([result[:3], (result[3] + nodal_term)[None]], axis=0)


def fold_axis(padded, spatial_axis, length):
    dim_index = spatial_axis + 1
    center = lax.slice_in_dim(padded, 1, length + 1, axis=dim_index)
    upper_side = lax.slice_in_dim(padded, 2, length + 2, axis=dim_index)
    lower_side = lax.slice_in_dim(padded, 0, length, axis=dim_index)
    within = lax.iota(jnp.int32, length) % 8
    target = [1] * padded.ndim
    target[dim_index] = length
    upper_mask = (within == 7).astype(padded.dtype).reshape(target)
    lower_mask = (within == 0).astype(padded.dtype).reshape(target)
    return center + upper_mask * upper_side + lower_mask * lower_side


def assemble_global(source):
    for spatial_axis in range(3):
        widths = [(0, 0)] * 4
        widths[spatial_axis + 1] = (1, 1)
        source = fold_axis(jnp.pad(source, widths), spatial_axis, source.shape[spatial_axis + 1])
    return source


def invert(order_row):
    positions = jnp.arange(order_row.shape[0], dtype=jnp.int32)
    return jnp.zeros_like(order_row).at[order_row].set(positions)


def pick_rows(block_data, row_list):
    return block_data[:, row_list, :]


def pick_flags(flag_row, row_list):
    return flag_row[row_list]


def to_bricks(stored, inverse):
    fields_n = stored.shape[0]
    per_device = stored.reshape(fields_n, DEVICES, EL_DEV, NODES).transpose(1, 0, 2, 3)
    arranged = jax.vmap(pick_rows)(per_device, inverse)
    arranged = arranged.reshape(DEVICES, fields_n, BX, BY, BZ, P_SIZE, P_SIZE, P_SIZE).transpose(0, 1, 2, 5, 3, 6, 4, 7)
    return arranged.reshape(DEVICES, fields_n, BX * P_SIZE, BY * P_SIZE, BZ * P_SIZE)


def from_bricks(bricks, order):
    fields_n = bricks.shape[1]
    arranged = bricks.reshape(DEVICES, fields_n, BX, P_SIZE, BY, P_SIZE, BZ, P_SIZE).transpose(0, 1, 2, 4, 6, 3, 5, 7)
    arranged = arranged.reshape(DEVICES, fields_n, EL_DEV, NODES)
    stored = jax.vmap(pick_rows)(arranged, order)
    return stored.transpose(1, 0, 2, 3).reshape(fields_n, ELEMS, NODES)


def globalize(bricks):
    fields_n = bricks.shape[1]
    shaped = bricks.reshape(N_GX, N_GY, N_GZ, fields_n, BX * P_SIZE, BY * P_SIZE, BZ * P_SIZE)
    return shaped.transpose(3, 0, 4, 1, 5, 2, 6).reshape(fields_n, GRID_X, GRID_Y, GRID_Z)


def localize(field_grid):
    fields_n = field_grid.shape[0]
    shaped = field_grid.reshape(fields_n, N_GX, BX * P_SIZE, N_GY, BY * P_SIZE, N_GZ, BZ * P_SIZE)
    return shaped.transpose(1, 3, 5, 0, 2, 4, 6).reshape(DEVICES, fields_n, BX * P_SIZE, BY * P_SIZE, BZ * P_SIZE)


def reference(adjoint, load, displace, damage, history, frozen, order):
    inverse = jax.vmap(invert)(order)
    weights, derivative = gll_tables()
    small = jnp.asarray(derivative, jnp.float32)
    line_x = np.tile(weights, BX)
    line_y = np.tile(weights, BY)
    line_z = np.tile(weights, BZ)
    weight_brick = jnp.asarray(line_x[:, None, None] * line_y[None, :, None] * line_z[None, None, :], jnp.float32)
    adjoint_dev = to_bricks(adjoint, inverse).astype(jnp.float32)
    displace_dev = to_bricks(displace, inverse).astype(jnp.float32)
    damage_dev = to_bricks(damage[None], inverse)[:, 0].astype(jnp.float32)
    history_dev = to_bricks(history[None], inverse)[:, 0].astype(jnp.float32)
    flags = jax.vmap(pick_flags)(frozen.reshape(DEVICES, EL_DEV), inverse).astype(jnp.float32)
    frozen_dev = jnp.broadcast_to(flags.reshape(DEVICES, BX, 1, BY, 1, BZ, 1), (DEVICES, BX, P_SIZE, BY, P_SIZE, BZ, P_SIZE))
    frozen_dev = frozen_dev.reshape(DEVICES, BX * P_SIZE, BY * P_SIZE, BZ * P_SIZE)

    def local_pass(adjoint_now):
        def one_device(inputs):
            adjoint_one, displace_one, damage_one, history_one, frozen_one = inputs
            state = state_terms(displace_one, damage_one, history_one, frozen_one, weight_brick, small)
            return apply_transposed(adjoint_one, state, weight_brick, small)
        return lax.map(one_device, (adjoint_now, displace_dev, damage_dev, history_dev, frozen_dev))

    counts = assemble_global(jnp.ones((1, GRID_X, GRID_Y, GRID_Z), jnp.float32))
    continuous = assemble_global(globalize(adjoint_dev)) / counts
    load_glob = globalize(to_bricks(load, inverse).astype(jnp.float32))
    first = assemble_global(load_glob - globalize(local_pass(localize(continuous))))
    second_input = continuous + relaxation * first
    residual = assemble_global(load_glob - globalize(local_pass(localize(second_input))))
    return from_bricks(localize(residual), order)
```

```python
import jax
import jax.numpy as jnp
import ml_dtypes
import numpy as np
from jax import lax
from jax.experimental import pallas as pl
from jax.experimental.pallas import tpu as pltpu
from jax.sharding import PartitionSpec as P

F32 = jnp.float32
BF16 = jnp.bfloat16
MESH = pl.DeviceIdType.MESH

lame_lambda = 0.15
lame_mu = 0.1
gc_length = 0.3
gc_inverse = 40.0
residual_stiff = 0.001
relaxation = 0.5
gll_points = (
    -1.0,
    -0.8717401485096066,
    -0.5917001814331423,
    -0.2092992179024789,
    0.2092992179024789,
    0.5917001814331423,
    0.8717401485096066,
    1.0,
)

DIRS = [
    (dx, dy, dz)
    for dx in (-1, 0, 1)
    for dy in (-1, 0, 1)
    for dz in (-1, 0, 1)
    if (dx, dy, dz) != (0, 0, 0)
]
X_DIRS = [d for d in DIRS if d[1] == 0 and d[2] == 0]
Y_DIRS = [d for d in DIRS if d[0] == 0 and d[1] != 0 and d[2] == 0]
XY_DIRS = [d for d in DIRS if d[0] != 0 and d[1] != 0 and d[2] == 0]
Z_DIRS = [d for d in DIRS if d[2] != 0]
SEND_ORDER = X_DIRS + Y_DIRS + XY_DIRS + Z_DIRS


def legendre_at(points, degree):
    values = []
    for point in points:
        previous = 1.0
        current = point
        for level in range(1, degree):
            following = ((2 * level + 1) * point * current - level * previous) / (level + 1)
            previous = current
            current = following
        values.append(current)
    return values


def gll_tables():
    degree = 7
    points = list(gll_points)
    legendre_vals = legendre_at(points, degree)
    weights = [2.0 / (degree * (degree + 1) * entry * entry) for entry in legendre_vals]
    derivative = []
    for row_index in range(degree + 1):
        row_vals = []
        for col_index in range(degree + 1):
            if row_index != col_index:
                row_vals.append(
                    legendre_vals[row_index]
                    / (legendre_vals[col_index] * (points[row_index] - points[col_index]))
                )
            else:
                row_vals.append(0.0)
        derivative.append(row_vals)
    derivative[0][0] = -degree * (degree + 1) / 4.0
    derivative[degree][degree] = degree * (degree + 1) / 4.0
    return (np.array(weights), np.array(derivative))


def split_np(matrix):
    high = matrix.astype(np.float32).astype(ml_dtypes.bfloat16)
    low = (matrix - high.astype(np.float64)).astype(np.float32).astype(ml_dtypes.bfloat16)
    return high, low


def even_odd_rows(matrix):
    even = (matrix + matrix[:, ::-1]) / 2
    odd = (matrix - matrix[:, ::-1]) / 2
    rows = []
    for part in (even, odd):
        for a in range(2):
            for b in range(2):
                same = [part[2 * a + h, 2 * b + h] for h in range(2)]
                cross = [part[2 * a + h, 2 * b + 1 - h] for h in range(2)]
                rows.append(np.repeat(same, 64))
                rows.append(np.repeat(cross, 64))
    return rows


def constants():
    weights, derivative = gll_tables()
    eye = np.eye
    forward_y = np.kron(eye(2), np.kron(derivative.T, eye(8)))
    forward_z = np.kron(eye(16), derivative.T)
    back_y = np.kron(eye(2), np.kron(derivative, eye(8)))
    back_z = np.kron(eye(16), derivative)
    f_high, f_low = split_np(np.concatenate([forward_y, forward_z], axis=1))
    forward = np.concatenate([f_high, f_high, f_low], axis=0)
    b_high, b_low = split_np(np.concatenate([back_y, back_z], axis=0))
    back = np.concatenate([b_high, b_low], axis=1)
    brick = (weights[:, None, None] * weights[None, :, None] * weights[None, None, :]).reshape(4, 128)
    rows = even_odd_rows(derivative) + even_odd_rows(derivative.T) + list(brick)
    rows = np.stack(rows + [np.zeros(128)] * 4).astype(np.float32)
    return forward, back, rows


def lane_roll(value, shift):
    shift = shift % 128
    if shift == 0:
        return value
    flat = value.reshape(-1, 128)
    return pltpu.roll(flat, shift, 1).reshape(value.shape)


def split(value):
    high = value.astype(BF16)
    low = (value - high.astype(F32)).astype(BF16)
    return high, low


def x_derivative(tiles, table, base):
    def row(index):
        return table[base + index : base + index + 1, :]

    r2 = lane_roll(tiles[2], 64)
    r3 = lane_roll(tiles[3], 64)
    even = [tiles[0] + r3, tiles[1] + r2]
    odd = [tiles[0] - r3, tiles[1] - r2]
    even_r = [lane_roll(v, 64) for v in even]
    odd_r = [lane_roll(v, 64) for v in odd]
    out = [None] * 4
    for a in range(2):
        parts = []
        for start, own, crossed in ((0, even, even_r), (8, odd, odd_r)):
            k = start + 4 * a
            parts.append(
                row(k) * own[0] + row(k + 1) * crossed[0] + row(k + 2) * own[1] + row(k + 3) * crossed[1]
            )
        out[a] = parts[1] + parts[0]
        out[3 - a] = lane_roll(parts[1] - parts[0], 64)
    return out


def kernel(
    adjoint_h,
    load_h,
    displace_h,
    damage_h,
    history_h,
    frozen_h,
    order_h,
    forward_h,
    back_h,
    table_h,
    out_ref,
    adjoint_b,
    load_b,
    displace_b,
    damage_b,
    history_b,
    frozen_b,
    order_b,
    forward,
    back,
    table,
    value,
    load,
    summed,
    state,
    keep,
    xs,
    ys,
    zs,
    xr,
    yr,
    xyr,
    zr,
    in_sem,
    send_sem,
    recv_sem,
):
    px, py, pz = (lax.axis_index("gx"), lax.axis_index("gy"), lax.axis_index("gz"))
    sizes = (lax.axis_size("gx"), lax.axis_size("gy"), lax.axis_size("gz"))

    pairs = (
        (order_h, order_b),
        (adjoint_h, adjoint_b),
        (displace_h, displace_b),
        (damage_h, damage_b),
        (history_h, history_b),
        (frozen_h, frozen_b),
        (forward_h, forward),
        (table_h, table),
        (load_h, load_b),
        (back_h, back),
    )
    copies = [pltpu.make_async_copy(src, dst, in_sem.at[n]) for n, (src, dst) in enumerate(pairs)]
    for copy in copies:
        copy.start()

    along = [
        {
            -1: lax.rem(p + n - 1, n),
            0: p,
            1: lax.rem(p + 1, n),
        }
        for p, n in zip((px, py, pz), sizes)
    ]

    def target(d):
        return tuple(along[axis][d[axis]] for axis in range(3))

    barrier = pltpu.get_barrier_semaphore()
    for d in DIRS:
        pl.semaphore_signal(barrier, inc=1, device_id=target(d), device_id_type=MESH)

    present = [
        {
            -1: (p > 0).astype(F32),
            1: (p < n - 1).astype(F32),
        }
        for p, n in zip((px, py, pz), sizes)
    ]

    lane = lax.broadcasted_iota(jnp.int32, (8, 128), 1)
    sub = lax.broadcasted_iota(jnp.int32, (8, 128), 0)
    lane_k = lane % 8
    lane_j = (lane // 8) % 8
    lane_h = lane // 64

    def fmask(condition):
        return jnp.where(condition, 1.0, 0.0).astype(F32)

    k_end = {-1: fmask(lane_k == 0), 1: fmask(lane_k == 7)}
    j_end = {-1: fmask(lane_j == 0), 1: fmask(lane_j == 7)}
    h_end = {-1: fmask(lane_h == 0), 1: fmask(lane_h == 1)}

    copies[0].wait()
    row_id = lax.broadcasted_iota(jnp.int32, (64, 64), 0)
    place = (row_id // 16) * 16 + 2 * (row_id % 8) + (row_id // 8) % 2
    chosen = fmask(place == order_b[...])
    pick = chosen.astype(BF16)
    unpick = chosen.T.astype(BF16)

    def placed(stored):
        return jnp.dot(pick, stored, preferred_element_type=F32)

    def to_rows(ref, target_ref):
        for f in range(4):
            rows = placed(ref[f])
            for a in range(4):
                target_ref[a, f * 64 : f * 64 + 64, :] = rows[:, a * 128 : a * 128 + 128]

    def sum_local():
        z_up = k_end[1] * fmask(sub < 7)
        z_down = k_end[-1] * fmask(sub > 0)
        for f in range(4):
            block = summed[:, f * 64 : f * 64 + 64, :].reshape(16, 2, 8, 128)
            x0, x1 = block[:, 0], block[:, 1]
            y0 = x0 + k_end[1] * lane_roll(x1, 7) + z_down * pltpu.roll(lane_roll(x1, -7), 1, 1)
            y1 = x1 + k_end[-1] * lane_roll(x0, -7) + z_up * pltpu.roll(lane_roll(x0, 7), 7, 1)
            both = jnp.stack([y0, y1], axis=1).reshape(4, 4, 16, 128)
            upper = j_end[1] * lane_roll(both[:, 1:], 56).reshape(4, 3, 2, 8, 128)
            lower = j_end[-1] * lane_roll(both[:, :3], -56).reshape(4, 3, 2, 8, 128)
            upper = upper.reshape(4, 3, 16, 128)
            lower = lower.reshape(4, 3, 16, 128)
            base = f * 64
            summed[:, base : base + 16, :] = both[:, 0] + upper[:, 0]
            summed[:, base + 16 : base + 32, :] = both[:, 1] + upper[:, 1] + lower[:, 0]
            summed[:, base + 32 : base + 48, :] = both[:, 2] + upper[:, 2] + lower[:, 1]
            summed[:, base + 48 : base + 64, :] = both[:, 3] + lower[:, 2]

    low_half = lax.broadcasted_iota(jnp.int32, (64, 128), 1) < 64
    wide_j = (lax.broadcasted_iota(jnp.int32, (16, 128), 1) // 8) % 8

    def pack(r):
        for p in range(2):
            first, second = 2 * p * 64, (2 * p + 1) * 64
            xs[r, 0, p] = jnp.where(
                low_half,
                summed[0, first : first + 64, :],
                lane_roll(summed[0, second : second + 64, :], 64),
            )
            xs[r, 1, p] = jnp.where(
                low_half,
                lane_roll(summed[3, first : first + 64, :], 64),
                summed[3, second : second + 64, :],
            )
        for n, (row, j) in enumerate(((0, 0), (48, 7))):
            for g in range(2):
                packed = jnp.zeros((16, 128), F32)
                for slot in range(8):
                    f, a = slot // 2, 2 * g + slot % 2
                    piece = lane_roll(summed[a, f * 64 + row : f * 64 + row + 16, :], 8 * (slot - j))
                    packed = jnp.where(wide_j == slot, piece, packed)
                ys[r, n, g] = packed
        for n, (row, k) in enumerate(((0, 0), (15, 7))):
            packed = jnp.zeros((8, 128), F32)
            for slot in range(8):
                a, half = slot // 2, slot % 2
                piece = summed[a, pl.ds(half * 128 + row, 8, stride=16), :]
                packed = jnp.where(lane_k == slot, lane_roll(piece, slot - k), packed)
            zs[r, n] = packed

    def message(r, d):
        n = DIRS.index(d)
        dx, dy, dz = d
        if d in X_DIRS:
            src, dst = xs.at[r, (dx + 1) // 2], xr.at[r, (dx + 1) // 2]
        elif d in Y_DIRS:
            src, dst = ys.at[r, (dy + 1) // 2], yr.at[r, (dy + 1) // 2]
        elif d in XY_DIRS:
            src, dst = ys.at[r, (dy + 1) // 2, (dx + 1) // 2], xyr.at[r, XY_DIRS.index(d)]
        else:
            src, dst = zs.at[r, (dz + 1) // 2], zr.at[r, Z_DIRS.index(d)]
        return pltpu.make_async_remote_copy(
            src_ref=src,
            dst_ref=dst,
            send_sem=send_sem.at[r, n],
            recv_sem=recv_sem.at[r, n],
            device_id=target(d),
            device_id_type=MESH,
        )

    def send(r):
        messages = {d: message(r, d) for d in SEND_ORDER}
        for d in SEND_ORDER:
            messages[d].start()
        return messages

    def receive(r, messages):
        for d in X_DIRS:
            messages[d].wait_recv()
            n = (d[0] + 1) // 2
            side = -d[0]
            a = 0 if side < 0 else 3
            weight = present[0][side]
            for f in range(4):
                face = xr[r, n, f // 2]
                if (f % 2 == 1) == (side < 0):
                    face = lane_roll(face, 64)
                mine = low_half if side < 0 else jnp.logical_not(low_half)
                rows = slice(f * 64, f * 64 + 64)
                summed[a, rows, :] += jnp.where(mine, face * weight, 0.0)
        for d in Y_DIRS:
            messages[d].wait_recv()
            dy = d[1]
            side = -dy
            faces = [yr[r, (dy + 1) // 2, g] for g in range(2)]
            for dx in (-1, 1):
                e = (dx, dy, 0)
                messages[e].wait_recv()
                edge = lane_roll(xyr[r, XY_DIRS.index(e)], -72 * dx).reshape(2, 8, 128)
                wanted = fmask(lane_j % 2 == (0 if dx > 0 else 1)) * h_end[-dx] * present[0][-dx]
                g = 0 if dx > 0 else 1
                faces[g] = faces[g] + (edge * wanted).reshape(16, 128)
            row, j = (0, 0) if side < 0 else (48, 7)
            wanted = j_end[side] * present[1][side]
            for f in range(4):
                for a in range(4):
                    slot = f * 2 + a % 2
                    piece = lane_roll(faces[a // 2], 8 * (j - slot)).reshape(2, 8, 128) * wanted
                    rows = slice(f * 64 + row, f * 64 + row + 16)
                    summed[a, rows, :] += piece.reshape(16, 128)
        for dz in (-1, 1):
            side = -dz
            face = None
            for d in Z_DIRS:
                if d[2] != dz:
                    continue
                messages[d].wait_recv()
                part = zr[r, Z_DIRS.index(d)]
                dx, dy, _ = d
                wanted = None
                if dx != 0:
                    slots = (lane_k < 2) if dx > 0 else (lane_k >= 6)
                    wanted = h_end[-dx] * fmask(slots) * present[0][-dx]
                if dy != 0:
                    mine = j_end[-dy] * fmask(sub % 4 == (0 if dy > 0 else 3)) * present[1][-dy]
                    wanted = mine if wanted is None else wanted * mine
                    part = pltpu.roll(part, (-3 * dy) % 8, 0)
                part = lane_roll(part, -70 * dx - 56 * dy)
                if wanted is not None:
                    part = part * wanted
                face = part if face is None else face + part
            row, k = (0, 0) if side < 0 else (15, 7)
            wanted = k_end[side] * present[2][side]
            for slot in range(8):
                a, half = slot // 2, slot % 2
                where = pl.ds(half * 128 + row, 8, stride=16)
                summed[a, where, :] = summed[a, where, :] + lane_roll(face, k - slot) * wanted

    def finish(messages):
        for d in SEND_ORDER:
            messages[d].wait_send()

    def w_rows():
        return table[32:36, :].reshape(4, 1, 128)

    def state_terms():
        for e in range(4):
            rows = slice(16 * e, 16 * e + 16)
            moved = [
                jnp.stack([value[a, f * 64 + 16 * e : f * 64 + 16 * e + 16, :] for a in range(4)])
                for f in range(3)
            ]
            stacked = jnp.stack(moved).reshape(192, 128).astype(BF16)
            both = jnp.concatenate([stacked, stacked], axis=1)
            yz = jnp.dot(both, forward[128:384, :], preferred_element_type=F32)
            gy = yz[:, :128].reshape(3, 4, 16, 128)
            gz = yz[:, 128:].reshape(3, 4, 16, 128)
            gx = [
                jnp.stack(x_derivative([moved[f][a] for a in range(4)], table, 0))
                for f in range(3)
            ]
            shear = [gy[0] + gx[1], gz[0] + gx[2], gz[1] + gy[2]]
            normal = [gx[0], gy[1], gz[2]]
            trace_sum = normal[0] + normal[1] + normal[2]
            stress = [lame_lambda * trace_sum + 2.0 * lame_mu * n for n in normal]
            stress += [lame_mu * s for s in shear]
            energy = stress[0] * normal[0] + stress[1] * normal[1] + stress[2] * normal[2]
            energy = 0.5 * (energy + stress[3] * shear[0] + stress[4] * shear[1] + stress[5] * shear[2])
            damage = keep[0, :, rows, :]
            history = keep[1, :, rows, :]
            loading = keep[2, 0, rows, :][None]
            driving = (1.0 - loading) * history + loading * energy
            intact = 1.0 - damage
            brick = w_rows()
            slope = -2.0 * intact * brick
            for n in range(6):
                state[n, :, rows, :] = slope * stress[n]
            state[6, :, rows, :] = lame_mu * brick * (intact * intact + residual_stiff)
            state[7, :, rows, :] = brick * (gc_inverse + 2.0 * driving)

    def apply_transposed():
        for e in range(4):
            rows = slice(16 * e, 16 * e + 16)
            field = [value[:, f * 64 + 16 * e : f * 64 + 16 * e + 16, :] for f in range(4)]
            high, low = split(jnp.stack(field).reshape(256, 128))
            three = jnp.concatenate([high, low, high], axis=1)
            yz = jnp.dot(three, forward[...], preferred_element_type=F32)
            gy = yz[:, :128].reshape(4, 4, 16, 128)
            gz = yz[:, 128:].reshape(4, 4, 16, 128)
            gx = [
                jnp.stack(x_derivative([field[f][a] for a in range(4)], table, 0)) for f in range(4)
            ]
            scaled = [state[n, :, rows, :] for n in range(6)]
            stiff = state[6, :, rows, :]
            vd = field[3]
            coupled = keep[2, 0, rows, :][None] * vd
            shear = [gy[0] + gx[1], gz[0] + gx[2], gz[1] + gy[2]]
            normal = [gx[0], gy[1], gz[2]]
            trace_sum = 1.5 * (normal[0] + normal[1] + normal[2])
            tensor = [stiff * (trace_sum + 2.0 * normal[n]) + scaled[n] * coupled for n in range(3)]
            tensor += [stiff * shear[n] + scaled[n + 3] * coupled for n in range(3)]
            nodal = state[7, :, rows, :] * vd
            for n in range(3):
                nodal = nodal + scaled[n] * normal[n] + scaled[n + 3] * shear[n]
            flux = gc_length * w_rows()
            along_x = [tensor[0], tensor[3], tensor[4], flux * gx[3]]
            along_y = [tensor[3], tensor[1], tensor[5], flux * gy[3]]
            along_z = [tensor[4], tensor[5], tensor[2], flux * gz[3]]
            y_high, y_low = split(jnp.stack(along_y).reshape(256, 128))
            z_high, z_low = split(jnp.stack(along_z).reshape(256, 128))
            one = jnp.dot(
                jnp.concatenate([y_high, z_high], axis=1), back[...], preferred_element_type=F32
            )
            two = jnp.dot(
                jnp.concatenate([y_low, z_low], axis=1), back[:, :128], preferred_element_type=F32
            )
            total = (one[:, :128] + one[:, 128:] + two).reshape(4, 4, 16, 128)
            for f in range(4):
                tx = jnp.stack(x_derivative([along_x[f][a] for a in range(4)], table, 16))
                result = total[f] + tx
                if f == 3:
                    result = result + nodal
                where = slice(f * 64 + 16 * e, f * 64 + 16 * e + 16)
                summed[:, where, :] = load[:, where, :] - result

    copies[1].wait()
    to_rows(adjoint_b, summed)
    sum_local()
    pack(0)
    pl.semaphore_wait(barrier, len(DIRS))
    messages = send(0)

    copies[2].wait()
    for f in range(3):
        rows = placed(displace_b[f])
        for a in range(4):
            value[a, f * 64 : f * 64 + 64, :] = rows[:, a * 128 : a * 128 + 128]
    for n, (copy, ref) in enumerate(((copies[3], damage_b), (copies[4], history_b))):
        copy.wait()
        rows = placed(ref[...])
        for a in range(4):
            keep[n, a] = rows[:, a * 128 : a * 128 + 128]
    copies[5].wait()
    frozen = jnp.sum(chosen * frozen_b[...].astype(F32), axis=1, keepdims=True)
    keep[2, 0] = jnp.broadcast_to(1.0 - frozen, (64, 128))
    copies[6].wait()
    copies[7].wait()
    state_terms()
    copies[8].wait()
    to_rows(load_b, load)
    copies[9].wait()

    receive(0, messages)

    def half_where(condition, scalar):
        return 1.0 - 0.5 * fmask(condition) * scalar

    inv_z = [
        half_where(lane_k == 7, 1.0) * half_where((lane_k == 0) & (sub > 0), 1.0)
        * half_where((lane_k == 0) & (sub == 0), present[2][-1]),
        half_where(lane_k == 0, 1.0) * half_where((lane_k == 7) & (sub < 7), 1.0)
        * half_where((lane_k == 7) & (sub == 7), present[2][1]),
    ]
    inv_y = []
    for e in range(4):
        lower = 1.0 if e > 0 else present[1][-1]
        upper = 1.0 if e < 3 else present[1][1]
        inv_y.append(half_where(lane_j == 0, lower) * half_where(lane_j == 7, upper))
    inv_x = [half_where(lane_h == 0, present[0][-1]), None, None, half_where(lane_h == 1, present[0][1])]
    for e in range(4):
        for a in range(4):
            scale = jnp.stack([inv_y[e] * inv_z[0], inv_y[e] * inv_z[1]])
            if inv_x[a] is not None:
                scale = scale * inv_x[a]
            scale = scale.reshape(16, 128)
            for f in range(4):
                rows = slice(f * 64 + 16 * e, f * 64 + 16 * e + 16)
                value[a, rows, :] = summed[a, rows, :] * scale

    apply_transposed()
    sum_local()
    pack(1)
    finish(messages)
    messages = send(1)
    receive(1, messages)
    value[...] = value[...] + relaxation * summed[...]

    apply_transposed()
    sum_local()
    pack(2)
    finish(messages)
    messages = send(2)
    receive(2, messages)
    twice = jnp.concatenate([unpick, unpick], axis=1)
    for f in range(4):
        for a in range(4):
            high, low = split(summed[a, f * 64 : f * 64 + 64, :])
            both = jnp.concatenate([high, low], axis=0)
            out_ref[f, :, a * 128 : a * 128 + 128] = jnp.dot(twice, both, preferred_element_type=F32)
    finish(messages)


def shards(adjoint, load, displace, damage, history, frozen, order):
    forward, back, table = (jnp.asarray(c) for c in constants())
    any_spec = pl.BlockSpec(memory_space=pl.ANY)
    return pl.pallas_call(
        kernel,
        out_shape=jax.ShapeDtypeStruct((4, 64, 512), F32),
        in_specs=[any_spec] * 10,
        out_specs=pl.BlockSpec(memory_space=pltpu.VMEM),
        scratch_shapes=[
            pltpu.VMEM((4, 64, 512), BF16),
            pltpu.VMEM((4, 64, 512), BF16),
            pltpu.VMEM((3, 64, 512), BF16),
            pltpu.VMEM((64, 512), BF16),
            pltpu.VMEM((64, 512), BF16),
            pltpu.VMEM((1, 64), jnp.int32),
            pltpu.VMEM((1, 64), jnp.int32),
            pltpu.VMEM((384, 256), BF16),
            pltpu.VMEM((256, 256), BF16),
            pltpu.VMEM((40, 128), F32),
            pltpu.VMEM((4, 256, 128), F32),
            pltpu.VMEM((4, 256, 128), F32),
            pltpu.VMEM((4, 256, 128), F32),
            pltpu.VMEM((8, 4, 64, 128), F32),
            pltpu.VMEM((3, 4, 64, 128), F32),
            pltpu.VMEM((3, 2, 2, 64, 128), F32),
            pltpu.VMEM((3, 2, 2, 16, 128), F32),
            pltpu.VMEM((3, 2, 8, 128), F32),
            pltpu.VMEM((3, 2, 2, 64, 128), F32),
            pltpu.VMEM((3, 2, 2, 16, 128), F32),
            pltpu.VMEM((3, 4, 16, 128), F32),
            pltpu.VMEM((3, 18, 8, 128), F32),
            pltpu.SemaphoreType.DMA((10,)),
            pltpu.SemaphoreType.DMA((3, 26)),
            pltpu.SemaphoreType.DMA((3, 26)),
        ],
        compiler_params=pltpu.CompilerParams(
            collective_id=0, has_side_effects=True, vmem_limit_bytes=32 * 1024 * 1024
        ),
    )(adjoint, load, displace, damage, history, frozen.reshape(1, 64), order, forward, back, table)


def solution(mesh):
    in_specs = (
        P(None, ("gx", "gy", "gz"), None),
        P(None, ("gx", "gy", "gz"), None),
        P(None, ("gx", "gy", "gz"), None),
        P(("gx", "gy", "gz"), None),
        P(("gx", "gy", "gz"), None),
        P(("gx", "gy", "gz")),
        P(("gx", "gy", "gz"), None),
    )
    out_specs = P(None, ("gx", "gy", "gz"), None)
    return jax.shard_map(shards, mesh=mesh, in_specs=in_specs, out_specs=out_specs, check_vma=False)
```

```python
import jax
import jax.numpy as jnp
import ml_dtypes
import numpy as np
from jax import lax
from jax.experimental import pallas as pl
from jax.experimental.pallas import tpu as pltpu
from jax.sharding import PartitionSpec as P

F32 = jnp.float32
BF16 = jnp.bfloat16
MESH = pl.DeviceIdType.MESH

lame_lambda = 0.15
lame_mu = 0.1
gc_length = 0.3
gc_inverse = 40.0
residual_stiff = 0.001
relaxation = 0.5
gll_points = (
    -1.0,
    -0.8717401485096066,
    -0.5917001814331423,
    -0.2092992179024789,
    0.2092992179024789,
    0.5917001814331423,
    0.8717401485096066,
    1.0,
)

DIRS = [
    (dx, dy, dz)
    for dx in (-1, 0, 1)
    for dy in (-1, 0, 1)
    for dz in (-1, 0, 1)
    if (dx, dy, dz) != (0, 0, 0)
]
X_DIRS = [d for d in DIRS if d[1] == 0 and d[2] == 0]
Y_DIRS = [d for d in DIRS if d[0] == 0 and d[1] != 0 and d[2] == 0]
XY_DIRS = [d for d in DIRS if d[0] != 0 and d[1] != 0 and d[2] == 0]
Z_DIRS = [d for d in DIRS if d[2] != 0]
Z_LATE = [d for d in Z_DIRS if d[1] != 0]
Z_EARLY = [d for d in Z_DIRS if d[1] == 0]
Z_ORDER = sorted(Z_DIRS, key=lambda d: -abs(d[0]) - abs(d[1]))


def legendre_at(points, degree):
    values = []
    for point in points:
        previous = 1.0
        current = point
        for level in range(1, degree):
            following = ((2 * level + 1) * point * current - level * previous) / (level + 1)
            previous = current
            current = following
        values.append(current)
    return values


def gll_tables():
    degree = 7
    points = list(gll_points)
    legendre_vals = legendre_at(points, degree)
    weights = [2.0 / (degree * (degree + 1) * entry * entry) for entry in legendre_vals]
    derivative = []
    for row_index in range(degree + 1):
        row_vals = []
        for col_index in range(degree + 1):
            if row_index != col_index:
                row_vals.append(
                    legendre_vals[row_index]
                    / (legendre_vals[col_index] * (points[row_index] - points[col_index]))
                )
            else:
                row_vals.append(0.0)
        derivative.append(row_vals)
    derivative[0][0] = -degree * (degree + 1) / 4.0
    derivative[degree][degree] = degree * (degree + 1) / 4.0
    return (np.array(weights), np.array(derivative))


def split_np(matrix):
    high = matrix.astype(np.float32).astype(ml_dtypes.bfloat16)
    low = (matrix - high.astype(np.float64)).astype(np.float32).astype(ml_dtypes.bfloat16)
    return high, low


def constants():
    _, derivative = gll_tables()
    eye = np.eye
    forward_y = np.kron(eye(2), np.kron(derivative.T, eye(8)))
    forward_z = np.kron(eye(16), derivative.T)
    back_y = np.kron(eye(2), np.kron(derivative, eye(8)))
    back_z = np.kron(eye(16), derivative)
    f_high, f_low = split_np(np.concatenate([forward_y, forward_z], axis=1))
    forward = np.concatenate([f_high, f_high, f_low], axis=0)
    b_high, b_low = split_np(np.concatenate([back_y, back_z], axis=0))
    back = np.concatenate([b_high, b_low], axis=1)
    swap = np.zeros((2, 2, 64, 2, 2, 64))
    for h in range(2):
        for odd in range(2):
            swap[h, odd, :, odd, h, :] = eye(64)
    swap = swap.reshape(256, 256).astype(ml_dtypes.bfloat16)
    return forward, back, swap


def lane_roll(value, shift):
    shift = shift % 128
    if shift == 0:
        return value
    flat = value.reshape(-1, 128)
    return pltpu.roll(flat, shift, 1).reshape(value.shape)


def lane_swap(value, mask):
    flat = value.reshape(-1, 128)
    index = jnp.bitwise_xor(lax.broadcasted_iota(jnp.int32, flat.shape, 1), mask)
    return jnp.take_along_axis(flat, index, axis=1).reshape(value.shape)


def split(value):
    high = value.astype(BF16)
    low = (value - high.astype(F32)).astype(BF16)
    return high, low


def x_derivative(tiles, matrix):
    even_part = (matrix + matrix[:, ::-1]) / 2
    odd_part = (matrix - matrix[:, ::-1]) / 2
    even = [tiles[n] + tiles[7 - n] for n in range(4)]
    odd = [tiles[n] - tiles[7 - n] for n in range(4)]
    out = [None] * 8
    for n in range(4):
        first = float(even_part[n, 0]) * even[0]
        second = float(odd_part[n, 0]) * odd[0]
        for m in range(1, 4):
            first = first + float(even_part[n, m]) * even[m]
            second = second + float(odd_part[n, m]) * odd[m]
        out[n] = second + first
        out[7 - n] = second - first
    return out


def kernel(
    adjoint_h,
    load_h,
    displace_h,
    damage_h,
    history_h,
    frozen_h,
    order_h,
    forward_h,
    back_h,
    swap_h,
    out_ref,
    adjoint_b,
    load_b,
    displace_b,
    damage_b,
    history_b,
    frozen_b,
    order_b,
    forward,
    back,
    swap,
    value,
    kept,
    load,
    summed,
    state,
    keep,
    ys,
    zs,
    xr,
    yr,
    xyr,
    zr,
    in_sem,
    send_sem,
    recv_sem,
):
    weights, derivative = gll_tables()
    px, py, pz = (lax.axis_index("gx"), lax.axis_index("gy"), lax.axis_index("gz"))
    sizes = (lax.axis_size("gx"), lax.axis_size("gy"), lax.axis_size("gz"))

    pairs = (
        (order_h, order_b),
        (adjoint_h, adjoint_b),
        (swap_h, swap),
        (displace_h, displace_b),
        (forward_h, forward),
        (damage_h, damage_b),
        (history_h, history_b),
        (frozen_h, frozen_b),
        (load_h, load_b),
        (back_h, back),
    )
    copies = [pltpu.make_async_copy(src, dst, in_sem.at[n]) for n, (src, dst) in enumerate(pairs)]
    for copy in copies[:3]:
        copy.start()

    along = [
        {
            -1: lax.rem(p + n - 1, n),
            0: p,
            1: lax.rem(p + 1, n),
        }
        for p, n in zip((px, py, pz), sizes)
    ]

    def target(d):
        return tuple(along[axis][d[axis]] for axis in range(3))

    barrier = pltpu.get_barrier_semaphore()
    for d in DIRS:
        pl.semaphore_signal(barrier, inc=1, device_id=target(d), device_id_type=MESH)
    for copy in copies[3:]:
        copy.start()

    present = [
        {
            -1: (p > 0).astype(F32),
            1: (p < n - 1).astype(F32),
        }
        for p, n in zip((px, py, pz), sizes)
    ]

    lane = lax.broadcasted_iota(jnp.int32, (8, 128), 1)
    sub = lax.broadcasted_iota(jnp.int32, (8, 128), 0)
    lane_k = lane % 8
    lane_j = (lane // 8) % 8
    lane_h = lane // 64

    def fmask(condition):
        return jnp.where(condition, 1.0, 0.0).astype(F32)

    j_end = {-1: fmask(lane_j == 0), 1: fmask(lane_j == 7)}
    h_end = {-1: fmask(lane_h == 0), 1: fmask(lane_h == 1)}
    first_z = (lane_h == 0) & (lane_k == 0)
    last_z = (lane_h == 1) & (lane_k == 7)
    z_end = {-1: fmask(first_z), 1: fmask(last_z)}
    inner_z = ((lane_h == 0) & (lane_k == 7)) | ((lane_h == 1) & (lane_k == 0))
    z_here = fmask(inner_z | (last_z & (sub < 7)))
    z_next = fmask(first_z & (sub > 0))

    copies[0].wait()
    row_id = lax.broadcasted_iota(jnp.int32, (64, 64), 0)
    place = ((row_id // 8) % 4) * 16 + 2 * (row_id % 8) + row_id // 32
    chosen = fmask(place == order_b[...])
    pick = chosen.astype(BF16)
    unpick = chosen.T.astype(BF16)

    def to_tiles(stored):
        rows = jnp.dot(pick, stored, preferred_element_type=F32).astype(BF16)
        sides = jnp.stack(
            [
                jnp.concatenate([rows[:32, n : n + 128], rows[32:, n : n + 128]], axis=1)
                for n in range(0, 512, 128)
            ]
        )
        tiles = jnp.dot(sides.reshape(128, 256), swap[...], preferred_element_type=F32)
        return tiles.reshape(4, 32, 256)

    def put_tiles(tiles, ref, start):
        for a in range(4):
            ref[2 * a, start : start + 32, :] = tiles[a, :, :128]
            ref[2 * a + 1, start : start + 32, :] = tiles[a, :, 128:]

    def group(ref, e):
        return jnp.stack([ref[:, f * 32 + 8 * e : f * 32 + 8 * e + 8, :] for f in range(4)], axis=1)

    def put_group(ref, e, block):
        for f in range(4):
            ref[:, f * 32 + 8 * e : f * 32 + 8 * e + 8, :] = block[:, f]

    def sum_z(block):
        flat = block.reshape(-1, 8, 128)
        taken = lane_swap(jnp.where(first_z, pltpu.roll(flat, 7, 1), flat), 71)
        total = flat + z_here * taken + z_next * pltpu.roll(taken, 1, 1)
        return total.reshape(block.shape)

    def sum_y(e):
        here, beyond = group(summed, e), group(summed, e + 1)
        taken = lane_swap(jnp.where(lane_j == 7, here, beyond), 56)
        put_group(summed, e, here + j_end[1] * taken)
        put_group(summed, e + 1, beyond + j_end[-1] * taken)

    def pack_z(r):
        for n, (row, h, k) in enumerate(((0, 0, 0), (7, 1, 7))):
            packed = jnp.zeros((8, 128), F32)
            for slot in range(16):
                i, half = slot // 2, slot % 2
                piece = summed[i, pl.ds(half * 64 + row, 8, stride=8), :]
                moved = lane_roll(piece, (slot // 8 - h) * 64 + slot % 8 - k)
                packed = jnp.where((lane_h == slot // 8) & (lane_k == slot % 8), moved, packed)
            zs[r, n] = packed

    def pack_y(r):
        for n, (e, j) in enumerate(((0, 0), (3, 7))):
            for g in range(4):
                packed = jnp.zeros((8, 128), F32)
                for slot in range(8):
                    row = (slot // 2) * 32 + 8 * e
                    piece = summed[2 * g + slot % 2, row : row + 8, :]
                    packed = jnp.where(lane_j == slot, lane_roll(piece, 8 * (slot - j)), packed)
                ys[r, n, g] = packed

    def message(r, d):
        n = DIRS.index(d)
        dx, dy, dz = d
        if d in X_DIRS:
            src, dst = summed.at[7 if dx > 0 else 0], xr.at[r, (dx + 1) // 2]
        elif d in Y_DIRS:
            src, dst = ys.at[r, (dy + 1) // 2], yr.at[r, (dy + 1) // 2]
        elif d in XY_DIRS:
            src, dst = ys.at[r, (dy + 1) // 2, 3 if dx > 0 else 0], xyr.at[r, XY_DIRS.index(d)]
        else:
            src, dst = zs.at[r, (dz + 1) // 2], zr.at[r, Z_DIRS.index(d)]
        return pltpu.make_async_remote_copy(
            src_ref=src,
            dst_ref=dst,
            send_sem=send_sem.at[r, n],
            recv_sem=recv_sem.at[r, n],
            device_id=target(d),
            device_id_type=MESH,
        )

    def send(r, messages, dirs):
        for d in dirs:
            messages[d] = message(r, d)
            messages[d].start()

    def finish(messages):
        for d in DIRS:
            messages[d].wait_send()

    def add_z(r, messages, dirs):
        for dz in (-1, 1):
            side = -dz
            face = None
            for d in dirs:
                if d[2] != dz:
                    continue
                messages[d].wait_recv()
                part = zr[r, Z_DIRS.index(d)]
                dx, dy, _ = d
                wanted = None
                if dx != 0:
                    slots = (lane_k < 2) if dx > 0 else (lane_k >= 6)
                    wanted = h_end[-dx] * fmask(slots) * present[0][-dx]
                if dy != 0:
                    mine = j_end[-dy] * fmask(sub % 4 == (0 if dy > 0 else 3)) * present[1][-dy]
                    wanted = mine if wanted is None else wanted * mine
                    part = pltpu.roll(part, (-3 * dy) % 8, 0)
                part = lane_roll(part, -70 * dx - 56 * dy)
                if wanted is not None:
                    part = part * wanted
                face = part if face is None else face + part
            row, h, k = (0, 0, 0) if side < 0 else (7, 1, 7)
            wanted = z_end[side] * present[2][side]
            for slot in range(16):
                i, half = slot // 2, slot % 2
                where = pl.ds(half * 64 + row, 8, stride=8)
                moved = lane_roll(face, (h - slot // 8) * 64 + k - slot % 8)
                value[i, where, :] = value[i, where, :] + moved * wanted

    def receive_early(r, messages):
        for i in range(1, 7):
            value[i] = summed[i]
        for d in X_DIRS:
            messages[d].wait_recv()
            i = 0 if d[0] > 0 else 7
            value[i] = summed[i] + xr[r, (d[0] + 1) // 2] * present[0][-d[0]]
        add_z(r, messages, Z_EARLY)

    def receive_late(r, messages):
        for d in Y_DIRS:
            messages[d].wait_recv()
            dy = d[1]
            side = -dy
            faces = [yr[r, (dy + 1) // 2, g] for g in range(4)]
            for dx in (-1, 1):
                e = (dx, dy, 0)
                messages[e].wait_recv()
                edge = lane_roll(xyr[r, XY_DIRS.index(e)], -8 * dx)
                wanted = fmask(lane_j % 2 == (0 if dx > 0 else 1)) * present[0][-dx]
                g = 0 if dx > 0 else 3
                faces[g] = faces[g] + edge * wanted
            e, j = (0, 0) if side < 0 else (3, 7)
            wanted = j_end[side] * present[1][side]
            for i in range(8):
                for f in range(4):
                    slot = f * 2 + i % 2
                    row = f * 32 + 8 * e
                    moved = lane_roll(faces[i // 2], 8 * (j - slot))
                    value[i, row : row + 8, :] = value[i, row : row + 8, :] + moved * wanted
        add_z(r, messages, Z_LATE)

    def brick():
        line_j = jnp.zeros((8, 128), F32)
        line_k = jnp.zeros((8, 128), F32)
        for n in range(8):
            line_j = jnp.where(lane_j == n, float(weights[n]), line_j)
            line_k = jnp.where(lane_k == n, float(weights[n]), line_k)
        plane = line_j * line_k
        return jnp.stack([plane * float(weights[n]) for n in range(8)])

    def gradients(block, count, exact):
        if exact:
            high = block.reshape(count * 64, 128).astype(BF16)
            left, table = jnp.concatenate([high, high], axis=1), forward[128:384, :]
        else:
            high, low = split(block.reshape(count * 64, 128))
            left, table = jnp.concatenate([high, low, high], axis=1), forward[...]
        yz = jnp.dot(left, table, preferred_element_type=F32)
        gx = jnp.stack(x_derivative([block[i] for i in range(8)], derivative))
        return gx, yz[:, :128].reshape(block.shape), yz[:, 128:].reshape(block.shape)

    def state_terms(e):
        rows = slice(8 * e, 8 * e + 8)
        moved = jnp.stack(
            [value[:, f * 32 + 8 * e : f * 32 + 8 * e + 8, :] for f in range(3)], axis=1
        )
        gx, gy, gz = gradients(moved, 3, True)
        shear = [gy[:, 0] + gx[:, 1], gz[:, 0] + gx[:, 2], gz[:, 1] + gy[:, 2]]
        normal = [gx[:, 0], gy[:, 1], gz[:, 2]]
        trace_sum = normal[0] + normal[1] + normal[2]
        stress = [lame_lambda * trace_sum + 2.0 * lame_mu * n for n in normal]
        stress += [lame_mu * s for s in shear]
        energy = stress[0] * normal[0] + stress[1] * normal[1] + stress[2] * normal[2]
        energy = 0.5 * (energy + stress[3] * shear[0] + stress[4] * shear[1] + stress[5] * shear[2])
        loading = keep[2, 0, rows, :][None]
        driving = (1.0 - loading) * keep[1, :, rows, :] + loading * energy
        intact = 1.0 - keep[0, :, rows, :]
        mass = brick()
        slope = -2.0 * intact * mass
        for n in range(6):
            state[n, :, rows, :] = slope * stress[n]
        state[6, :, rows, :] = lame_mu * mass * (intact * intact + residual_stiff)
        state[7, :, rows, :] = mass * (gc_inverse + 2.0 * driving)

    def apply_transposed(e, block):
        rows = slice(8 * e, 8 * e + 8)
        gx, gy, gz = gradients(block, 4, False)
        scaled = [state[n, :, rows, :] for n in range(6)]
        stiff = state[6, :, rows, :]
        vd = block[:, 3]
        coupled = keep[2, 0, rows, :][None] * vd
        shear = [gy[:, 0] + gx[:, 1], gz[:, 0] + gx[:, 2], gz[:, 1] + gy[:, 2]]
        normal = [gx[:, 0], gy[:, 1], gz[:, 2]]
        trace_sum = 1.5 * (normal[0] + normal[1] + normal[2])
        tensor = [stiff * (trace_sum + 2.0 * normal[n]) + scaled[n] * coupled for n in range(3)]
        tensor += [stiff * shear[n] + scaled[n + 3] * coupled for n in range(3)]
        nodal = state[7, :, rows, :] * vd
        for n in range(3):
            nodal = nodal + scaled[n] * normal[n] + scaled[n + 3] * shear[n]
        flux = gc_length * brick()
        along_x = jnp.stack([tensor[0], tensor[3], tensor[4], flux * gx[:, 3]], axis=1)
        along_y = jnp.stack([tensor[3], tensor[1], tensor[5], flux * gy[:, 3]], axis=1)
        along_z = jnp.stack([tensor[4], tensor[5], tensor[2], flux * gz[:, 3]], axis=1)
        y_high, y_low = split(along_y.reshape(256, 128))
        z_high, z_low = split(along_z.reshape(256, 128))
        one = jnp.dot(
            jnp.concatenate([y_high, z_high], axis=1), back[...], preferred_element_type=F32
        )
        two = jnp.dot(
            jnp.concatenate([y_low, z_low], axis=1), back[:, :128], preferred_element_type=F32
        )
        total = (one[:, :128] + one[:, 128:] + two).reshape(8, 4, 8, 128)
        total = total + jnp.stack(x_derivative([along_x[i] for i in range(8)], derivative.T))
        result = group(load, e) - total
        result = jnp.concatenate([result[:, :3], (result[:, 3] - nodal)[:, None]], axis=1)
        put_group(summed, e, sum_z(result))

    def ship(r):
        messages = {}
        pack_z(r)
        if r == 0:
            pl.semaphore_wait(barrier, len(DIRS))
        send(r, messages, Z_ORDER)
        send(r, messages, X_DIRS)
        pack_y(r)
        send(r, messages, XY_DIRS + Y_DIRS)
        return messages

    copies[1].wait()
    copies[2].wait()
    for f in range(4):
        put_tiles(to_tiles(adjoint_b[f]), summed, f * 32)
    for e in range(4):
        put_group(summed, e, sum_z(group(summed, e)))
    for e in range(3):
        sum_y(e)
    messages = ship(0)

    copies[3].wait()
    for f in range(3):
        put_tiles(to_tiles(displace_b[f]), value, f * 32)
    copies[4].wait()
    copies[5].wait()
    put_tiles(to_tiles(damage_b[...]), keep.at[0], 0)
    copies[6].wait()
    put_tiles(to_tiles(history_b[...]), keep.at[1], 0)
    copies[7].wait()
    frozen = 1.0 - jnp.sum(chosen * frozen_b[...].astype(F32), axis=1, keepdims=True)
    low_half = lax.broadcasted_iota(jnp.int32, (32, 128), 1) < 64
    keep[2, 0] = jnp.where(low_half, frozen[:32], frozen[32:])
    for e in range(4):
        state_terms(e)
    copies[8].wait()
    for f in range(4):
        put_tiles(to_tiles(load_b[f]), load, f * 32)
    copies[9].wait()

    def halved(condition, scalar):
        return 1.0 - 0.5 * fmask(condition) * scalar

    inv_z = halved(inner_z, 1.0) * halved(first_z & (sub > 0), 1.0) * halved(last_z & (sub < 7), 1.0)
    inv_z = inv_z * halved(first_z & (sub == 0), present[2][-1]) * halved(last_z & (sub == 7), present[2][1])

    def average(e):
        lower = 1.0 if e > 0 else present[1][-1]
        upper = 1.0 if e < 3 else present[1][1]
        scale = inv_z * halved(lane_j == 0, lower) * halved(lane_j == 7, upper)
        scales = [scale] * 8
        scales[0] = scale * (1.0 - 0.5 * present[0][-1])
        scales[7] = scale * (1.0 - 0.5 * present[0][1])
        block = group(value, e) * jnp.stack(scales)[:, None]
        put_group(kept, e, block)
        return block

    def relax(e):
        return group(kept, e) + relaxation * group(value, e)

    for r, ready in ((0, average), (1, relax)):
        receive_early(r, messages)
        finish(messages)
        early = [ready(e) for e in (1, 2)]
        for e in (1, 2):
            apply_transposed(e, early[e - 1])
        sum_y(1)
        receive_late(r, messages)
        for e in (0, 3):
            apply_transposed(e, ready(e))
        sum_y(0)
        sum_y(2)
        messages = ship(r + 1)

    receive_early(2, messages)
    receive_late(2, messages)
    twice = jnp.concatenate([unpick, unpick], axis=1)
    for f in range(4):
        rows = slice(f * 32, f * 32 + 32)
        sides = jnp.stack(
            [jnp.concatenate([value[2 * a, rows, :], value[2 * a + 1, rows, :]], axis=1) for a in range(4)]
        )
        high, low = split(sides.reshape(128, 256))
        both = jnp.concatenate([high, low], axis=0)
        moved = jnp.dot(both, swap[...], preferred_element_type=F32).astype(BF16)
        for a in range(4):
            parts = []
            for n in (a * 32, 128 + a * 32):
                parts += [moved[n : n + 32, :128], moved[n : n + 32, 128:]]
            stacked = jnp.concatenate(parts, axis=0)
            out_ref[f, :, a * 128 : a * 128 + 128] = jnp.dot(
                twice, stacked, preferred_element_type=F32
            )
    finish(messages)


def shards(adjoint, load, displace, damage, history, frozen, order):
    forward, back, swap = (jnp.asarray(c) for c in constants())
    hbm = pl.BlockSpec(memory_space=pltpu.HBM)
    return pl.pallas_call(
        kernel,
        out_shape=jax.ShapeDtypeStruct((4, 64, 512), F32),
        in_specs=[hbm] * 10,
        out_specs=pl.BlockSpec(memory_space=pltpu.VMEM),
        scratch_shapes=[
            pltpu.VMEM((4, 64, 512), BF16),
            pltpu.VMEM((4, 64, 512), BF16),
            pltpu.VMEM((3, 64, 512), BF16),
            pltpu.VMEM((64, 512), BF16),
            pltpu.VMEM((64, 512), BF16),
            pltpu.VMEM((1, 64), jnp.int32),
            pltpu.VMEM((1, 64), jnp.int32),
            pltpu.VMEM((384, 256), BF16),
            pltpu.VMEM((256, 256), BF16),
            pltpu.VMEM((256, 256), BF16),
            pltpu.VMEM((8, 128, 128), F32),
            pltpu.VMEM((8, 128, 128), F32),
            pltpu.VMEM((8, 128, 128), F32),
            pltpu.VMEM((8, 128, 128), F32),
            pltpu.VMEM((8, 8, 32, 128), F32),
            pltpu.VMEM((3, 8, 32, 128), F32),
            pltpu.VMEM((3, 2, 4, 8, 128), F32),
            pltpu.VMEM((3, 2, 8, 128), F32),
            pltpu.VMEM((3, 2, 128, 128), F32),
            pltpu.VMEM((3, 2, 4, 8, 128), F32),
            pltpu.VMEM((3, 4, 8, 128), F32),
            pltpu.VMEM((3, 18, 8, 128), F32),
            pltpu.SemaphoreType.DMA((10,)),
            pltpu.SemaphoreType.DMA((3, 26)),
            pltpu.SemaphoreType.DMA((3, 26)),
        ],
        compiler_params=pltpu.CompilerParams(
            collective_id=0, has_side_effects=True, vmem_limit_bytes=32 * 1024 * 1024
        ),
    )(adjoint, load, displace, damage, history, frozen.reshape(1, 64), order, forward, back, swap)


def solution(mesh):
    in_specs = (
        P(None, ("gx", "gy", "gz"), None),
        P(None, ("gx", "gy", "gz"), None),
        P(None, ("gx", "gy", "gz"), None),
        P(("gx", "gy", "gz"), None),
        P(("gx", "gy", "gz"), None),
        P(("gx", "gy", "gz")),
        P(("gx", "gy", "gz"), None),
    )
    out_specs = P(None, ("gx", "gy", "gz"), None)
    return jax.shard_map(shards, mesh=mesh, in_specs=in_specs, out_specs=out_specs, check_vma=False)
```

```python
import jax
import jax.numpy as jnp
import ml_dtypes
import numpy as np
from jax import lax
from jax.experimental import pallas as pl
from jax.experimental.pallas import tpu as pltpu
from jax.sharding import PartitionSpec as P

F32 = jnp.float32
BF16 = jnp.bfloat16
MESH = pl.DeviceIdType.MESH

lame_lambda = 0.15
lame_mu = 0.1
gc_length = 0.3
gc_inverse = 40.0
residual_stiff = 0.001
relaxation = 0.5
gll_points = (
    -1.0,
    -0.8717401485096066,
    -0.5917001814331423,
    -0.2092992179024789,
    0.2092992179024789,
    0.5917001814331423,
    0.8717401485096066,
    1.0,
)

EY = (0, 3, 1, 2)
TILE = (0, 2, 3, 1)

DIRS = [
    (dx, dy, dz)
    for dx in (-1, 0, 1)
    for dy in (-1, 0, 1)
    for dz in (-1, 0, 1)
    if (dx, dy, dz) != (0, 0, 0)
]
X_DIRS = [d for d in DIRS if d[1] == 0 and d[2] == 0]
Y_DIRS = [d for d in DIRS if d[0] == 0 and d[1] != 0 and d[2] == 0]
XY_DIRS = [d for d in DIRS if d[0] != 0 and d[1] != 0 and d[2] == 0]
Z_DIRS = [d for d in DIRS if d[2] != 0]
Z_LATE = [d for d in Z_DIRS if d[1] != 0]
Z_EARLY = [d for d in Z_DIRS if d[1] == 0]
Z_ORDER = sorted(Z_DIRS, key=lambda d: -abs(d[0]) - abs(d[1]))


def legendre_at(points, degree):
    values = []
    for point in points:
        previous = 1.0
        current = point
        for level in range(1, degree):
            following = ((2 * level + 1) * point * current - level * previous) / (level + 1)
            previous = current
            current = following
        values.append(current)
    return values


def gll_tables():
    degree = 7
    points = list(gll_points)
    legendre_vals = legendre_at(points, degree)
    weights = [2.0 / (degree * (degree + 1) * entry * entry) for entry in legendre_vals]
    derivative = []
    for row_index in range(degree + 1):
        row_vals = []
        for col_index in range(degree + 1):
            if row_index != col_index:
                row_vals.append(
                    legendre_vals[row_index]
                    / (legendre_vals[col_index] * (points[row_index] - points[col_index]))
                )
            else:
                row_vals.append(0.0)
        derivative.append(row_vals)
    derivative[0][0] = -degree * (degree + 1) / 4.0
    derivative[degree][degree] = degree * (degree + 1) / 4.0
    return (np.array(weights), np.array(derivative))


def split_np(matrix):
    high = matrix.astype(np.float32).astype(ml_dtypes.bfloat16)
    low = (matrix - high.astype(np.float64)).astype(np.float32).astype(ml_dtypes.bfloat16)
    return high, low


def constants():
    _, derivative = gll_tables()
    eye = np.eye
    forward_y = np.kron(eye(2), np.kron(derivative.T, eye(8)))
    forward_z = np.kron(eye(16), derivative.T)
    back_y = np.kron(eye(2), np.kron(derivative, eye(8)))
    back_z = np.kron(eye(16), derivative)
    f_high, f_low = split_np(np.concatenate([forward_y, forward_z], axis=1))
    forward = np.concatenate([f_high, f_high, f_low], axis=0)
    b_high, b_low = split_np(np.concatenate([back_y, back_z], axis=0))
    back = np.concatenate([b_high, b_low], axis=1)
    swap = np.zeros((2, 2, 64, 2, 2, 64))
    for h in range(2):
        for odd in range(2):
            swap[h, odd, :, odd, h, :] = eye(64)
    swap = swap.reshape(256, 256).astype(ml_dtypes.bfloat16)
    return forward, back, swap


def lane_roll(value, shift):
    shift = shift % 128
    if shift == 0:
        return value
    flat = value.reshape(-1, 128)
    return pltpu.roll(flat, shift, 1).reshape(value.shape)


def lane_swap(value, mask):
    flat = value.reshape(-1, 128)
    index = jnp.bitwise_xor(lax.broadcasted_iota(jnp.int32, flat.shape, 1), mask)
    return jnp.take_along_axis(flat, index, axis=1).reshape(value.shape)


def split(value):
    high = value.astype(BF16)
    low = (value - high.astype(F32)).astype(BF16)
    return high, low


def x_derivative(tiles, matrix):
    even_part = (matrix + matrix[:, ::-1]) / 2
    odd_part = (matrix - matrix[:, ::-1]) / 2
    even = [tiles[n] + tiles[7 - n] for n in range(4)]
    odd = [tiles[n] - tiles[7 - n] for n in range(4)]
    out = [None] * 8
    for n in range(4):
        first = float(even_part[n, 0]) * even[0]
        second = float(odd_part[n, 0]) * odd[0]
        for m in range(1, 4):
            first = first + float(even_part[n, m]) * even[m]
            second = second + float(odd_part[n, m]) * odd[m]
        out[n] = second + first
        out[7 - n] = second - first
    return out


def kernel(
    adjoint_h,
    load_h,
    displace_h,
    damage_h,
    history_h,
    frozen_h,
    order_h,
    forward_h,
    back_h,
    swap_h,
    out_ref,
    adjoint_b,
    load_b,
    displace_b,
    damage_b,
    history_b,
    frozen_b,
    order_b,
    forward,
    back,
    swap,
    value,
    kept,
    load,
    summed,
    state,
    keep,
    ys,
    zs,
    xr,
    yr,
    xyr,
    zr,
    in_sem,
    send_sem,
    recv_sem,
):
    weights, derivative = gll_tables()
    px, py, pz = (lax.axis_index("gx"), lax.axis_index("gy"), lax.axis_index("gz"))
    sizes = (lax.axis_size("gx"), lax.axis_size("gy"), lax.axis_size("gz"))

    pairs = (
        (order_h, order_b),
        (adjoint_h, adjoint_b),
        (swap_h, swap),
        (displace_h, displace_b),
        (forward_h, forward),
        (damage_h, damage_b),
        (history_h, history_b),
        (frozen_h, frozen_b),
        (load_h, load_b),
        (back_h, back),
    )
    copies = [pltpu.make_async_copy(src, dst, in_sem.at[n]) for n, (src, dst) in enumerate(pairs)]
    for copy in copies[:3]:
        copy.start()

    along = [
        {
            -1: lax.rem(p + n - 1, n),
            0: p,
            1: lax.rem(p + 1, n),
        }
        for p, n in zip((px, py, pz), sizes)
    ]

    def target(d):
        return tuple(along[axis][d[axis]] for axis in range(3))

    barrier = pltpu.get_barrier_semaphore()
    for d in DIRS:
        pl.semaphore_signal(barrier, inc=1, device_id=target(d), device_id_type=MESH)
    for copy in copies[3:]:
        copy.start()

    present = [
        {
            -1: (p > 0).astype(F32),
            1: (p < n - 1).astype(F32),
        }
        for p, n in zip((px, py, pz), sizes)
    ]

    lane = lax.broadcasted_iota(jnp.int32, (8, 128), 1)
    sub = lax.broadcasted_iota(jnp.int32, (8, 128), 0)
    lane_k = lane % 8
    lane_j = (lane // 8) % 8
    lane_h = lane // 64

    def fmask(condition):
        return jnp.where(condition, 1.0, 0.0).astype(F32)

    j_end = {-1: fmask(lane_j == 0), 1: fmask(lane_j == 7)}
    h_end = {-1: fmask(lane_h == 0), 1: fmask(lane_h == 1)}
    first_z = (lane_h == 0) & (lane_k == 0)
    last_z = (lane_h == 1) & (lane_k == 7)
    z_end = {-1: fmask(first_z), 1: fmask(last_z)}
    inner_z = ((lane_h == 0) & (lane_k == 7)) | ((lane_h == 1) & (lane_k == 0))
    z_here = fmask(inner_z | (last_z & (sub < 7)))
    z_next = fmask(first_z & (sub > 0))

    copies[0].wait()
    row_id = lax.broadcasted_iota(jnp.int32, (64, 64), 0)
    tile_id = (row_id // 8) % 4
    row_ey = jnp.where(tile_id == 1, 3, jnp.where(tile_id > 1, tile_id - 1, 0))
    place = row_ey * 16 + 2 * (row_id % 8) + row_id // 32
    chosen = fmask(place == order_b[...])
    pick = chosen.astype(BF16)
    unpick = chosen.T.astype(BF16)

    def to_tiles(fields):
        sides = []
        for stored in fields:
            rows = jnp.dot(pick, stored, preferred_element_type=F32).astype(BF16)
            for n in range(0, 512, 128):
                sides.append(jnp.concatenate([rows[:32, n : n + 128], rows[32:, n : n + 128]], axis=1))
        tiles = jnp.dot(
            jnp.concatenate(sides, axis=0), swap[...], preferred_element_type=F32
        )
        return tiles.reshape(len(fields) * 4, 32, 256)

    def put_tiles(tiles, places):
        for n, (ref, start) in enumerate(places):
            for a in range(4):
                ref[2 * a, start : start + 32, :] = tiles[4 * n + a, :, :128]
                ref[2 * a + 1, start : start + 32, :] = tiles[4 * n + a, :, 128:]

    def group(ref, start, rows, fields=4):
        return jnp.stack(
            [ref[:, f * 32 + start : f * 32 + start + rows, :] for f in range(fields)], axis=1
        )

    def put_group(ref, start, rows, block):
        for f in range(4):
            ref[:, f * 32 + start : f * 32 + start + rows, :] = block[:, f]

    def sum_z(block):
        flat = block.reshape(-1, 8, 128)
        taken = lane_swap(jnp.where(first_z, pltpu.roll(flat, 7, 1), flat), 71)
        total = flat + z_here * taken + z_next * pltpu.roll(taken, 1, 1)
        return total.reshape(block.shape)

    def sum_y(e):
        lower, upper = 8 * TILE[e], 8 * TILE[e + 1]
        here, beyond = group(summed, lower, 8), group(summed, upper, 8)
        taken = lane_swap(jnp.where(lane_j == 7, here, beyond), 56)
        put_group(summed, lower, 8, here + j_end[1] * taken)
        put_group(summed, upper, 8, beyond + j_end[-1] * taken)

    def pack_z(r):
        for n, (row, h, k) in enumerate(((0, 0, 0), (7, 1, 7))):
            packed = jnp.zeros((8, 128), F32)
            for slot in range(16):
                i, half = slot // 2, slot % 2
                piece = summed[i, pl.ds(half * 64 + row, 8, stride=8), :]
                moved = lane_roll(piece, (slot // 8 - h) * 64 + slot % 8 - k)
                packed = jnp.where((lane_h == slot // 8) & (lane_k == slot % 8), moved, packed)
            zs[r, n] = packed

    def pack_y(r):
        for n, (t, j) in enumerate(((0, 0), (1, 7))):
            for g in range(4):
                packed = jnp.zeros((8, 128), F32)
                for slot in range(8):
                    row = (slot // 2) * 32 + 8 * t
                    piece = summed[2 * g + slot % 2, row : row + 8, :]
                    packed = jnp.where(lane_j == slot, lane_roll(piece, 8 * (slot - j)), packed)
                ys[r, n, g] = packed

    def message(r, d):
        n = DIRS.index(d)
        dx, dy, dz = d
        if d in X_DIRS:
            src, dst = summed.at[7 if dx > 0 else 0], xr.at[r, (dx + 1) // 2]
        elif d in Y_DIRS:
            src, dst = ys.at[r, (dy + 1) // 2], yr.at[r, (dy + 1) // 2]
        elif d in XY_DIRS:
            src, dst = ys.at[r, (dy + 1) // 2, 3 if dx > 0 else 0], xyr.at[r, XY_DIRS.index(d)]
        else:
            src, dst = zs.at[r, (dz + 1) // 2], zr.at[r, Z_DIRS.index(d)]
        return pltpu.make_async_remote_copy(
            src_ref=src,
            dst_ref=dst,
            send_sem=send_sem.at[r, n],
            recv_sem=recv_sem.at[r, n],
            device_id=target(d),
            device_id_type=MESH,
        )

    def send(r, messages, dirs):
        for d in dirs:
            messages[d] = message(r, d)
            messages[d].start()

    def finish(messages):
        for d in DIRS:
            messages[d].wait_send()

    def add_z(r, messages, dirs):
        for dz in (-1, 1):
            side = -dz
            face = None
            for d in dirs:
                if d[2] != dz:
                    continue
                messages[d].wait_recv()
                part = zr[r, Z_DIRS.index(d)]
                dx, dy, _ = d
                wanted = None
                if dx != 0:
                    slots = (lane_k < 2) if dx > 0 else (lane_k >= 6)
                    wanted = h_end[-dx] * fmask(slots) * present[0][-dx]
                if dy != 0:
                    mine = j_end[-dy] * fmask(sub % 4 == (0 if dy > 0 else 1)) * present[1][-dy]
                    wanted = mine if wanted is None else wanted * mine
                    part = pltpu.roll(part, -dy % 8, 0)
                part = lane_roll(part, -70 * dx - 56 * dy)
                if wanted is not None:
                    part = part * wanted
                face = part if face is None else face + part
            row, h, k = (0, 0, 0) if side < 0 else (7, 1, 7)
            wanted = z_end[side] * present[2][side]
            for slot in range(16):
                i, half = slot // 2, slot % 2
                where = pl.ds(half * 64 + row, 8, stride=8)
                moved = lane_roll(face, (h - slot // 8) * 64 + k - slot % 8)
                value[i, where, :] = value[i, where, :] + moved * wanted

    def receive_early(r, messages):
        for i in range(1, 7):
            value[i] = summed[i]
        for d in X_DIRS:
            messages[d].wait_recv()
            i = 0 if d[0] > 0 else 7
            value[i] = summed[i] + xr[r, (d[0] + 1) // 2] * present[0][-d[0]]
        add_z(r, messages, Z_EARLY)

    def receive_late(r, messages):
        for d in Y_DIRS:
            messages[d].wait_recv()
            dy = d[1]
            side = -dy
            faces = [yr[r, (dy + 1) // 2, g] for g in range(4)]
            for dx in (-1, 1):
                e = (dx, dy, 0)
                messages[e].wait_recv()
                edge = lane_roll(xyr[r, XY_DIRS.index(e)], -8 * dx)
                wanted = fmask(lane_j % 2 == (0 if dx > 0 else 1)) * present[0][-dx]
                g = 0 if dx > 0 else 3
                faces[g] = faces[g] + edge * wanted
            t, j = (0, 0) if side < 0 else (1, 7)
            wanted = j_end[side] * present[1][side]
            for i in range(8):
                for f in range(4):
                    slot = f * 2 + i % 2
                    row = f * 32 + 8 * t
                    moved = lane_roll(faces[i // 2], 8 * (j - slot))
                    value[i, row : row + 8, :] = value[i, row : row + 8, :] + moved * wanted
        add_z(r, messages, Z_LATE)

    def brick():
        line_j = jnp.zeros((8, 128), F32)
        line_k = jnp.zeros((8, 128), F32)
        for n in range(8):
            line_j = jnp.where(lane_j == n, float(weights[n]), line_j)
            line_k = jnp.where(lane_k == n, float(weights[n]), line_k)
        plane = (line_j * line_k)[:1]
        return jnp.stack([plane * float(weights[n]) for n in range(8)])

    def gradients(block, exact):
        if exact:
            high = block.reshape(-1, 128).astype(BF16)
            left, table = jnp.concatenate([high, high], axis=1), forward[128:384, :]
        else:
            high, low = split(block.reshape(-1, 128))
            left, table = jnp.concatenate([high, low, high], axis=1), forward[...]
        yz = jnp.dot(left, table, preferred_element_type=F32)
        gx = jnp.stack(x_derivative([block[i] for i in range(8)], derivative))
        return gx, yz[:, :128].reshape(block.shape), yz[:, 128:].reshape(block.shape)

    def state_terms(start):
        rows = slice(start, start + 16)
        moved = group(value, start, 16, 3)
        gx, gy, gz = gradients(moved, True)
        shear = [gy[:, 0] + gx[:, 1], gz[:, 0] + gx[:, 2], gz[:, 1] + gy[:, 2]]
        normal = [gx[:, 0], gy[:, 1], gz[:, 2]]
        trace_sum = normal[0] + normal[1] + normal[2]
        stress = [lame_lambda * trace_sum + 2.0 * lame_mu * n for n in normal]
        stress += [lame_mu * s for s in shear]
        energy = stress[0] * normal[0] + stress[1] * normal[1] + stress[2] * normal[2]
        energy = 0.5 * (energy + stress[3] * shear[0] + stress[4] * shear[1] + stress[5] * shear[2])
        loading = keep[2, 0, rows, :][None]
        driving = (1.0 - loading) * keep[1, :, rows, :] + loading * energy
        intact = 1.0 - keep[0, :, rows, :]
        mass = brick()
        slope = -2.0 * intact * mass
        for n in range(6):
            state[n, :, rows, :] = slope * stress[n]
        state[6, :, rows, :] = lame_mu * mass * (intact * intact + residual_stiff)
        state[7, :, rows, :] = mass * (gc_inverse + 2.0 * driving)

    def apply_transposed(start, block):
        rows = slice(start, start + 16)
        gx, gy, gz = gradients(block, False)
        scaled = [state[n, :, rows, :] for n in range(6)]
        stiff = state[6, :, rows, :]
        vd = block[:, 3]
        coupled = keep[2, 0, rows, :][None] * vd
        shear = [gy[:, 0] + gx[:, 1], gz[:, 0] + gx[:, 2], gz[:, 1] + gy[:, 2]]
        normal = [gx[:, 0], gy[:, 1], gz[:, 2]]
        trace_sum = 1.5 * (normal[0] + normal[1] + normal[2])
        tensor = [stiff * (trace_sum + 2.0 * normal[n]) + scaled[n] * coupled for n in range(3)]
        tensor += [stiff * shear[n] + scaled[n + 3] * coupled for n in range(3)]
        nodal = state[7, :, rows, :] * vd
        for n in range(3):
            nodal = nodal + scaled[n] * normal[n] + scaled[n + 3] * shear[n]
        flux = gc_length * brick()
        along_x = jnp.stack([tensor[0], tensor[3], tensor[4], flux * gx[:, 3]], axis=1)
        along_y = jnp.stack([tensor[3], tensor[1], tensor[5], flux * gy[:, 3]], axis=1)
        along_z = jnp.stack([tensor[4], tensor[5], tensor[2], flux * gz[:, 3]], axis=1)
        y_high, y_low = split(along_y.reshape(-1, 128))
        z_high, z_low = split(along_z.reshape(-1, 128))
        one = jnp.dot(
            jnp.concatenate([y_high, z_high], axis=1), back[...], preferred_element_type=F32
        )
        two = jnp.dot(
            jnp.concatenate([y_low, z_low], axis=1), back[:, :128], preferred_element_type=F32
        )
        total = (one[:, :128] + one[:, 128:] + two).reshape(block.shape)
        total = total + jnp.stack(x_derivative([along_x[i] for i in range(8)], derivative.T))
        result = group(load, start, 16) - total
        result = jnp.concatenate([result[:, :3], (result[:, 3] - nodal)[:, None]], axis=1)
        put_group(summed, start, 16, sum_z(result))

    def ship(r):
        messages = {}
        pack_z(r)
        if r == 0:
            pl.semaphore_wait(barrier, len(DIRS))
        send(r, messages, Z_ORDER)
        send(r, messages, X_DIRS)
        pack_y(r)
        send(r, messages, XY_DIRS + Y_DIRS)
        return messages

    copies[1].wait()
    copies[2].wait()
    put_tiles(to_tiles([adjoint_b[f] for f in range(4)]), [(summed, f * 32) for f in range(4)])
    for start in (0, 16):
        put_group(summed, start, 16, sum_z(group(summed, start, 16)))
    for e in range(3):
        sum_y(e)
    messages = ship(0)

    copies[3].wait()
    copies[4].wait()
    copies[5].wait()
    copies[6].wait()
    put_tiles(
        to_tiles([displace_b[0], displace_b[1], displace_b[2], damage_b[...], history_b[...]]),
        [(value, 0), (value, 32), (value, 64), (keep.at[0], 0), (keep.at[1], 0)],
    )
    copies[7].wait()
    frozen = 1.0 - jnp.sum(chosen * frozen_b[...].astype(F32), axis=1, keepdims=True)
    low_half = lax.broadcasted_iota(jnp.int32, (32, 128), 1) < 64
    keep[2, 0] = jnp.where(low_half, frozen[:32], frozen[32:])
    for start in (0, 16):
        state_terms(start)
    copies[8].wait()
    put_tiles(to_tiles([load_b[f] for f in range(4)]), [(load, f * 32) for f in range(4)])
    copies[9].wait()

    def halved(condition, scalar):
        return 1.0 - 0.5 * fmask(condition) * scalar

    inv_z = halved(inner_z, 1.0) * halved(first_z & (sub > 0), 1.0) * halved(last_z & (sub < 7), 1.0)
    inv_z = inv_z * halved(first_z & (sub == 0), present[2][-1]) * halved(last_z & (sub == 7), present[2][1])

    def average(start):
        planes = []
        for t in (start // 8, start // 8 + 1):
            lower = 1.0 if EY[t] > 0 else present[1][-1]
            upper = 1.0 if EY[t] < 3 else present[1][1]
            planes.append(inv_z * halved(lane_j == 0, lower) * halved(lane_j == 7, upper))
        scale = jnp.concatenate(planes, axis=0)
        scales = [scale] * 8
        scales[0] = scale * (1.0 - 0.5 * present[0][-1])
        scales[7] = scale * (1.0 - 0.5 * present[0][1])
        block = group(value, start, 16) * jnp.stack(scales)[:, None]
        put_group(kept, start, 16, block)
        return block

    def relax(start):
        return group(kept, start, 16) + relaxation * group(value, start, 16)

    for r, ready in ((0, average), (1, relax)):
        receive_early(r, messages)
        finish(messages)
        apply_transposed(16, ready(16))
        sum_y(1)
        receive_late(r, messages)
        apply_transposed(0, ready(0))
        sum_y(0)
        sum_y(2)
        messages = ship(r + 1)

    receive_early(2, messages)
    receive_late(2, messages)
    twice = jnp.concatenate([unpick, unpick], axis=1)
    for f in range(4):
        rows = slice(f * 32, f * 32 + 32)
        sides = jnp.stack(
            [jnp.concatenate([value[2 * a, rows, :], value[2 * a + 1, rows, :]], axis=1) for a in range(4)]
        )
        high, low = split(sides.reshape(128, 256))
        both = jnp.concatenate([high, low], axis=0)
        moved = jnp.dot(both, swap[...], preferred_element_type=F32).astype(BF16)
        for a in range(4):
            parts = []
            for n in (a * 32, 128 + a * 32):
                parts += [moved[n : n + 32, :128], moved[n : n + 32, 128:]]
            stacked = jnp.concatenate(parts, axis=0)
            out_ref[f, :, a * 128 : a * 128 + 128] = jnp.dot(
                twice, stacked, preferred_element_type=F32
            )
    finish(messages)


def shards(adjoint, load, displace, damage, history, frozen, order):
    forward, back, swap = (jnp.asarray(c) for c in constants())
    hbm = pl.BlockSpec(memory_space=pltpu.HBM)
    return pl.pallas_call(
        kernel,
        out_shape=jax.ShapeDtypeStruct((4, 64, 512), F32),
        in_specs=[hbm] * 10,
        out_specs=pl.BlockSpec(memory_space=pltpu.VMEM),
        scratch_shapes=[
            pltpu.VMEM((4, 64, 512), BF16),
            pltpu.VMEM((4, 64, 512), BF16),
            pltpu.VMEM((3, 64, 512), BF16),
            pltpu.VMEM((64, 512), BF16),
            pltpu.VMEM((64, 512), BF16),
            pltpu.VMEM((1, 64), jnp.int32),
            pltpu.VMEM((1, 64), jnp.int32),
            pltpu.VMEM((384, 256), BF16),
            pltpu.VMEM((256, 256), BF16),
            pltpu.VMEM((256, 256), BF16),
            pltpu.VMEM((8, 128, 128), F32),
            pltpu.VMEM((8, 128, 128), F32),
            pltpu.VMEM((8, 128, 128), F32),
            pltpu.VMEM((8, 128, 128), F32),
            pltpu.VMEM((8, 8, 32, 128), F32),
            pltpu.VMEM((3, 8, 32, 128), F32),
            pltpu.VMEM((3, 2, 4, 8, 128), F32),
            pltpu.VMEM((3, 2, 8, 128), F32),
            pltpu.VMEM((3, 2, 128, 128), F32),
            pltpu.VMEM((3, 2, 4, 8, 128), F32),
            pltpu.VMEM((3, 4, 8, 128), F32),
            pltpu.VMEM((3, 18, 8, 128), F32),
            pltpu.SemaphoreType.DMA((10,)),
            pltpu.SemaphoreType.DMA((3, 26)),
            pltpu.SemaphoreType.DMA((3, 26)),
        ],
        compiler_params=pltpu.CompilerParams(
            collective_id=0, has_side_effects=True, vmem_limit_bytes=56 * 1024 * 1024
        ),
    )(adjoint, load, displace, damage, history, frozen.reshape(1, 64), order, forward, back, swap)


def solution(mesh):
    in_specs = (
        P(None, ("gx", "gy", "gz"), None),
        P(None, ("gx", "gy", "gz"), None),
        P(None, ("gx", "gy", "gz"), None),
        P(("gx", "gy", "gz"), None),
        P(("gx", "gy", "gz"), None),
        P(("gx", "gy", "gz")),
        P(("gx", "gy", "gz"), None),
    )
    out_specs = P(None, ("gx", "gy", "gz"), None)
    return jax.shard_map(shards, mesh=mesh, in_specs=in_specs, out_specs=out_specs, check_vma=False)
```

```python
import jax
import jax.numpy as jnp
import ml_dtypes
import numpy as np
from jax import lax
from jax.experimental import pallas as pl
from jax.experimental.pallas import tpu as pltpu
from jax.sharding import PartitionSpec as P

F32 = jnp.float32
BF16 = jnp.bfloat16
MESH = pl.DeviceIdType.MESH

lame_lambda = 0.15
lame_mu = 0.1
gc_length = 0.3
gc_inverse = 40.0
residual_stiff = 0.001
relaxation = 0.5
gll_points = (
    -1.0,
    -0.8717401485096066,
    -0.5917001814331423,
    -0.2092992179024789,
    0.2092992179024789,
    0.5917001814331423,
    0.8717401485096066,
    1.0,
)

EY = ((3, 0), (1, 2))
START = {ey: 64 * half + 8 * tile for half in range(2) for tile, ey in enumerate(EY[half])}

DIRS = [
    (dx, dy, dz)
    for dx in (-1, 0, 1)
    for dy in (-1, 0, 1)
    for dz in (-1, 0, 1)
    if (dx, dy, dz) != (0, 0, 0)
]
X_DIRS = [d for d in DIRS if d[1] == 0 and d[2] == 0]
Y_DIRS = [d for d in DIRS if d[0] == 0 and d[1] != 0 and d[2] == 0]
XY_DIRS = [d for d in DIRS if d[0] != 0 and d[1] != 0 and d[2] == 0]
Z_DIRS = [d for d in DIRS if d[2] != 0]
Z_LATE = [d for d in Z_DIRS if d[1] != 0]
Z_EARLY = [d for d in Z_DIRS if d[1] == 0]
Z_ORDER = sorted(Z_DIRS, key=lambda d: -abs(d[0]) - abs(d[1]))


def legendre_at(points, degree):
    values = []
    for point in points:
        previous = 1.0
        current = point
        for level in range(1, degree):
            following = ((2 * level + 1) * point * current - level * previous) / (level + 1)
            previous = current
            current = following
        values.append(current)
    return values


def gll_tables():
    degree = 7
    points = list(gll_points)
    legendre_vals = legendre_at(points, degree)
    weights = [2.0 / (degree * (degree + 1) * entry * entry) for entry in legendre_vals]
    derivative = []
    for row_index in range(degree + 1):
        row_vals = []
        for col_index in range(degree + 1):
            if row_index != col_index:
                row_vals.append(
                    legendre_vals[row_index]
                    / (legendre_vals[col_index] * (points[row_index] - points[col_index]))
                )
            else:
                row_vals.append(0.0)
        derivative.append(row_vals)
    derivative[0][0] = -degree * (degree + 1) / 4.0
    derivative[degree][degree] = degree * (degree + 1) / 4.0
    return (np.array(weights), np.array(derivative))


def split_np(matrix):
    high = matrix.astype(np.float32).astype(ml_dtypes.bfloat16)
    low = (matrix - high.astype(np.float64)).astype(np.float32).astype(ml_dtypes.bfloat16)
    return high, low


def constants():
    _, derivative = gll_tables()
    eye = np.eye
    forward_y = np.kron(eye(2), np.kron(derivative.T, eye(8)))
    forward_z = np.kron(eye(16), derivative.T)
    back_y = np.kron(eye(2), np.kron(derivative, eye(8)))
    back_z = np.kron(eye(16), derivative)
    f_high, f_low = split_np(np.concatenate([forward_y, forward_z], axis=1))
    forward = np.concatenate([f_high, f_high, f_low], axis=0)
    b_high, b_low = split_np(np.concatenate([back_y, back_z], axis=0))
    back = np.concatenate([b_high, b_low], axis=1)
    swap = np.zeros((2, 2, 64, 2, 2, 64))
    for h in range(2):
        for odd in range(2):
            swap[h, odd, :, odd, h, :] = eye(64)
    swap = swap.reshape(256, 256).astype(ml_dtypes.bfloat16)
    return forward, back, swap


def lane_roll(value, shift):
    shift = shift % 128
    if shift == 0:
        return value
    flat = value.reshape(-1, 128)
    return pltpu.roll(flat, shift, 1).reshape(value.shape)


def lane_swap(value, mask):
    flat = value.reshape(-1, 128)
    index = jnp.bitwise_xor(lax.broadcasted_iota(jnp.int32, flat.shape, 1), mask)
    return jnp.take_along_axis(flat, index, axis=1).reshape(value.shape)


def split(value):
    high = value.astype(BF16)
    low = (value - high.astype(F32)).astype(BF16)
    return high, low


def x_derivative(tiles, matrix):
    even_part = (matrix + matrix[:, ::-1]) / 2
    odd_part = (matrix - matrix[:, ::-1]) / 2
    even = [tiles[n] + tiles[7 - n] for n in range(4)]
    odd = [tiles[n] - tiles[7 - n] for n in range(4)]
    out = [None] * 8
    for n in range(4):
        first = float(even_part[n, 0]) * even[0]
        second = float(odd_part[n, 0]) * odd[0]
        for m in range(1, 4):
            first = first + float(even_part[n, m]) * even[m]
            second = second + float(odd_part[n, m]) * odd[m]
        out[n] = second + first
        out[7 - n] = second - first
    return out


def kernel(
    adjoint_h,
    load_h,
    displace_h,
    damage_h,
    history_h,
    frozen_h,
    order_h,
    forward_h,
    back_h,
    swap_h,
    out_ref,
    adjoint_b,
    load_b,
    displace_b,
    damage_b,
    history_b,
    frozen_b,
    order_b,
    forward,
    back,
    swap,
    value,
    kept,
    load,
    summed,
    state,
    keep,
    ys,
    zs,
    xr,
    yr,
    xyr,
    zr,
    in_sem,
    send_sem,
    recv_sem,
):
    weights, derivative = gll_tables()
    px, py, pz = (lax.axis_index("gx"), lax.axis_index("gy"), lax.axis_index("gz"))
    sizes = (lax.axis_size("gx"), lax.axis_size("gy"), lax.axis_size("gz"))

    pairs = (
        (order_h, order_b),
        (adjoint_h, adjoint_b),
        (swap_h, swap),
        (displace_h, displace_b),
        (forward_h, forward),
        (damage_h, damage_b),
        (history_h, history_b),
        (frozen_h, frozen_b),
        (load_h, load_b),
        (back_h, back),
    )
    copies = [pltpu.make_async_copy(src, dst, in_sem.at[n]) for n, (src, dst) in enumerate(pairs)]
    for copy in copies[:3]:
        copy.start()

    along = [
        {
            -1: lax.rem(p + n - 1, n),
            0: p,
            1: lax.rem(p + 1, n),
        }
        for p, n in zip((px, py, pz), sizes)
    ]

    def target(d):
        return tuple(along[axis][d[axis]] for axis in range(3))

    has = [{-1: p > 0, 1: p < n - 1} for p, n in zip((px, py, pz), sizes)]
    present = [{s: side[s].astype(F32) for s in (-1, 1)} for side in has]

    def there(d):
        sides = [has[axis][d[axis]] for axis in range(3) if d[axis] != 0]
        found = sides[0]
        for side in sides[1:]:
            found = jnp.logical_and(found, side)
        return found

    to_there = {d: there(d) for d in DIRS}

    def from_there(d):
        return to_there[(-d[0], -d[1], -d[2])]

    barrier = pltpu.get_barrier_semaphore()
    for d in DIRS:

        @pl.when(to_there[d])
        def _(d=d):
            pl.semaphore_signal(barrier, inc=1, device_id=target(d), device_id_type=MESH)

    around = [1 + side[-1].astype(jnp.int32) + side[1].astype(jnp.int32) for side in has]
    neighbours = around[0] * around[1] * around[2] - 1
    for copy in copies[3:]:
        copy.start()

    lane = lax.broadcasted_iota(jnp.int32, (8, 128), 1)
    sub = lax.broadcasted_iota(jnp.int32, (8, 128), 0)
    lane_k = lane % 8
    lane_j = (lane // 8) % 8
    lane_h = lane // 64

    def fmask(condition):
        return jnp.where(condition, 1.0, 0.0).astype(F32)

    j_end = {-1: fmask(lane_j == 0), 1: fmask(lane_j == 7)}
    h_end = {-1: fmask(lane_h == 0), 1: fmask(lane_h == 1)}
    first_z = (lane_h == 0) & (lane_k == 0)
    last_z = (lane_h == 1) & (lane_k == 7)
    z_end = {-1: fmask(first_z), 1: fmask(last_z)}
    inner_z = ((lane_h == 0) & (lane_k == 7)) | ((lane_h == 1) & (lane_k == 0))
    z_here = fmask(inner_z | (last_z & (sub < 7)))
    z_next = fmask(first_z & (sub > 0))

    copies[0].wait()
    row_id = lax.broadcasted_iota(jnp.int32, (64, 64), 0)
    tile_id = (row_id // 8) % 4
    row_ey = (tile_id + 3) % 4
    place = row_ey * 16 + 2 * (row_id % 8) + row_id // 32
    chosen = fmask(place == order_b[...])
    pick = chosen.astype(BF16)
    unpick = chosen.T.astype(BF16)

    def to_tiles(fields):
        sides = []
        for stored in fields:
            rows = jnp.dot(pick, stored, preferred_element_type=F32).astype(BF16)
            for n in range(0, 512, 128):
                sides.append(jnp.concatenate([rows[:32, n : n + 128], rows[32:, n : n + 128]], axis=1))
        tiles = jnp.dot(
            jnp.concatenate(sides, axis=0), swap[...], preferred_element_type=F32
        )
        return tiles.reshape(len(fields) * 4, 32, 256)

    def put_fields(tiles, ref, fields):
        for f in range(fields):
            for a in range(4):
                for half in range(2):
                    rows = slice(half * 64 + f * 16, half * 64 + f * 16 + 16)
                    both = tiles[4 * f + a, half * 16 : half * 16 + 16, :]
                    ref[2 * a, rows, :] = both[:, :128]
                    ref[2 * a + 1, rows, :] = both[:, 128:]

    def put_single(tiles, n):
        for a in range(4):
            keep[n, 2 * a] = tiles[a, :, :128]
            keep[n, 2 * a + 1] = tiles[a, :, 128:]

    def group(ref, half):
        return ref[:, half * 64 : half * 64 + 64, :].reshape(8, 4, 16, 128)

    def put_group(ref, half, block):
        ref[:, half * 64 : half * 64 + 64, :] = block.reshape(8, 64, 128)

    def sum_z(block):
        flat = block.reshape(-1, 8, 128)
        taken = lane_swap(jnp.where(first_z, pltpu.roll(flat, 7, 1), flat), 71)
        total = flat + z_here * taken + z_next * pltpu.roll(taken, 1, 1)
        return total.reshape(block.shape)

    def sum_y(e, spans=((0, 8),)):
        for first, last in spans:
            for f in range(4):
                lower = slice(START[e] + f * 16, START[e] + f * 16 + 8)
                upper = slice(START[e + 1] + f * 16, START[e + 1] + f * 16 + 8)
                here, beyond = summed[first:last, lower, :], summed[first:last, upper, :]
                taken = lane_swap(jnp.where(lane_j == 7, here, beyond), 56)
                summed[first:last, lower, :] = here + j_end[1] * taken
                summed[first:last, upper, :] = beyond + j_end[-1] * taken

    def mask_of(half, tile, j):
        return fmask((lane_k % 2 == half) & (sub % 2 == tile) & (lane_j == j))

    inner_i = fmask(((lane_h == 1) | (lane_k > 1)) & ((lane_h == 0) | (lane_k < 6)))
    packed_y = []
    for ey in (0, 2):
        half, tile = (START[ey] // 64, (START[ey] // 8) % 2)
        half_up, tile_up = (START[ey + 1] // 64, (START[ey + 1] // 8) % 2)
        packed_y.append((inner_i * mask_of(half, tile, 7), tile - tile_up, 56 + half - half_up))
        packed_y.append((inner_i * mask_of(half_up, tile_up, 0), tile_up - tile, half_up - half - 56))

    def packed_sum_y(face):
        total = face
        for wanted, tiles, lanes in packed_y:
            total = total + wanted * lane_roll(pltpu.roll(face, tiles % 8, 0), lanes)
        return total

    def pack_z(r):
        for n, (row, h, k) in enumerate(((0, 0, 0), (7, 1, 7))):
            packed = jnp.zeros((8, 128), F32)
            for slot in range(16):
                i, half = slot // 2, slot % 2
                piece = summed[i, pl.ds(half * 64 + row, 8, stride=8), :]
                moved = lane_roll(piece, (slot // 8 - h) * 64 + slot % 8 - k)
                packed = jnp.where((lane_h == slot // 8) & (lane_k == slot % 8), moved, packed)
            zs[r, n] = packed_sum_y(packed)

    def pack_y(r):
        for n, (ey, j) in enumerate(((0, 0), (3, 7))):
            for g in range(4):
                packed = jnp.zeros((8, 128), F32)
                for slot in range(8):
                    row = (slot // 2) * 16 + START[ey]
                    piece = summed[2 * g + slot % 2, row : row + 8, :]
                    packed = jnp.where(lane_j == slot, lane_roll(piece, 8 * (slot - j)), packed)
                ys[r, n, g] = packed

    def message(r, d, half=0):
        n = DIRS.index(d)
        dx, dy, dz = d
        if d in X_DIRS:
            rows = pl.ds(64 * half, 64)
            src, dst = summed.at[7 if dx > 0 else 0, rows], xr.at[r, (dx + 1) // 2, rows]
            n = n if half == 0 else 26 + (dx + 1) // 2
        elif d in Y_DIRS:
            src, dst = ys.at[r, (dy + 1) // 2], yr.at[r, (dy + 1) // 2]
        elif d in XY_DIRS:
            src, dst = ys.at[r, (dy + 1) // 2, 3 if dx > 0 else 0], xyr.at[r, XY_DIRS.index(d)]
        else:
            src, dst = zs.at[r, (dz + 1) // 2], zr.at[r, Z_DIRS.index(d)]
        return pltpu.make_async_remote_copy(
            src_ref=src,
            dst_ref=dst,
            send_sem=send_sem.at[r, n],
            recv_sem=recv_sem.at[r, n],
            device_id=target(d),
            device_id_type=MESH,
        )

    def send(r, dirs, half=0):
        for d in dirs:
            pl.when(to_there[d])(message(r, d, half).start)

    def finish(r):
        for d in DIRS:
            pl.when(to_there[d])(message(r, d).wait_send)
        for d in X_DIRS:
            pl.when(to_there[d])(message(r, d, 1).wait_send)

    def arrive(r, dirs, half=0):
        for d in dirs:
            pl.when(from_there(d))(message(r, d, half).wait_recv)

    def arrived(d, data):
        return lax.select(from_there(d), data, jnp.zeros_like(data))

    def z_faces(r, dirs):
        arrive(r, dirs)
        faces = []
        for dz in (-1, 1):
            face = None
            for d in dirs:
                if d[2] != dz:
                    continue
                part = arrived(d, zr[r, Z_DIRS.index(d)])
                dx, dy, _ = d
                wanted = None
                if dx != 0:
                    slots = (lane_k < 2) if dx > 0 else (lane_k >= 6)
                    wanted = h_end[-dx] * fmask(slots)
                if dy != 0:
                    mine = mask_of(0, 1 if dy > 0 else 0, 0 if dy > 0 else 7)
                    wanted = mine if wanted is None else wanted * mine
                    part = pltpu.roll(part, dy % 8, 0)
                part = lane_roll(part, -70 * dx - 56 * dy)
                if wanted is not None:
                    part = part * wanted
                face = part if face is None else face + part
            faces.append(face)
        return faces

    def add_z(faces, half):
        for dz, face in zip((-1, 1), faces):
            row, h, k = (0, 0, 0) if dz > 0 else (7, 1, 7)
            for i in range(8):
                slot = 2 * i + half
                where = pl.ds(half * 64 + row, 8, stride=8)
                moved = lane_roll(face, (h - slot // 8) * 64 + k - slot % 8)
                value[i, where, :] = value[i, where, :] + moved * z_end[-dz]

    def take_x(r, half):
        rows = slice(64 * half, 64 * half + 64)
        arrive(r, X_DIRS, half)
        for i in range(1, 7):
            value[i, rows, :] = summed[i, rows, :]
        for d in X_DIRS:
            i = 0 if d[0] > 0 else 7
            value[i, rows, :] = summed[i, rows, :] + arrived(d, xr[r, (d[0] + 1) // 2, rows, :])

    def receive_early(r):
        take_x(r, 1)
        faces = z_faces(r, Z_EARLY)
        add_z(faces, 1)
        return faces

    def receive_late(r, faces):
        take_x(r, 0)
        arrive(r, Y_DIRS + XY_DIRS)
        for d in Y_DIRS:
            dy = d[1]
            sides = [arrived(d, yr[r, (dy + 1) // 2, g]) for g in range(4)]
            for dx in (-1, 1):
                e = (dx, dy, 0)
                edge = lane_roll(arrived(e, xyr[r, XY_DIRS.index(e)]), -8 * dx)
                g = 0 if dx > 0 else 3
                sides[g] = sides[g] + edge * fmask(lane_j % 2 == (0 if dx > 0 else 1))
            ey, j = (0, 0) if dy > 0 else (3, 7)
            for i in range(8):
                for f in range(4):
                    row = f * 16 + START[ey]
                    moved = lane_roll(sides[i // 2], 8 * (j - f * 2 - i % 2))
                    value[i, row : row + 8, :] = value[i, row : row + 8, :] + moved * j_end[-dy]
        late = z_faces(r, Z_LATE)
        add_z([face + more for face, more in zip(faces, late)], 0)

    def brick():
        line_j = jnp.zeros((8, 128), F32)
        line_k = jnp.zeros((8, 128), F32)
        for n in range(8):
            line_j = jnp.where(lane_j == n, float(weights[n]), line_j)
            line_k = jnp.where(lane_k == n, float(weights[n]), line_k)
        plane = (line_j * line_k)[:1]
        return jnp.stack([plane * float(weights[n]) for n in range(8)])

    def gradients(block, exact):
        if exact:
            high = block.reshape(-1, 128).astype(BF16)
            left, table = jnp.concatenate([high, high], axis=1), forward[128:384, :]
        else:
            high, low = split(block.reshape(-1, 128))
            left, table = jnp.concatenate([high, low, high], axis=1), forward[...]
        yz = jnp.dot(left, table, preferred_element_type=F32)
        gx = jnp.stack(x_derivative([block[i] for i in range(8)], derivative))
        return gx, yz[:, :128].reshape(block.shape), yz[:, 128:].reshape(block.shape)

    def state_terms(half):
        rows = slice(16 * half, 16 * half + 16)
        moved = group(value, half)[:, :3]
        gx, gy, gz = gradients(moved, True)
        shear = [gy[:, 0] + gx[:, 1], gz[:, 0] + gx[:, 2], gz[:, 1] + gy[:, 2]]
        normal = [gx[:, 0], gy[:, 1], gz[:, 2]]
        trace_sum = normal[0] + normal[1] + normal[2]
        stress = [lame_lambda * trace_sum + 2.0 * lame_mu * n for n in normal]
        stress += [lame_mu * s for s in shear]
        energy = stress[0] * normal[0] + stress[1] * normal[1] + stress[2] * normal[2]
        energy = 0.5 * (energy + stress[3] * shear[0] + stress[4] * shear[1] + stress[5] * shear[2])
        loading = keep[2, 0, rows, :][None]
        driving = (1.0 - loading) * keep[1, :, rows, :] + loading * energy
        intact = 1.0 - keep[0, :, rows, :]
        mass = brick()
        slope = -2.0 * intact * mass
        for n in range(6):
            state[n, :, rows, :] = slope * stress[n]
        state[6, :, rows, :] = lame_mu * mass * (intact * intact + residual_stiff)
        state[7, :, rows, :] = mass * (gc_inverse + 2.0 * driving)

    def apply_transposed(half, block):
        rows = slice(16 * half, 16 * half + 16)
        gx, gy, gz = gradients(block, False)
        scaled = [state[n, :, rows, :] for n in range(6)]
        stiff = state[6, :, rows, :]
        vd = block[:, 3]
        coupled = keep[2, 0, rows, :][None] * vd
        shear = [gy[:, 0] + gx[:, 1], gz[:, 0] + gx[:, 2], gz[:, 1] + gy[:, 2]]
        normal = [gx[:, 0], gy[:, 1], gz[:, 2]]
        trace_sum = 1.5 * (normal[0] + normal[1] + normal[2])
        tensor = [stiff * (trace_sum + 2.0 * normal[n]) + scaled[n] * coupled for n in range(3)]
        tensor += [stiff * shear[n] + scaled[n + 3] * coupled for n in range(3)]
        nodal = state[7, :, rows, :] * vd
        for n in range(3):
            nodal = nodal + scaled[n] * normal[n] + scaled[n + 3] * shear[n]
        flux = gc_length * brick()
        along_x = jnp.stack([tensor[0], tensor[3], tensor[4], flux * gx[:, 3]], axis=1)
        along_y = jnp.stack([tensor[3], tensor[1], tensor[5], flux * gy[:, 3]], axis=1)
        along_z = jnp.stack([tensor[4], tensor[5], tensor[2], flux * gz[:, 3]], axis=1)
        y_high, y_low = split(along_y.reshape(-1, 128))
        z_high, z_low = split(along_z.reshape(-1, 128))
        one = jnp.dot(
            jnp.concatenate([y_high, z_high], axis=1), back[...], preferred_element_type=F32
        )
        two = jnp.dot(
            jnp.concatenate([y_low, z_low], axis=1), back[:, :128], preferred_element_type=F32
        )
        total = (one[:, :128] + one[:, 128:] + two).reshape(block.shape)
        total = total + jnp.stack(x_derivative([along_x[i] for i in range(8)], derivative.T))
        result = group(load, half) - total
        result = jnp.concatenate([result[:, :3], (result[:, 3] - nodal)[:, None]], axis=1)
        put_group(summed, half, sum_z(result))

    def ship(r):
        for e in (0, 2):
            sum_y(e, ((0, 1), (7, 8)))
        pack_z(r)
        if r == 0:
            pl.semaphore_wait(barrier, neighbours)
        send(r, X_DIRS, 1)
        send(r, Z_ORDER)
        send(r, X_DIRS, 0)
        pack_y(r)
        send(r, XY_DIRS + Y_DIRS)
        for e in (0, 2):
            sum_y(e, ((1, 7),))

    copies[1].wait()
    copies[2].wait()
    put_fields(to_tiles([adjoint_b[f] for f in range(4)]), summed, 4)
    for half in range(2):
        put_group(summed, half, sum_z(group(summed, half)))
    sum_y(1)
    ship(0)

    copies[3].wait()
    copies[4].wait()
    copies[5].wait()
    copies[6].wait()
    tiles = to_tiles([displace_b[0], displace_b[1], displace_b[2], damage_b[...], history_b[...]])
    put_fields(tiles, value, 3)
    put_single(tiles[12:16], 0)
    put_single(tiles[16:20], 1)
    copies[7].wait()
    frozen = 1.0 - jnp.sum(chosen * frozen_b[...].astype(F32), axis=1, keepdims=True)
    low_half = lax.broadcasted_iota(jnp.int32, (32, 128), 1) < 64
    keep[2, 0] = jnp.where(low_half, frozen[:32], frozen[32:])
    for half in range(2):
        state_terms(half)
    copies[8].wait()
    put_fields(to_tiles([load_b[f] for f in range(4)]), load, 4)
    copies[9].wait()

    def halved(condition, scalar):
        return 1.0 - 0.5 * fmask(condition) * scalar

    inv_z = halved(inner_z, 1.0) * halved(first_z & (sub > 0), 1.0) * halved(last_z & (sub < 7), 1.0)
    inv_z = inv_z * halved(first_z & (sub == 0), present[2][-1]) * halved(last_z & (sub == 7), present[2][1])

    def average(half):
        planes = []
        for ey in EY[half]:
            lower = 1.0 if ey > 0 else present[1][-1]
            upper = 1.0 if ey < 3 else present[1][1]
            planes.append(inv_z * halved(lane_j == 0, lower) * halved(lane_j == 7, upper))
        scale = jnp.concatenate(planes, axis=0)
        scales = [scale] * 8
        scales[0] = scale * (1.0 - 0.5 * present[0][-1])
        scales[7] = scale * (1.0 - 0.5 * present[0][1])
        block = group(value, half) * jnp.stack(scales)[:, None]
        put_group(kept, half, block)
        return block

    def relax(half):
        return group(kept, half) + relaxation * group(value, half)

    for r, ready in ((0, average), (1, relax)):
        finish(r)
        faces = receive_early(r)
        apply_transposed(1, ready(1))
        sum_y(1)
        receive_late(r, faces)
        apply_transposed(0, ready(0))
        ship(r + 1)

    finish(2)
    receive_late(2, receive_early(2))
    twice = jnp.concatenate([unpick, unpick], axis=1)
    for f in range(4):
        sides = []
        for a in range(4):
            pair = []
            for i in (2 * a, 2 * a + 1):
                halves = [value[i, 64 * half + 16 * f : 64 * half + 16 * f + 16, :] for half in range(2)]
                pair.append(jnp.concatenate(halves, axis=0))
            sides.append(jnp.concatenate(pair, axis=1))
        sides = jnp.stack(sides)
        high, low = split(sides.reshape(128, 256))
        both = jnp.concatenate([high, low], axis=0)
        moved = jnp.dot(both, swap[...], preferred_element_type=F32).astype(BF16)
        for a in range(4):
            parts = []
            for n in (a * 32, 128 + a * 32):
                parts += [moved[n : n + 32, :128], moved[n : n + 32, 128:]]
            stacked = jnp.concatenate(parts, axis=0)
            out_ref[f, :, a * 128 : a * 128 + 128] = jnp.dot(
                twice, stacked, preferred_element_type=F32
            )


def shards(adjoint, load, displace, damage, history, frozen, order):
    forward, back, swap = (jnp.asarray(c) for c in constants())
    hbm = pl.BlockSpec(memory_space=pltpu.HBM)
    return pl.pallas_call(
        kernel,
        out_shape=pltpu.VMEM((4, 64, 512), F32),
        in_specs=[hbm] * 10,
        out_specs=pl.BlockSpec(memory_space=pltpu.VMEM),
        scratch_shapes=[
            pltpu.VMEM((4, 64, 512), BF16),
            pltpu.VMEM((4, 64, 512), BF16),
            pltpu.VMEM((3, 64, 512), BF16),
            pltpu.VMEM((64, 512), BF16),
            pltpu.VMEM((64, 512), BF16),
            pltpu.VMEM((1, 64), jnp.int32),
            pltpu.VMEM((1, 64), jnp.int32),
            pltpu.VMEM((384, 256), BF16),
            pltpu.VMEM((256, 256), BF16),
            pltpu.VMEM((256, 256), BF16),
            pltpu.VMEM((8, 128, 128), F32),
            pltpu.VMEM((8, 128, 128), F32),
            pltpu.VMEM((8, 128, 128), F32),
            pltpu.VMEM((8, 128, 128), F32),
            pltpu.VMEM((8, 8, 32, 128), F32),
            pltpu.VMEM((3, 8, 32, 128), F32),
            pltpu.VMEM((3, 2, 4, 8, 128), F32),
            pltpu.VMEM((3, 2, 8, 128), F32),
            pltpu.VMEM((3, 2, 128, 128), F32),
            pltpu.VMEM((3, 2, 4, 8, 128), F32),
            pltpu.VMEM((3, 4, 8, 128), F32),
            pltpu.VMEM((3, 18, 8, 128), F32),
            pltpu.SemaphoreType.DMA((10,)),
            pltpu.SemaphoreType.DMA((3, 28)),
            pltpu.SemaphoreType.DMA((3, 28)),
        ],
        compiler_params=pltpu.CompilerParams(
            collective_id=0, has_side_effects=True, vmem_limit_bytes=56 * 1024 * 1024
        ),
    )(adjoint, load, displace, damage, history, frozen.reshape(1, 64), order, forward, back, swap)


def solution(mesh):
    in_specs = (
        P(None, ("gx", "gy", "gz"), None),
        P(None, ("gx", "gy", "gz"), None),
        P(None, ("gx", "gy", "gz"), None),
        P(("gx", "gy", "gz"), None),
        P(("gx", "gy", "gz"), None),
        P(("gx", "gy", "gz")),
        P(("gx", "gy", "gz"), None),
    )
    out_specs = P(None, ("gx", "gy", "gz"), None)
    return jax.shard_map(shards, mesh=mesh, in_specs=in_specs, out_specs=out_specs, check_vma=False)
```

```python
import jax
import jax.numpy as jnp
import ml_dtypes
import numpy as np
from jax import lax
from jax.experimental import pallas as pl
from jax.experimental.pallas import tpu as pltpu
from jax.sharding import PartitionSpec as P

F32 = jnp.float32
BF16 = jnp.bfloat16
MESH = pl.DeviceIdType.MESH

lame_lambda = 0.15
lame_mu = 0.1
gc_length = 0.3
gc_inverse = 40.0
residual_stiff = 0.001
relaxation = 0.5
gll_points = (
    -1.0,
    -0.8717401485096066,
    -0.5917001814331423,
    -0.2092992179024789,
    0.2092992179024789,
    0.5917001814331423,
    0.8717401485096066,
    1.0,
)

EY = ((3, 0), (1, 2))
START = {ey: 64 * half + 8 * tile for half in range(2) for tile, ey in enumerate(EY[half])}

DIRS = [
    (dx, dy, dz)
    for dx in (-1, 0, 1)
    for dy in (-1, 0, 1)
    for dz in (-1, 0, 1)
    if (dx, dy, dz) != (0, 0, 0)
]
X_DIRS = [d for d in DIRS if d[1] == 0 and d[2] == 0]
Y_DIRS = [d for d in DIRS if d[0] == 0 and d[1] != 0 and d[2] == 0]
XY_DIRS = [d for d in DIRS if d[0] != 0 and d[1] != 0 and d[2] == 0]
Z_DIRS = [d for d in DIRS if d[2] != 0]
Z_LATE = [d for d in Z_DIRS if d[1] != 0]
Z_EARLY = [d for d in Z_DIRS if d[1] == 0]
Z_ORDER = sorted(Z_DIRS, key=lambda d: -abs(d[0]) - abs(d[1]))
GROUPS = (X_DIRS, X_DIRS, Y_DIRS, XY_DIRS, Z_EARLY, Z_LATE)


def legendre_at(points, degree):
    values = []
    for point in points:
        previous = 1.0
        current = point
        for level in range(1, degree):
            following = ((2 * level + 1) * point * current - level * previous) / (level + 1)
            previous = current
            current = following
        values.append(current)
    return values


def gll_tables():
    degree = 7
    points = list(gll_points)
    legendre_vals = legendre_at(points, degree)
    weights = [2.0 / (degree * (degree + 1) * entry * entry) for entry in legendre_vals]
    derivative = []
    for row_index in range(degree + 1):
        row_vals = []
        for col_index in range(degree + 1):
            if row_index != col_index:
                row_vals.append(
                    legendre_vals[row_index]
                    / (legendre_vals[col_index] * (points[row_index] - points[col_index]))
                )
            else:
                row_vals.append(0.0)
        derivative.append(row_vals)
    derivative[0][0] = -degree * (degree + 1) / 4.0
    derivative[degree][degree] = degree * (degree + 1) / 4.0
    return (np.array(weights), np.array(derivative))


def split_np(matrix):
    high = matrix.astype(np.float32).astype(ml_dtypes.bfloat16)
    low = (matrix - high.astype(np.float64)).astype(np.float32).astype(ml_dtypes.bfloat16)
    return high, low


def constants():
    _, derivative = gll_tables()
    eye = np.eye
    forward_y = np.kron(eye(2), np.kron(derivative.T, eye(8)))
    forward_z = np.kron(eye(16), derivative.T)
    back_y = np.kron(eye(2), np.kron(derivative, eye(8)))
    back_z = np.kron(eye(16), derivative)
    f_high, f_low = split_np(np.concatenate([forward_y, forward_z], axis=1))
    forward = np.concatenate([f_high, f_high, f_low], axis=0)
    b_high, b_low = split_np(np.concatenate([back_y, back_z], axis=0))
    back = np.concatenate([b_high, b_high, b_low], axis=0)
    swap = np.zeros((2, 2, 64, 2, 2, 64))
    for h in range(2):
        for odd in range(2):
            swap[h, odd, :, odd, h, :] = eye(64)
    swap = swap.reshape(256, 256).astype(ml_dtypes.bfloat16)
    return forward, back, swap


def lane_roll(value, shift):
    shift = shift % 128
    if shift == 0:
        return value
    flat = value.reshape(-1, 128)
    return pltpu.roll(flat, shift, 1).reshape(value.shape)


def lane_swap(value, mask):
    flat = value.reshape(-1, 128)
    index = jnp.bitwise_xor(lax.broadcasted_iota(jnp.int32, flat.shape, 1), mask)
    return jnp.take_along_axis(flat, index, axis=1).reshape(value.shape)


def split(value):
    high = value.astype(BF16)
    low = (value - high.astype(F32)).astype(BF16)
    return high, low


def x_derivative(tiles, matrix):
    even_part = (matrix + matrix[:, ::-1]) / 2
    odd_part = (matrix - matrix[:, ::-1]) / 2
    even = [tiles[n] + tiles[7 - n] for n in range(4)]
    odd = [tiles[n] - tiles[7 - n] for n in range(4)]
    out = [None] * 8
    for n in range(4):
        first = float(even_part[n, 0]) * even[0]
        second = float(odd_part[n, 0]) * odd[0]
        for m in range(1, 4):
            first = first + float(even_part[n, m]) * even[m]
            second = second + float(odd_part[n, m]) * odd[m]
        out[n] = second + first
        out[7 - n] = second - first
    return out


def kernel(
    adjoint_h,
    load_h,
    displace_h,
    damage_h,
    history_h,
    frozen_h,
    order_h,
    forward_h,
    back_h,
    swap_h,
    out_ref,
    adjoint_b,
    load_b,
    displace_b,
    damage_b,
    history_b,
    frozen_b,
    order_b,
    forward,
    back,
    swap,
    value,
    kept,
    load,
    summed,
    state,
    keep,
    ys,
    zs,
    xr,
    yr,
    xyr,
    zer,
    zlr,
    zero,
    in_sem,
    send_sem,
    recv_sem,
):
    weights, derivative = gll_tables()
    px, py, pz = (lax.axis_index("gx"), lax.axis_index("gy"), lax.axis_index("gz"))
    sizes = (lax.axis_size("gx"), lax.axis_size("gy"), lax.axis_size("gz"))

    pairs = (
        (order_h, order_b),
        (adjoint_h, adjoint_b),
        (swap_h, swap),
        (displace_h, displace_b),
        (forward_h, forward),
        (damage_h, damage_b),
        (history_h, history_b),
        (frozen_h, frozen_b),
        (load_h, load_b),
        (back_h, back),
    )
    copies = [pltpu.make_async_copy(src, dst, in_sem.at[n]) for n, (src, dst) in enumerate(pairs)]
    for copy in copies[:3]:
        copy.start()

    along = [
        {
            -1: lax.rem(p + n - 1, n),
            0: p,
            1: lax.rem(p + 1, n),
        }
        for p, n in zip((px, py, pz), sizes)
    ]

    def target(d):
        return tuple(along[axis][d[axis]] for axis in range(3))

    has = [{-1: p > 0, 1: p < n - 1} for p, n in zip((px, py, pz), sizes)]
    present = [{s: side[s].astype(F32) for s in (-1, 1)} for side in has]

    def there(d):
        sides = [has[axis][d[axis]] for axis in range(3) if d[axis] != 0]
        found = sides[0]
        for side in sides[1:]:
            found = jnp.logical_and(found, side)
        return found

    to_there = {d: there(d) for d in DIRS}

    def from_there(d):
        return to_there[(-d[0], -d[1], -d[2])]

    barrier = pltpu.get_barrier_semaphore()
    for d in DIRS:

        @pl.when(to_there[d])
        def _(d=d):
            pl.semaphore_signal(barrier, inc=1, device_id=target(d), device_id_type=MESH)

    around = [1 + side[-1].astype(jnp.int32) + side[1].astype(jnp.int32) for side in has]
    neighbours = around[0] * around[1] * around[2] - 1
    for copy in copies[3:]:
        copy.start()

    lane = lax.broadcasted_iota(jnp.int32, (8, 128), 1)
    sub = lax.broadcasted_iota(jnp.int32, (8, 128), 0)
    lane_k = lane % 8
    lane_j = (lane // 8) % 8
    lane_h = lane // 64

    def fmask(condition):
        return jnp.where(condition, 1.0, 0.0).astype(F32)

    j_end = {-1: fmask(lane_j == 0), 1: fmask(lane_j == 7)}
    h_end = {-1: fmask(lane_h == 0), 1: fmask(lane_h == 1)}
    first_z = (lane_h == 0) & (lane_k == 0)
    last_z = (lane_h == 1) & (lane_k == 7)
    z_end = {-1: fmask(first_z), 1: fmask(last_z)}
    inner_z = ((lane_h == 0) & (lane_k == 7)) | ((lane_h == 1) & (lane_k == 0))
    z_here = fmask(inner_z | (last_z & (sub < 7)))
    z_next = fmask(first_z & (sub > 0))

    copies[0].wait()
    row_id = lax.broadcasted_iota(jnp.int32, (64, 64), 0)
    tile_id = (row_id // 8) % 4
    row_ey = (tile_id + 3) % 4
    place = row_ey * 16 + 2 * (row_id % 8) + row_id // 32
    chosen = fmask(place == order_b[...])
    pick = chosen.astype(BF16)

    def to_tiles(fields):
        sides = []
        for stored in fields:
            rows = jnp.dot(pick, stored, preferred_element_type=F32).astype(BF16)
            for n in range(0, 512, 128):
                sides.append(jnp.concatenate([rows[:32, n : n + 128], rows[32:, n : n + 128]], axis=1))
        tiles = jnp.dot(
            jnp.concatenate(sides, axis=0), swap[...], preferred_element_type=F32
        )
        return tiles.reshape(len(fields) * 4, 32, 256)

    def put_fields(tiles, ref, fields):
        for f in range(fields):
            for a in range(4):
                for half in range(2):
                    rows = slice(half * 64 + f * 16, half * 64 + f * 16 + 16)
                    both = tiles[4 * f + a, half * 16 : half * 16 + 16, :]
                    ref[2 * a, rows, :] = both[:, :128]
                    ref[2 * a + 1, rows, :] = both[:, 128:]

    def put_single(tiles, n):
        for a in range(4):
            keep[n, 2 * a] = tiles[a, :, :128]
            keep[n, 2 * a + 1] = tiles[a, :, 128:]

    def group(ref, half):
        return ref[:, half * 64 : half * 64 + 64, :].reshape(8, 4, 16, 128)

    def put_group(ref, half, block):
        ref[:, half * 64 : half * 64 + 64, :] = block.reshape(8, 64, 128)

    def sum_z(half, first, last):
        rows = slice(64 * half, 64 * half + 64)
        flat = summed[first:last, rows, :].reshape(-1, 8, 128)
        taken = lane_swap(jnp.where(first_z, pltpu.roll(flat, 7, 1), flat), 71)
        total = flat + z_here * taken + z_next * pltpu.roll(taken, 1, 1)
        summed[first:last, rows, :] = total.reshape(last - first, 64, 128)

    def sum_y(e, spans=((0, 8),)):
        for first, last in spans:
            for f in range(4):
                lower = slice(START[e] + f * 16, START[e] + f * 16 + 8)
                upper = slice(START[e + 1] + f * 16, START[e + 1] + f * 16 + 8)
                here, beyond = summed[first:last, lower, :], summed[first:last, upper, :]
                taken = lane_swap(jnp.where(lane_j == 7, here, beyond), 56)
                summed[first:last, lower, :] = here + j_end[1] * taken
                summed[first:last, upper, :] = beyond + j_end[-1] * taken

    def mask_of(half, tile, j):
        return fmask((lane_k % 2 == half) & (sub % 2 == tile) & (lane_j == j))

    inner_i = fmask(((lane_h == 1) | (lane_k > 1)) & ((lane_h == 0) | (lane_k < 6)))
    packed_y = []
    for ey in range(3):
        half, tile = (START[ey] // 64, (START[ey] // 8) % 2)
        half_up, tile_up = (START[ey + 1] // 64, (START[ey + 1] // 8) % 2)
        packed_y.append(
            (
                (inner_i * mask_of(half, tile, 7), tile - tile_up, 56 + half - half_up),
                (inner_i * mask_of(half_up, tile_up, 0), tile_up - tile, half_up - half - 56),
            )
        )

    def packed_sum_y(face, pairs):
        total = face
        for e in pairs:
            for wanted, tiles, lanes in packed_y[e]:
                total = total + wanted * lane_roll(pltpu.roll(face, tiles % 8, 0), lanes)
        return total

    def pack_z(r, pairs):
        for n, (row, h, k) in enumerate(((0, 0, 0), (7, 1, 7))):
            packed = jnp.zeros((8, 128), F32)
            for slot in range(16):
                i, half = slot // 2, slot % 2
                piece = summed[i, pl.ds(half * 64 + row, 8, stride=8), :]
                moved = lane_roll(piece, (slot // 8 - h) * 64 + slot % 8 - k)
                packed = jnp.where((lane_h == slot // 8) & (lane_k == slot % 8), moved, packed)
            zs[r, n] = packed_sum_y(packed, pairs)

    def pack_y(r):
        for n, (ey, j) in enumerate(((0, 0), (3, 7))):
            for g in range(4):
                packed = jnp.zeros((8, 128), F32)
                for slot in range(8):
                    row = (slot // 2) * 16 + START[ey]
                    piece = summed[2 * g + slot % 2, row : row + 8, :]
                    packed = jnp.where(lane_j == slot, lane_roll(piece, 8 * (slot - j)), packed)
                ys[r, n, 8 * g : 8 * g + 8] = packed

    def slot_of(r, g, d):
        n = GROUPS[g].index(d)
        return (xr.at[r, 0], xr.at[r, 1], yr.at[r], xyr.at[r], zer.at[r], zlr.at[r])[g].at[n]

    def message(r, g, d):
        dx, dy, dz = d
        if g < 2:
            src = summed.at[7 if dx > 0 else 0, pl.ds(64 * g, 64)]
        elif g == 2:
            src = ys.at[r, (dy + 1) // 2]
        elif g == 3:
            src = ys.at[r, (dy + 1) // 2, pl.ds(24 if dx > 0 else 0, 8)]
        else:
            src = zs.at[r, (dz + 1) // 2]
        n = sum(len(dirs) for dirs in GROUPS[:g]) + GROUPS[g].index(d)
        return pltpu.make_async_remote_copy(
            src_ref=src,
            dst_ref=slot_of(r, g, d),
            send_sem=send_sem.at[r, n],
            recv_sem=recv_sem.at[r, g],
            device_id=target(d),
            device_id_type=MESH,
        )

    def send(r, g, dirs=None):
        for d in dirs or GROUPS[g]:
            pl.when(to_there[d])(message(r, g, d).start)

    def fill_absent(r):
        for g in range(6):
            source = zero if g < 2 else zero.at[pl.ds(0, 32)] if g == 2 else zero.at[pl.ds(0, 8)]
            for d in GROUPS[g]:
                slot = slot_of(r, g, d)
                copy = pltpu.make_async_copy(source, slot, recv_sem.at[r, g])
                pl.when(jnp.logical_not(from_there(d)))(copy.start)

    def finish(r):
        for g in range(6):
            for d in GROUPS[g]:
                pl.when(to_there[d])(message(r, g, d).wait_send)

    def arrive(r, g):
        slots = (xr.at[r, 0], xr.at[r, 1], yr.at[r], xyr.at[r], zer.at[r], zlr.at[r])[g]
        pltpu.make_async_copy(slots, slots, recv_sem.at[r, g]).wait()

    def z_faces(slots, dirs):
        faces = []
        for dz in (-1, 1):
            face = None
            for n, d in enumerate(dirs):
                if d[2] != dz:
                    continue
                part = slots[n]
                dx, dy, _ = d
                wanted = None
                if dx != 0:
                    near = (lane_k < 2) if dx > 0 else (lane_k >= 6)
                    wanted = h_end[-dx] * fmask(near)
                if dy != 0:
                    mine = mask_of(0, 1 if dy > 0 else 0, 0 if dy > 0 else 7)
                    wanted = mine if wanted is None else wanted * mine
                    part = pltpu.roll(part, dy % 8, 0)
                part = lane_roll(part, -70 * dx - 56 * dy)
                if wanted is not None:
                    part = part * wanted
                face = part if face is None else face + part
            faces.append(face)
        return faces

    def add_z(faces, half):
        for dz, face in zip((-1, 1), faces):
            row, h, k = (0, 0, 0) if dz > 0 else (7, 1, 7)
            for i in range(8):
                slot = 2 * i + half
                where = pl.ds(half * 64 + row, 8, stride=8)
                moved = lane_roll(face, (h - slot // 8) * 64 + k - slot % 8)
                value[i, where, :] = value[i, where, :] + moved * z_end[-dz]

    def take_x(r, half):
        rows = slice(64 * half, 64 * half + 64)
        arrive(r, half)
        for n, d in enumerate(X_DIRS):
            i = 0 if d[0] > 0 else 7
            value[i, rows, :] = value[i, rows, :] + xr[r, half, n]

    def receive_early(r):
        arrive(r, 4)
        faces = z_faces(zer.at[r], Z_EARLY)
        take_x(r, 1)
        add_z(faces, 1)
        return faces

    def receive_late(r, faces):
        take_x(r, 0)
        arrive(r, 2)
        arrive(r, 3)
        for n, d in enumerate(Y_DIRS):
            dy = d[1]
            sides = [yr[r, n, 8 * g : 8 * g + 8] for g in range(4)]
            for dx in (-1, 1):
                edge = lane_roll(xyr[r, XY_DIRS.index((dx, dy, 0))], -8 * dx)
                g = 0 if dx > 0 else 3
                sides[g] = sides[g] + edge * fmask(lane_j % 2 == (0 if dx > 0 else 1))
            ey, j = (0, 0) if dy > 0 else (3, 7)
            for i in range(8):
                for f in range(4):
                    row = f * 16 + START[ey]
                    moved = lane_roll(sides[i // 2], 8 * (j - f * 2 - i % 2))
                    value[i, row : row + 8, :] = value[i, row : row + 8, :] + moved * j_end[-dy]
        arrive(r, 5)
        late = z_faces(zlr.at[r], Z_LATE)
        add_z([face + more for face, more in zip(faces, late)], 0)

    def brick():
        line_j = jnp.zeros((8, 128), F32)
        line_k = jnp.zeros((8, 128), F32)
        for n in range(8):
            line_j = jnp.where(lane_j == n, float(weights[n]), line_j)
            line_k = jnp.where(lane_k == n, float(weights[n]), line_k)
        plane = (line_j * line_k)[:1]
        return jnp.stack([plane * float(weights[n]) for n in range(8)])

    def gradients(block, exact):
        if exact:
            high = block.reshape(-1, 128).astype(BF16)
            left, table = jnp.concatenate([high, high], axis=1), forward[128:384, :]
        else:
            high, low = split(block.reshape(-1, 128))
            left, table = jnp.concatenate([high, low, high], axis=1), forward[...]
        yz = jnp.dot(left, table, preferred_element_type=F32)
        gx = jnp.stack(x_derivative([block[i] for i in range(8)], derivative))
        return gx, yz[:, :128].reshape(block.shape), yz[:, 128:].reshape(block.shape)

    def state_terms(half):
        rows = slice(16 * half, 16 * half + 16)
        moved = group(kept, half)[:, :3]
        gx, gy, gz = gradients(moved, True)
        shear = [gy[:, 0] + gx[:, 1], gz[:, 0] + gx[:, 2], gz[:, 1] + gy[:, 2]]
        normal = [gx[:, 0], gy[:, 1], gz[:, 2]]
        trace_sum = normal[0] + normal[1] + normal[2]
        stress = [lame_lambda * trace_sum + 2.0 * lame_mu * n for n in normal]
        stress += [lame_mu * s for s in shear]
        energy = stress[0] * normal[0] + stress[1] * normal[1] + stress[2] * normal[2]
        energy = 0.5 * (energy + stress[3] * shear[0] + stress[4] * shear[1] + stress[5] * shear[2])
        loading = keep[2, 0, rows, :][None]
        driving = (1.0 - loading) * keep[1, :, rows, :] + loading * energy
        intact = 1.0 - keep[0, :, rows, :]
        mass = brick()
        slope = -2.0 * intact * mass
        for n in range(6):
            state[n, :, rows, :] = slope * stress[n]
        state[6, :, rows, :] = lame_mu * mass * (intact * intact + residual_stiff)
        state[7, :, rows, :] = mass * (gc_inverse + 2.0 * driving)

    def apply_transposed(half, block):
        rows = slice(16 * half, 16 * half + 16)
        gx, gy, gz = gradients(block, False)
        scaled = [state[n, :, rows, :] for n in range(6)]
        stiff = state[6, :, rows, :]
        vd = block[:, 3]
        coupled = keep[2, 0, rows, :][None] * vd
        shear = [gy[:, 0] + gx[:, 1], gz[:, 0] + gx[:, 2], gz[:, 1] + gy[:, 2]]
        normal = [gx[:, 0], gy[:, 1], gz[:, 2]]
        trace_sum = 1.5 * (normal[0] + normal[1] + normal[2])
        tensor = [stiff * (trace_sum + 2.0 * normal[n]) + scaled[n] * coupled for n in range(3)]
        tensor += [stiff * shear[n] + scaled[n + 3] * coupled for n in range(3)]
        nodal = state[7, :, rows, :] * vd
        for n in range(3):
            nodal = nodal + scaled[n] * normal[n] + scaled[n + 3] * shear[n]
        flux = gc_length * brick()
        along_x = jnp.stack([tensor[0], tensor[3], tensor[4], flux * gx[:, 3]], axis=1)
        along_y = jnp.stack([tensor[3], tensor[1], tensor[5], flux * gy[:, 3]], axis=1)
        along_z = jnp.stack([tensor[4], tensor[5], tensor[2], flux * gz[:, 3]], axis=1)
        y_high, y_low = split(along_y.reshape(-1, 128))
        z_high, z_low = split(along_z.reshape(-1, 128))
        total = jnp.dot(
            jnp.concatenate([y_high, z_high, y_low, z_low, y_high, z_high], axis=1),
            back[...],
            preferred_element_type=F32,
        ).reshape(block.shape)
        total = total + jnp.stack(x_derivative([along_x[i] for i in range(8)], derivative.T))
        result = group(load, half) - total
        result = jnp.concatenate([result[:, :3], (result[:, 3] - nodal)[:, None]], axis=1)
        put_group(summed, half, result)

    def ship(r):
        halves, pairs = ((0, 1), (0, 1, 2)) if r == 0 else ((0,), (0, 2))
        for half in halves:
            sum_z(half, 0, 1)
            sum_z(half, 7, 8)
        for e in pairs:
            sum_y(e, ((0, 1), (7, 8)))
        pack_z(r, pairs)
        if r == 0:
            pl.semaphore_wait(barrier, neighbours)
        send(r, 1)
        for d in Z_ORDER:
            send(r, 4 if d in Z_EARLY else 5, [d])
        send(r, 0)
        for half in halves:
            sum_z(half, 1, 7)
        pack_y(r)
        send(r, 3)
        send(r, 2)
        for e in pairs:
            sum_y(e, ((1, 7),))
        value[...] = summed[...]

    copies[1].wait()
    copies[2].wait()
    put_fields(to_tiles([adjoint_b[f] for f in range(4)]), summed, 4)
    ship(0)

    zero[...] = jnp.zeros((64, 128), F32)
    fill_absent(0)

    copies[3].wait()
    copies[4].wait()
    copies[5].wait()
    copies[6].wait()
    tiles = to_tiles([displace_b[0], displace_b[1], displace_b[2], damage_b[...], history_b[...]])
    put_fields(tiles, kept, 3)
    put_single(tiles[12:16], 0)
    put_single(tiles[16:20], 1)
    copies[7].wait()
    frozen = 1.0 - jnp.sum(chosen * frozen_b[...].astype(F32), axis=1, keepdims=True)
    low_half = lax.broadcasted_iota(jnp.int32, (32, 128), 1) < 64
    keep[2, 0] = jnp.where(low_half, frozen[:32], frozen[32:])
    for half in range(2):
        state_terms(half)
    copies[8].wait()
    put_fields(to_tiles([load_b[f] for f in range(4)]), load, 4)
    copies[9].wait()

    def halved(condition, scalar):
        return 1.0 - 0.5 * fmask(condition) * scalar

    inv_z = halved(inner_z, 1.0) * halved(first_z & (sub > 0), 1.0) * halved(last_z & (sub < 7), 1.0)
    inv_z = inv_z * halved(first_z & (sub == 0), present[2][-1]) * halved(last_z & (sub == 7), present[2][1])

    def average(half):
        planes = []
        for ey in EY[half]:
            lower = 1.0 if ey > 0 else present[1][-1]
            upper = 1.0 if ey < 3 else present[1][1]
            planes.append(inv_z * halved(lane_j == 0, lower) * halved(lane_j == 7, upper))
        scale = jnp.concatenate(planes, axis=0)
        scales = [scale] * 8
        scales[0] = scale * (1.0 - 0.5 * present[0][-1])
        scales[7] = scale * (1.0 - 0.5 * present[0][1])
        block = group(value, half) * jnp.stack(scales)[:, None]
        put_group(kept, half, block)
        return block

    def relax(half):
        return group(kept, half) + relaxation * group(value, half)

    fill_absent(1)
    fill_absent(2)

    for r, ready in ((0, average), (1, relax)):
        finish(r)
        faces = receive_early(r)
        apply_transposed(1, ready(1))
        sum_z(1, 0, 8)
        sum_y(1)
        receive_late(r, faces)
        apply_transposed(0, ready(0))
        ship(r + 1)

    def emit(half):
        block = value[:, 64 * half : 64 * half + 64, :].reshape(4, 2, 4, 16, 128)
        sides = jnp.concatenate([block[:, 0], block[:, 1]], axis=3).reshape(256, 256)
        high, low = split(sides)
        moved = jnp.dot(
            jnp.concatenate([high, low], axis=0), swap[...], preferred_element_type=F32
        ).astype(BF16)
        rows = jnp.concatenate([chosen[16 * half : 16 * half + 16], chosen[32 + 16 * half : 48 + 16 * half]], axis=0)
        unpick = jnp.concatenate([rows, rows], axis=0).T.astype(BF16)
        for f in range(4):
            columns = []
            for a in range(4):
                parts = []
                for n in (a * 64 + f * 16, 256 + a * 64 + f * 16):
                    parts += [moved[n : n + 16, :128], moved[n : n + 16, 128:]]
                columns.append(jnp.concatenate(parts, axis=0))
            stacked = jnp.concatenate(columns, axis=1)
            out = jnp.dot(unpick, stacked, preferred_element_type=F32)
            out_ref[f] = out if half == 1 else out_ref[f] + out

    finish(2)
    faces = receive_early(2)
    emit(1)
    receive_late(2, faces)
    emit(0)


def shards(adjoint, load, displace, damage, history, frozen, order):
    forward, back, swap = (jnp.asarray(c) for c in constants())
    hbm = pl.BlockSpec(memory_space=pltpu.HBM)
    return pl.pallas_call(
        kernel,
        out_shape=pltpu.VMEM((4, 64, 512), F32),
        in_specs=[hbm] * 10,
        out_specs=pl.BlockSpec(memory_space=pltpu.VMEM),
        scratch_shapes=[
            pltpu.VMEM((4, 64, 512), BF16),
            pltpu.VMEM((4, 64, 512), BF16),
            pltpu.VMEM((3, 64, 512), BF16),
            pltpu.VMEM((64, 512), BF16),
            pltpu.VMEM((64, 512), BF16),
            pltpu.VMEM((1, 64), jnp.int32),
            pltpu.VMEM((1, 64), jnp.int32),
            pltpu.VMEM((384, 256), BF16),
            pltpu.VMEM((768, 128), BF16),
            pltpu.VMEM((256, 256), BF16),
            pltpu.VMEM((8, 128, 128), F32),
            pltpu.VMEM((8, 128, 128), F32),
            pltpu.VMEM((8, 128, 128), F32),
            pltpu.VMEM((8, 128, 128), F32),
            pltpu.VMEM((8, 8, 32, 128), F32),
            pltpu.VMEM((3, 8, 32, 128), F32),
            pltpu.VMEM((3, 2, 32, 128), F32),
            pltpu.VMEM((3, 2, 8, 128), F32),
            pltpu.VMEM((3, 2, 2, 64, 128), F32),
            pltpu.VMEM((3, 2, 32, 128), F32),
            pltpu.VMEM((3, 4, 8, 128), F32),
            pltpu.VMEM((3, 6, 8, 128), F32),
            pltpu.VMEM((3, 12, 8, 128), F32),
            pltpu.VMEM((64, 128), F32),
            pltpu.SemaphoreType.DMA((10,)),
            pltpu.SemaphoreType.DMA((3, 28)),
            pltpu.SemaphoreType.DMA((3, 6)),
        ],
        compiler_params=pltpu.CompilerParams(
            collective_id=0, has_side_effects=True, vmem_limit_bytes=56 * 1024 * 1024
        ),
    )(adjoint, load, displace, damage, history, frozen.reshape(1, 64), order, forward, back, swap)


def solution(mesh):
    in_specs = (
        P(None, ("gx", "gy", "gz"), None),
        P(None, ("gx", "gy", "gz"), None),
        P(None, ("gx", "gy", "gz"), None),
        P(("gx", "gy", "gz"), None),
        P(("gx", "gy", "gz"), None),
        P(("gx", "gy", "gz")),
        P(("gx", "gy", "gz"), None),
    )
    out_specs = P(None, ("gx", "gy", "gz"), None)
    return jax.shard_map(shards, mesh=mesh, in_specs=in_specs, out_specs=out_specs, check_vma=False)
```

```python
import jax
import jax.numpy as jnp
import ml_dtypes
import numpy as np
from jax import lax
from jax.experimental import pallas as pl
from jax.experimental.pallas import tpu as pltpu
from jax.sharding import PartitionSpec as P

F32 = jnp.float32
BF16 = jnp.bfloat16
MESH = pl.DeviceIdType.MESH

lame_lambda = 0.15
lame_mu = 0.1
gc_length = 0.3
gc_inverse = 40.0
residual_stiff = 0.001
relaxation = 0.5
gll_points = (
    -1.0,
    -0.8717401485096066,
    -0.5917001814331423,
    -0.2092992179024789,
    0.2092992179024789,
    0.5917001814331423,
    0.8717401485096066,
    1.0,
)

EY = ((3, 0), (1, 2))
START = {ey: 64 * half + 8 * tile for half in range(2) for tile, ey in enumerate(EY[half])}

DIRS = [
    (dx, dy, dz)
    for dx in (-1, 0, 1)
    for dy in (-1, 0, 1)
    for dz in (-1, 0, 1)
    if (dx, dy, dz) != (0, 0, 0)
]
X_DIRS = [d for d in DIRS if d[1] == 0 and d[2] == 0]
Y_DIRS = [d for d in DIRS if d[0] == 0 and d[1] != 0 and d[2] == 0]
XY_DIRS = [d for d in DIRS if d[0] != 0 and d[1] != 0 and d[2] == 0]
Z_DIRS = [d for d in DIRS if d[2] != 0]
Z_LATE = [d for d in Z_DIRS if d[1] != 0]
Z_EARLY = [d for d in Z_DIRS if d[1] == 0]
Z_ORDER = sorted(Z_DIRS, key=lambda d: -abs(d[0]) - abs(d[1]))
GROUPS = (X_DIRS, X_DIRS, Y_DIRS, XY_DIRS, Z_EARLY, Z_LATE)


def legendre_at(points, degree):
    values = []
    for point in points:
        previous = 1.0
        current = point
        for level in range(1, degree):
            following = ((2 * level + 1) * point * current - level * previous) / (level + 1)
            previous = current
            current = following
        values.append(current)
    return values


def gll_tables():
    degree = 7
    points = list(gll_points)
    legendre_vals = legendre_at(points, degree)
    weights = [2.0 / (degree * (degree + 1) * entry * entry) for entry in legendre_vals]
    derivative = []
    for row_index in range(degree + 1):
        row_vals = []
        for col_index in range(degree + 1):
            if row_index != col_index:
                row_vals.append(
                    legendre_vals[row_index]
                    / (legendre_vals[col_index] * (points[row_index] - points[col_index]))
                )
            else:
                row_vals.append(0.0)
        derivative.append(row_vals)
    derivative[0][0] = -degree * (degree + 1) / 4.0
    derivative[degree][degree] = degree * (degree + 1) / 4.0
    return (np.array(weights), np.array(derivative))


def split_np(matrix):
    high = matrix.astype(np.float32).astype(ml_dtypes.bfloat16)
    low = (matrix - high.astype(np.float64)).astype(np.float32).astype(ml_dtypes.bfloat16)
    return high, low


def constants():
    _, derivative = gll_tables()
    eye = np.eye
    forward_y = np.kron(eye(2), np.kron(derivative.T, eye(8)))
    forward_z = np.kron(eye(16), derivative.T)
    back_y = np.kron(eye(2), np.kron(derivative, eye(8)))
    back_z = np.kron(eye(16), derivative)
    f_high, f_low = split_np(np.concatenate([forward_y, forward_z], axis=1))
    forward = np.concatenate([f_high, f_high, f_low], axis=0)
    b_high, b_low = split_np(np.concatenate([back_y, back_z], axis=0))
    back = np.concatenate([b_high, b_low], axis=1)
    swap = np.zeros((2, 2, 64, 2, 2, 64))
    for h in range(2):
        for odd in range(2):
            swap[h, odd, :, odd, h, :] = eye(64)
    swap = swap.reshape(256, 256).astype(ml_dtypes.bfloat16)
    return forward, back, swap


def lane_roll(value, shift):
    shift = shift % 128
    if shift == 0:
        return value
    flat = value.reshape(-1, 128)
    return pltpu.roll(flat, shift, 1).reshape(value.shape)


def lane_swap(value, mask):
    flat = value.reshape(-1, 128)
    index = jnp.bitwise_xor(lax.broadcasted_iota(jnp.int32, flat.shape, 1), mask)
    return jnp.take_along_axis(flat, index, axis=1).reshape(value.shape)


def split(value):
    high = value.astype(BF16)
    low = (value - high.astype(F32)).astype(BF16)
    return high, low


def x_derivative(tiles, matrix):
    even_part = (matrix + matrix[:, ::-1]) / 2
    odd_part = (matrix - matrix[:, ::-1]) / 2
    even = [tiles[n] + tiles[7 - n] for n in range(4)]
    odd = [tiles[n] - tiles[7 - n] for n in range(4)]
    out = [None] * 8
    for n in range(4):
        first = float(even_part[n, 0]) * even[0]
        second = float(odd_part[n, 0]) * odd[0]
        for m in range(1, 4):
            first = first + float(even_part[n, m]) * even[m]
            second = second + float(odd_part[n, m]) * odd[m]
        out[n] = second + first
        out[7 - n] = second - first
    return out


def kernel(
    adjoint_h,
    load_h,
    displace_h,
    damage_h,
    history_h,
    frozen_h,
    order_h,
    forward_h,
    back_h,
    swap_h,
    out_ref,
    adjoint_b,
    load_b,
    displace_b,
    damage_b,
    history_b,
    frozen_b,
    order_b,
    forward,
    back,
    swap,
    value,
    kept,
    load,
    summed,
    state,
    keep,
    ys,
    zs,
    xr,
    yr,
    xyr,
    zer,
    zlr,
    zero,
    in_sem,
    send_sem,
    recv_sem,
):
    weights, derivative = gll_tables()
    px, py, pz = (lax.axis_index("gx"), lax.axis_index("gy"), lax.axis_index("gz"))
    sizes = (lax.axis_size("gx"), lax.axis_size("gy"), lax.axis_size("gz"))

    pairs = (
        (order_h, order_b),
        (adjoint_h, adjoint_b),
        (swap_h, swap),
        (displace_h, displace_b),
        (forward_h, forward),
        (damage_h, damage_b),
        (history_h, history_b),
        (frozen_h, frozen_b),
        (load_h, load_b),
        (back_h, back),
    )
    copies = [pltpu.make_async_copy(src, dst, in_sem.at[n]) for n, (src, dst) in enumerate(pairs)]
    for copy in copies[:3]:
        copy.start()

    along = [
        {
            -1: lax.rem(p + n - 1, n),
            0: p,
            1: lax.rem(p + 1, n),
        }
        for p, n in zip((px, py, pz), sizes)
    ]

    def target(d):
        return tuple(along[axis][d[axis]] for axis in range(3))

    has = [{-1: p > 0, 1: p < n - 1} for p, n in zip((px, py, pz), sizes)]
    present = [{s: side[s].astype(F32) for s in (-1, 1)} for side in has]

    def there(d):
        sides = [has[axis][d[axis]] for axis in range(3) if d[axis] != 0]
        found = sides[0]
        for side in sides[1:]:
            found = jnp.logical_and(found, side)
        return found

    to_there = {d: there(d) for d in DIRS}

    def from_there(d):
        return to_there[(-d[0], -d[1], -d[2])]

    barrier = pltpu.get_barrier_semaphore()
    for d in sorted(DIRS, key=lambda d: -abs(d[0]) - abs(d[1]) - abs(d[2])):

        @pl.when(to_there[d])
        def _(d=d):
            pl.semaphore_signal(barrier, inc=1, device_id=target(d), device_id_type=MESH)

    around = [1 + side[-1].astype(jnp.int32) + side[1].astype(jnp.int32) for side in has]
    neighbours = around[0] * around[1] * around[2] - 1
    for copy in copies[3:]:
        copy.start()

    lane = lax.broadcasted_iota(jnp.int32, (8, 128), 1)
    sub = lax.broadcasted_iota(jnp.int32, (8, 128), 0)
    lane_k = lane % 8
    lane_j = (lane // 8) % 8
    lane_h = lane // 64

    def fmask(condition):
        return jnp.where(condition, 1.0, 0.0).astype(F32)

    j_end = {-1: fmask(lane_j == 0), 1: fmask(lane_j == 7)}
    h_end = {-1: fmask(lane_h == 0), 1: fmask(lane_h == 1)}
    first_z = (lane_h == 0) & (lane_k == 0)
    last_z = (lane_h == 1) & (lane_k == 7)
    z_end = {-1: fmask(first_z), 1: fmask(last_z)}
    inner_z = ((lane_h == 0) & (lane_k == 7)) | ((lane_h == 1) & (lane_k == 0))
    z_here = fmask(inner_z | (last_z & (sub < 7)))
    z_next = fmask(first_z & (sub > 0))

    copies[0].wait()
    row_id = lax.broadcasted_iota(jnp.int32, (64, 64), 0)
    tile_id = (row_id // 8) % 4
    row_ey = (tile_id + 3) % 4
    place = row_ey * 16 + 2 * (row_id % 8) + row_id // 32
    chosen = fmask(place == order_b[...])
    pick = chosen.astype(BF16)

    def to_tiles(fields):
        sides = []
        for stored in fields:
            rows = jnp.dot(pick, stored, preferred_element_type=F32).astype(BF16)
            for n in range(0, 512, 128):
                sides.append(jnp.concatenate([rows[:32, n : n + 128], rows[32:, n : n + 128]], axis=1))
        tiles = jnp.dot(
            jnp.concatenate(sides, axis=0), swap[...], preferred_element_type=F32
        )
        return tiles.reshape(len(fields) * 4, 32, 256)

    def put_fields(tiles, ref, fields):
        for f in range(fields):
            for a in range(4):
                for half in range(2):
                    rows = slice(half * 64 + f * 16, half * 64 + f * 16 + 16)
                    both = tiles[4 * f + a, half * 16 : half * 16 + 16, :]
                    ref[2 * a, rows, :] = both[:, :128]
                    ref[2 * a + 1, rows, :] = both[:, 128:]

    def put_single(tiles, n):
        for a in range(4):
            keep[n, 2 * a] = tiles[a, :, :128]
            keep[n, 2 * a + 1] = tiles[a, :, 128:]

    def group(ref, half):
        return ref[:, half * 64 : half * 64 + 64, :].reshape(8, 4, 16, 128)

    def put_group(ref, half, block):
        ref[:, half * 64 : half * 64 + 64, :] = block.reshape(8, 64, 128)

    def sum_z(half, first, last):
        rows = slice(64 * half, 64 * half + 64)
        flat = summed[first:last, rows, :].reshape(-1, 8, 128)
        taken = lane_swap(jnp.where(first_z, pltpu.roll(flat, 7, 1), flat), 71)
        total = flat + z_here * taken + z_next * pltpu.roll(taken, 1, 1)
        summed[first:last, rows, :] = total.reshape(last - first, 64, 128)

    def sum_y(e, spans):
        for first, last in spans:
            for f in range(4):
                lower = slice(START[e] + f * 16, START[e] + f * 16 + 8)
                upper = slice(START[e + 1] + f * 16, START[e + 1] + f * 16 + 8)
                here, beyond = summed[first:last, lower, :], summed[first:last, upper, :]
                taken = lane_swap(jnp.where(lane_j == 7, here, beyond), 56)
                summed[first:last, lower, :] = here + j_end[1] * taken
                summed[first:last, upper, :] = beyond + j_end[-1] * taken

    def mask_of(half, tile, j):
        return fmask((lane_k % 2 == half) & (sub % 2 == tile) & (lane_j == j))

    inner_i = fmask(((lane_h == 1) | (lane_k > 1)) & ((lane_h == 0) | (lane_k < 6)))
    packed_y = []
    for ey in range(3):
        half, tile = (START[ey] // 64, (START[ey] // 8) % 2)
        half_up, tile_up = (START[ey + 1] // 64, (START[ey + 1] // 8) % 2)
        packed_y += [
            (inner_i * mask_of(half, tile, 7), tile - tile_up, 56 + half - half_up),
            (inner_i * mask_of(half_up, tile_up, 0), tile_up - tile, half_up - half - 56),
        ]

    def packed_sum_y(face):
        total = face
        for wanted, tiles, lanes in packed_y:
            total = total + wanted * lane_roll(pltpu.roll(face, tiles % 8, 0), lanes)
        return total

    def pack_z(r):
        for n, (row, h, k) in enumerate(((0, 0, 0), (7, 1, 7))):
            packed = jnp.zeros((8, 128), F32)
            for slot in range(16):
                i, half = slot // 2, slot % 2
                piece = summed[i, pl.ds(half * 64 + row, 8, stride=8), :]
                moved = lane_roll(piece, (slot // 8 - h) * 64 + slot % 8 - k)
                packed = jnp.where((lane_h == slot // 8) & (lane_k == slot % 8), moved, packed)
            zs[r, n] = packed_sum_y(packed)

    def pack_y(r):
        for n, (ey, j) in enumerate(((0, 0), (3, 7))):
            for g in range(4):
                packed = jnp.zeros((8, 128), F32)
                for slot in range(8):
                    row = (slot // 2) * 16 + START[ey]
                    piece = summed[2 * g + slot % 2, row : row + 8, :]
                    packed = jnp.where(lane_j == slot, lane_roll(piece, 8 * (slot - j)), packed)
                ys[r, n, 8 * g : 8 * g + 8] = packed

    def slot_of(r, g, d):
        n = GROUPS[g].index(d)
        return (xr.at[r, 0], xr.at[r, 1], yr.at[r], xyr.at[r], zer.at[r], zlr.at[r])[g].at[n]

    def message(r, g, d):
        dx, dy, dz = d
        if g < 2:
            src = summed.at[7 if dx > 0 else 0, pl.ds(64 * g, 64)]
        elif g == 2:
            src = ys.at[r, (dy + 1) // 2]
        elif g == 3:
            src = ys.at[r, (dy + 1) // 2, pl.ds(24 if dx > 0 else 0, 8)]
        else:
            src = zs.at[r, (dz + 1) // 2]
        n = sum(len(dirs) for dirs in GROUPS[:g]) + GROUPS[g].index(d)
        return pltpu.make_async_remote_copy(
            src_ref=src,
            dst_ref=slot_of(r, g, d),
            send_sem=send_sem.at[r, n],
            recv_sem=recv_sem.at[r, g],
            device_id=target(d),
            device_id_type=MESH,
        )

    def send(r, g, dirs=None):
        for d in dirs or GROUPS[g]:
            pl.when(to_there[d])(message(r, g, d).start)

    def fill_absent(r):
        for g in range(6):
            source = zero if g < 2 else zero.at[pl.ds(0, 32)] if g == 2 else zero.at[pl.ds(0, 8)]
            for d in GROUPS[g]:
                slot = slot_of(r, g, d)
                copy = pltpu.make_async_copy(source, slot, recv_sem.at[r, g])
                pl.when(jnp.logical_not(from_there(d)))(copy.start)

    def finish(r):
        for g in range(6):
            for d in GROUPS[g]:
                pl.when(to_there[d])(message(r, g, d).wait_send)

    def arrive(r, g):
        slots = (xr.at[r, 0], xr.at[r, 1], yr.at[r], xyr.at[r], zer.at[r], zlr.at[r])[g]
        pltpu.make_async_copy(slots, slots, recv_sem.at[r, g]).wait()

    def z_faces(slots, dirs):
        faces = []
        for dz in (-1, 1):
            face = None
            for n, d in enumerate(dirs):
                if d[2] != dz:
                    continue
                part = slots[n]
                dx, dy, _ = d
                wanted = None
                if dx != 0:
                    near = (lane_k < 2) if dx > 0 else (lane_k >= 6)
                    wanted = h_end[-dx] * fmask(near)
                if dy != 0:
                    mine = mask_of(0, 1 if dy > 0 else 0, 0 if dy > 0 else 7)
                    wanted = mine if wanted is None else wanted * mine
                    part = pltpu.roll(part, dy % 8, 0)
                part = lane_roll(part, -70 * dx - 56 * dy)
                if wanted is not None:
                    part = part * wanted
                face = part if face is None else face + part
            faces.append(face)
        return faces

    def add_z(faces, half):
        for dz, face in zip((-1, 1), faces):
            row, h, k = (0, 0, 0) if dz > 0 else (7, 1, 7)
            for i in range(8):
                slot = 2 * i + half
                where = pl.ds(half * 64 + row, 8, stride=8)
                moved = lane_roll(face, (h - slot // 8) * 64 + k - slot % 8)
                value[i, where, :] = value[i, where, :] + moved * z_end[-dz]

    def take_x(r, half):
        rows = slice(64 * half, 64 * half + 64)
        arrive(r, half)
        for n, d in enumerate(X_DIRS):
            i = 0 if d[0] > 0 else 7
            value[i, rows, :] = value[i, rows, :] + xr[r, half, n]

    def receive_early(r):
        arrive(r, 4)
        faces = z_faces(zer.at[r], Z_EARLY)
        take_x(r, 1)
        add_z(faces, 1)
        return faces

    def receive_late(r, faces):
        take_x(r, 0)
        arrive(r, 2)
        arrive(r, 3)
        for n, d in enumerate(Y_DIRS):
            dy = d[1]
            sides = [yr[r, n, 8 * g : 8 * g + 8] for g in range(4)]
            for dx in (-1, 1):
                edge = lane_roll(xyr[r, XY_DIRS.index((dx, dy, 0))], -8 * dx)
                g = 0 if dx > 0 else 3
                sides[g] = sides[g] + edge * fmask(lane_j % 2 == (0 if dx > 0 else 1))
            ey, j = (0, 0) if dy > 0 else (3, 7)
            for i in range(8):
                for f in range(4):
                    row = f * 16 + START[ey]
                    moved = lane_roll(sides[i // 2], 8 * (j - f * 2 - i % 2))
                    value[i, row : row + 8, :] = value[i, row : row + 8, :] + moved * j_end[-dy]
        arrive(r, 5)
        late = z_faces(zlr.at[r], Z_LATE)
        add_z([face + more for face, more in zip(faces, late)], 0)

    def brick():
        line_j = jnp.zeros((8, 128), F32)
        line_k = jnp.zeros((8, 128), F32)
        for n in range(8):
            line_j = jnp.where(lane_j == n, float(weights[n]), line_j)
            line_k = jnp.where(lane_k == n, float(weights[n]), line_k)
        plane = (line_j * line_k)[:1]
        return jnp.stack([plane * float(weights[n]) for n in range(8)])

    def gradients(block, exact):
        if exact:
            high = block.reshape(-1, 128).astype(BF16)
            left, table = jnp.concatenate([high, high], axis=1), forward[128:384, :]
        else:
            high, low = split(block.reshape(-1, 128))
            left, table = jnp.concatenate([high, low, high], axis=1), forward[...]
        yz = jnp.dot(left, table, preferred_element_type=F32)
        gx = jnp.stack(x_derivative([block[i] for i in range(8)], derivative))
        return gx, yz[:, :128].reshape(block.shape), yz[:, 128:].reshape(block.shape)

    def state_terms(half):
        rows = slice(16 * half, 16 * half + 16)
        moved = group(kept, half)[:, :3]
        gx, gy, gz = gradients(moved, True)
        shear = [gy[:, 0] + gx[:, 1], gz[:, 0] + gx[:, 2], gz[:, 1] + gy[:, 2]]
        normal = [gx[:, 0], gy[:, 1], gz[:, 2]]
        trace_sum = normal[0] + normal[1] + normal[2]
        stress = [lame_lambda * trace_sum + 2.0 * lame_mu * n for n in normal]
        stress += [lame_mu * s for s in shear]
        energy = stress[0] * normal[0] + stress[1] * normal[1] + stress[2] * normal[2]
        energy = 0.5 * (energy + stress[3] * shear[0] + stress[4] * shear[1] + stress[5] * shear[2])
        loading = keep[2, 0, rows, :][None]
        driving = (1.0 - loading) * keep[1, :, rows, :] + loading * energy
        intact = 1.0 - keep[0, :, rows, :]
        mass = brick()
        slope = -2.0 * intact * mass
        for n in range(6):
            state[n, :, rows, :] = slope * stress[n]
        state[6, :, rows, :] = lame_mu * mass * (intact * intact + residual_stiff)
        state[7, :, rows, :] = mass * (gc_inverse + 2.0 * driving)

    def apply_tile(half, tile, block):
        rows = slice(16 * half + 8 * tile, 16 * half + 8 * tile + 8)
        gx, gy, gz = gradients(block, False)
        scaled = [state[n, :, rows, :] for n in range(6)]
        stiff = state[6, :, rows, :]
        vd = block[:, 3]
        coupled = keep[2, 0, rows, :][None] * vd
        shear = [gy[:, 0] + gx[:, 1], gz[:, 0] + gx[:, 2], gz[:, 1] + gy[:, 2]]
        normal = [gx[:, 0], gy[:, 1], gz[:, 2]]
        trace_sum = 1.5 * (normal[0] + normal[1] + normal[2])
        tensor = [stiff * (trace_sum + 2.0 * normal[n]) + scaled[n] * coupled for n in range(3)]
        tensor += [stiff * shear[n] + scaled[n + 3] * coupled for n in range(3)]
        nodal = state[7, :, rows, :] * vd
        for n in range(3):
            nodal = nodal + scaled[n] * normal[n] + scaled[n + 3] * shear[n]
        flux = gc_length * brick()
        along_x = jnp.stack([tensor[0], tensor[3], tensor[4], flux * gx[:, 3]], axis=1)
        along_y = jnp.stack([tensor[3], tensor[1], tensor[5], flux * gy[:, 3]], axis=1)
        along_z = jnp.stack([tensor[4], tensor[5], tensor[2], flux * gz[:, 3]], axis=1)
        y_high, y_low = split(along_y.reshape(-1, 128))
        z_high, z_low = split(along_z.reshape(-1, 128))
        one = jnp.dot(
            jnp.concatenate([y_high, z_high], axis=1), back[...], preferred_element_type=F32
        )
        two = jnp.dot(
            jnp.concatenate([y_low, z_low], axis=1), back[:, :128], preferred_element_type=F32
        )
        total = (one[:, :128] + one[:, 128:] + two).reshape(block.shape)
        total = total + jnp.stack(x_derivative([along_x[i] for i in range(8)], derivative.T))
        result = group(load, half)[:, :, 8 * tile : 8 * tile + 8] - total
        return jnp.concatenate([result[:, :3], (result[:, 3] - nodal)[:, None]], axis=1)

    def apply_transposed(half, block):
        parts = [apply_tile(half, n, block[:, :, 8 * n : 8 * n + 8]) for n in range(2)]
        put_group(summed, half, jnp.concatenate(parts, axis=2))

    def ship(r):
        for half in range(2):
            sum_z(half, 0, 1)
            sum_z(half, 7, 8)
        for e in range(3):
            sum_y(e, ((0, 1), (7, 8)))
        pack_z(r)
        if r == 0:
            pl.semaphore_wait(barrier, neighbours)
        send(r, 1)
        for d in Z_ORDER:
            send(r, 4 if d in Z_EARLY else 5, [d])
        send(r, 0)
        for half in range(2):
            sum_z(half, 1, 7)
        pack_y(r)
        send(r, 3)
        send(r, 2)
        for e in range(3):
            sum_y(e, ((1, 7),))
        value[...] = summed[...]

    copies[1].wait()
    copies[2].wait()
    put_fields(to_tiles([adjoint_b[f] for f in range(4)]), summed, 4)
    ship(0)

    zero[...] = jnp.zeros((64, 128), F32)
    fill_absent(0)

    copies[3].wait()
    copies[4].wait()
    copies[5].wait()
    copies[6].wait()
    tiles = to_tiles([displace_b[0], displace_b[1], displace_b[2], damage_b[...], history_b[...]])
    put_fields(tiles, kept, 3)
    put_single(tiles[12:16], 0)
    put_single(tiles[16:20], 1)
    copies[7].wait()
    frozen = 1.0 - jnp.sum(chosen * frozen_b[...].astype(F32), axis=1, keepdims=True)
    low_half = lax.broadcasted_iota(jnp.int32, (32, 128), 1) < 64
    keep[2, 0] = jnp.where(low_half, frozen[:32], frozen[32:])
    for half in range(2):
        state_terms(half)
    copies[8].wait()
    put_fields(to_tiles([load_b[f] for f in range(4)]), load, 4)
    copies[9].wait()

    def halved(condition, scalar):
        return 1.0 - 0.5 * fmask(condition) * scalar

    inv_z = halved(inner_z, 1.0) * halved(first_z & (sub > 0), 1.0) * halved(last_z & (sub < 7), 1.0)
    inv_z = inv_z * halved(first_z & (sub == 0), present[2][-1]) * halved(last_z & (sub == 7), present[2][1])

    def average(half):
        planes = []
        for ey in EY[half]:
            lower = 1.0 if ey > 0 else present[1][-1]
            upper = 1.0 if ey < 3 else present[1][1]
            planes.append(inv_z * halved(lane_j == 0, lower) * halved(lane_j == 7, upper))
        scale = jnp.concatenate(planes, axis=0)
        scales = [scale] * 8
        scales[0] = scale * (1.0 - 0.5 * present[0][-1])
        scales[7] = scale * (1.0 - 0.5 * present[0][1])
        block = group(value, half) * jnp.stack(scales)[:, None]
        put_group(kept, half, block)
        return block

    def relax(half):
        return group(kept, half) + relaxation * group(value, half)

    fill_absent(1)
    fill_absent(2)

    for r, ready in ((0, average), (1, relax)):
        finish(r)
        faces = receive_early(r)
        apply_transposed(1, ready(1))
        receive_late(r, faces)
        apply_transposed(0, ready(0))
        ship(r + 1)

    def emit(half):
        block = value[:, 64 * half : 64 * half + 64, :].reshape(4, 2, 4, 16, 128)
        sides = jnp.concatenate([block[:, 0], block[:, 1]], axis=3).reshape(256, 256)
        high, low = split(sides)
        moved = jnp.dot(
            jnp.concatenate([high, low], axis=0), swap[...], preferred_element_type=F32
        ).astype(BF16)
        rows = jnp.concatenate([chosen[16 * half : 16 * half + 16], chosen[32 + 16 * half : 48 + 16 * half]], axis=0)
        unpick = jnp.concatenate([rows, rows], axis=0).T.astype(BF16)
        for f in range(4):
            columns = []
            for a in range(4):
                parts = []
                for n in (a * 64 + f * 16, 256 + a * 64 + f * 16):
                    parts += [moved[n : n + 16, :128], moved[n : n + 16, 128:]]
                columns.append(jnp.concatenate(parts, axis=0))
            stacked = jnp.concatenate(columns, axis=1)
            out = jnp.dot(unpick, stacked, preferred_element_type=F32)
            out_ref[f] = out if half == 1 else out_ref[f] + out

    finish(2)
    faces = receive_early(2)
    emit(1)
    receive_late(2, faces)
    emit(0)


def shards(adjoint, load, displace, damage, history, frozen, order):
    forward, back, swap = (jnp.asarray(c) for c in constants())
    hbm = pl.BlockSpec(memory_space=pltpu.HBM)
    return pl.pallas_call(
        kernel,
        out_shape=pltpu.VMEM((4, 64, 512), F32),
        in_specs=[hbm] * 10,
        out_specs=pl.BlockSpec(memory_space=pltpu.VMEM),
        scratch_shapes=[
            pltpu.VMEM((4, 64, 512), BF16),
            pltpu.VMEM((4, 64, 512), BF16),
            pltpu.VMEM((3, 64, 512), BF16),
            pltpu.VMEM((64, 512), BF16),
            pltpu.VMEM((64, 512), BF16),
            pltpu.VMEM((1, 64), jnp.int32),
            pltpu.VMEM((1, 64), jnp.int32),
            pltpu.VMEM((384, 256), BF16),
            pltpu.VMEM((256, 256), BF16),
            pltpu.VMEM((256, 256), BF16),
            pltpu.VMEM((8, 128, 128), F32),
            pltpu.VMEM((8, 128, 128), F32),
            pltpu.VMEM((8, 128, 128), F32),
            pltpu.VMEM((8, 128, 128), F32),
            pltpu.VMEM((8, 8, 32, 128), F32),
            pltpu.VMEM((3, 8, 32, 128), F32),
            pltpu.VMEM((3, 2, 32, 128), F32),
            pltpu.VMEM((3, 2, 8, 128), F32),
            pltpu.VMEM((3, 2, 2, 64, 128), F32),
            pltpu.VMEM((3, 2, 32, 128), F32),
            pltpu.VMEM((3, 4, 8, 128), F32),
            pltpu.VMEM((3, 6, 8, 128), F32),
            pltpu.VMEM((3, 12, 8, 128), F32),
            pltpu.VMEM((64, 128), F32),
            pltpu.SemaphoreType.DMA((10,)),
            pltpu.SemaphoreType.DMA((3, 28)),
            pltpu.SemaphoreType.DMA((3, 6)),
        ],
        compiler_params=pltpu.CompilerParams(
            collective_id=0, has_side_effects=True, vmem_limit_bytes=56 * 1024 * 1024
        ),
    )(adjoint, load, displace, damage, history, frozen.reshape(1, 64), order, forward, back, swap)


def solution(mesh):
    in_specs = (
        P(None, ("gx", "gy", "gz"), None),
        P(None, ("gx", "gy", "gz"), None),
        P(None, ("gx", "gy", "gz"), None),
        P(("gx", "gy", "gz"), None),
        P(("gx", "gy", "gz"), None),
        P(("gx", "gy", "gz")),
        P(("gx", "gy", "gz"), None),
    )
    out_specs = P(None, ("gx", "gy", "gz"), None)
    return jax.shard_map(shards, mesh=mesh, in_specs=in_specs, out_specs=out_specs, check_vma=False)
```

```python
import jax
import jax.numpy as jnp
import ml_dtypes
import numpy as np
from jax import lax
from jax.experimental import pallas as pl
from jax.experimental.pallas import tpu as pltpu
from jax.sharding import PartitionSpec as P

F32 = jnp.float32
BF16 = jnp.bfloat16
MESH = pl.DeviceIdType.MESH

lame_lambda = 0.15
lame_mu = 0.1
gc_length = 0.3
gc_inverse = 40.0
residual_stiff = 0.001
relaxation = 0.5
gll_points = (
    -1.0,
    -0.8717401485096066,
    -0.5917001814331423,
    -0.2092992179024789,
    0.2092992179024789,
    0.5917001814331423,
    0.8717401485096066,
    1.0,
)

EY = ((3, 0), (1, 2))
START = {ey: 64 * half + 8 * tile for half in range(2) for tile, ey in enumerate(EY[half])}

DIRS = [
    (dx, dy, dz)
    for dx in (-1, 0, 1)
    for dy in (-1, 0, 1)
    for dz in (-1, 0, 1)
    if (dx, dy, dz) != (0, 0, 0)
]
X_DIRS = [d for d in DIRS if d[1] == 0 and d[2] == 0]
Y_DIRS = [d for d in DIRS if d[0] == 0 and d[1] != 0 and d[2] == 0]
XY_DIRS = [d for d in DIRS if d[0] != 0 and d[1] != 0 and d[2] == 0]
Z_DIRS = [d for d in DIRS if d[2] != 0]
Z_LATE = [d for d in Z_DIRS if d[1] != 0]
Z_EARLY = [d for d in Z_DIRS if d[1] == 0]
Z_ORDER = sorted(Z_DIRS, key=lambda d: -abs(d[0]) - abs(d[1]))
GROUPS = (X_DIRS, X_DIRS, Y_DIRS, XY_DIRS, Z_EARLY, Z_LATE)


def legendre_at(points, degree):
    values = []
    for point in points:
        previous = 1.0
        current = point
        for level in range(1, degree):
            following = ((2 * level + 1) * point * current - level * previous) / (level + 1)
            previous = current
            current = following
        values.append(current)
    return values


def gll_tables():
    degree = 7
    points = list(gll_points)
    legendre_vals = legendre_at(points, degree)
    weights = [2.0 / (degree * (degree + 1) * entry * entry) for entry in legendre_vals]
    derivative = []
    for row_index in range(degree + 1):
        row_vals = []
        for col_index in range(degree + 1):
            if row_index != col_index:
                row_vals.append(
                    legendre_vals[row_index]
                    / (legendre_vals[col_index] * (points[row_index] - points[col_index]))
                )
            else:
                row_vals.append(0.0)
        derivative.append(row_vals)
    derivative[0][0] = -degree * (degree + 1) / 4.0
    derivative[degree][degree] = degree * (degree + 1) / 4.0
    return (np.array(weights), np.array(derivative))


def split_np(matrix):
    high = matrix.astype(np.float32).astype(ml_dtypes.bfloat16)
    low = (matrix - high.astype(np.float64)).astype(np.float32).astype(ml_dtypes.bfloat16)
    return high, low


def constants():
    _, derivative = gll_tables()
    eye = np.eye
    forward_y = np.kron(eye(2), np.kron(derivative.T, eye(8)))
    forward_z = np.kron(eye(16), derivative.T)
    back_y = np.kron(eye(2), np.kron(derivative, eye(8)))
    back_z = np.kron(eye(16), derivative)
    f_high, f_low = split_np(np.concatenate([forward_y, forward_z], axis=1))
    forward = np.concatenate([f_high, f_high, f_low], axis=0)
    b_high, b_low = split_np(np.concatenate([back_y, back_z], axis=0))
    back = np.concatenate([b_high, b_low], axis=1)
    swap = np.zeros((2, 2, 64, 2, 2, 64))
    for h in range(2):
        for odd in range(2):
            swap[h, odd, :, odd, h, :] = eye(64)
    swap = swap.reshape(256, 256).astype(ml_dtypes.bfloat16)
    return forward, back, swap


def lane_roll(value, shift):
    shift = shift % 128
    if shift == 0:
        return value
    flat = value.reshape(-1, 128)
    return pltpu.roll(flat, shift, 1).reshape(value.shape)


def lane_swap(value, mask):
    flat = value.reshape(-1, 128)
    index = jnp.bitwise_xor(lax.broadcasted_iota(jnp.int32, flat.shape, 1), mask)
    return jnp.take_along_axis(flat, index, axis=1).reshape(value.shape)


def split(value):
    high = value.astype(BF16)
    low = (value - high.astype(F32)).astype(BF16)
    return high, low


def x_derivative(tiles, matrix):
    even_part = (matrix + matrix[:, ::-1]) / 2
    odd_part = (matrix - matrix[:, ::-1]) / 2
    even = [tiles[n] + tiles[7 - n] for n in range(4)]
    odd = [tiles[n] - tiles[7 - n] for n in range(4)]
    out = [None] * 8
    for n in range(4):
        first = float(even_part[n, 0]) * even[0]
        second = float(odd_part[n, 0]) * odd[0]
        for m in range(1, 4):
            first = first + float(even_part[n, m]) * even[m]
            second = second + float(odd_part[n, m]) * odd[m]
        out[n] = second + first
        out[7 - n] = second - first
    return out


def kernel(
    adjoint_h,
    load_h,
    displace_h,
    damage_h,
    history_h,
    frozen_h,
    order_h,
    forward_h,
    back_h,
    swap_h,
    out_ref,
    adjoint_b,
    load_b,
    displace_b,
    damage_b,
    history_b,
    frozen_b,
    order_b,
    forward,
    back,
    swap,
    value,
    kept,
    load,
    summed,
    state,
    keep,
    ys,
    zs,
    xr,
    yr,
    xyr,
    zer,
    zlr,
    zero,
    in_sem,
    send_sem,
    recv_sem,
):
    weights, derivative = gll_tables()
    px, py, pz = (lax.axis_index("gx"), lax.axis_index("gy"), lax.axis_index("gz"))
    sizes = (lax.axis_size("gx"), lax.axis_size("gy"), lax.axis_size("gz"))

    pairs = (
        (order_h, order_b),
        (adjoint_h, adjoint_b),
        (swap_h, swap),
        (displace_h, displace_b),
        (forward_h, forward),
        (damage_h, damage_b),
        (history_h, history_b),
        (frozen_h, frozen_b),
        (load_h, load_b),
        (back_h, back),
    )
    copies = [pltpu.make_async_copy(src, dst, in_sem.at[n]) for n, (src, dst) in enumerate(pairs)]
    for copy in copies[:3]:
        copy.start()

    along = [
        {
            -1: lax.rem(p + n - 1, n),
            0: p,
            1: lax.rem(p + 1, n),
        }
        for p, n in zip((px, py, pz), sizes)
    ]

    def target(d):
        return tuple(along[axis][d[axis]] for axis in range(3))

    has = [{-1: p > 0, 1: p < n - 1} for p, n in zip((px, py, pz), sizes)]
    present = [{s: side[s].astype(F32) for s in (-1, 1)} for side in has]

    def there(d):
        sides = [has[axis][d[axis]] for axis in range(3) if d[axis] != 0]
        found = sides[0]
        for side in sides[1:]:
            found = jnp.logical_and(found, side)
        return found

    to_there = {d: there(d) for d in DIRS}

    def from_there(d):
        return to_there[(-d[0], -d[1], -d[2])]

    barrier = pltpu.get_barrier_semaphore()
    for d in sorted(DIRS, key=lambda d: -abs(d[0]) - abs(d[1]) - abs(d[2])):

        @pl.when(to_there[d])
        def _(d=d):
            pl.semaphore_signal(barrier, inc=1, device_id=target(d), device_id_type=MESH)

    around = [1 + side[-1].astype(jnp.int32) + side[1].astype(jnp.int32) for side in has]
    neighbours = around[0] * around[1] * around[2] - 1
    for copy in copies[3:]:
        copy.start()

    lane = lax.broadcasted_iota(jnp.int32, (8, 128), 1)
    sub = lax.broadcasted_iota(jnp.int32, (8, 128), 0)
    lane_k = lane % 8
    lane_j = (lane // 8) % 8
    lane_h = lane // 64

    def fmask(condition):
        return jnp.where(condition, 1.0, 0.0).astype(F32)

    j_end = {-1: fmask(lane_j == 0), 1: fmask(lane_j == 7)}
    h_end = {-1: fmask(lane_h == 0), 1: fmask(lane_h == 1)}
    first_z = (lane_h == 0) & (lane_k == 0)
    last_z = (lane_h == 1) & (lane_k == 7)
    z_end = {-1: fmask(first_z), 1: fmask(last_z)}
    inner_z = ((lane_h == 0) & (lane_k == 7)) | ((lane_h == 1) & (lane_k == 0))
    z_here = fmask(inner_z | (last_z & (sub < 7)))
    z_next = fmask(first_z & (sub > 0))

    copies[0].wait()
    row_id = lax.broadcasted_iota(jnp.int32, (64, 64), 0)
    tile_id = (row_id // 8) % 4
    row_ey = (tile_id + 3) % 4
    place = row_ey * 16 + 2 * (row_id % 8) + row_id // 32
    chosen = fmask(place == order_b[...])
    pick = chosen.astype(BF16)

    def to_tiles(fields):
        sides = []
        for stored in fields:
            rows = jnp.dot(pick, stored, preferred_element_type=F32).astype(BF16)
            for n in range(0, 512, 128):
                sides.append(jnp.concatenate([rows[:32, n : n + 128], rows[32:, n : n + 128]], axis=1))
        tiles = jnp.dot(
            jnp.concatenate(sides, axis=0), swap[...], preferred_element_type=F32
        )
        return tiles.reshape(len(fields) * 4, 32, 256)

    def put_fields(tiles, ref, fields):
        for f in range(fields):
            for a in range(4):
                for half in range(2):
                    rows = slice(half * 64 + f * 16, half * 64 + f * 16 + 16)
                    both = tiles[4 * f + a, half * 16 : half * 16 + 16, :]
                    ref[2 * a, rows, :] = both[:, :128]
                    ref[2 * a + 1, rows, :] = both[:, 128:]

    def put_single(tiles, n):
        for a in range(4):
            keep[n, 2 * a] = tiles[a, :, :128]
            keep[n, 2 * a + 1] = tiles[a, :, 128:]

    def group(ref, half):
        return ref[:, half * 64 : half * 64 + 64, :].reshape(8, 4, 16, 128)

    def put_group(ref, half, block):
        ref[:, half * 64 : half * 64 + 64, :] = block.reshape(8, 64, 128)

    def sum_z(half, first, last):
        rows = slice(64 * half, 64 * half + 64)
        flat = summed[first:last, rows, :].reshape(-1, 8, 128)
        taken = lane_swap(jnp.where(first_z, pltpu.roll(flat, 7, 1), flat), 71)
        total = flat + z_here * taken + z_next * pltpu.roll(taken, 1, 1)
        summed[first:last, rows, :] = total.reshape(last - first, 64, 128)

    def sum_y(e, spans):
        for first, last in spans:
            for f in range(4):
                lower = slice(START[e] + f * 16, START[e] + f * 16 + 8)
                upper = slice(START[e + 1] + f * 16, START[e + 1] + f * 16 + 8)
                here, beyond = summed[first:last, lower, :], summed[first:last, upper, :]
                taken = lane_swap(jnp.where(lane_j == 7, here, beyond), 56)
                summed[first:last, lower, :] = here + j_end[1] * taken
                summed[first:last, upper, :] = beyond + j_end[-1] * taken

    def mask_of(half, tile, j):
        return fmask((lane_k % 2 == half) & (sub % 2 == tile) & (lane_j == j))

    packed_y = []
    for ey in range(3):
        half, tile = (START[ey] // 64, (START[ey] // 8) % 2)
        half_up, tile_up = (START[ey + 1] // 64, (START[ey + 1] // 8) % 2)
        packed_y += [
            (mask_of(half, tile, 7), tile - tile_up, 56 + half - half_up),
            (mask_of(half_up, tile_up, 0), tile_up - tile, half_up - half - 56),
        ]

    def packed_sum_y(face):
        total = face
        for wanted, tiles, lanes in packed_y:
            total = total + wanted * lane_roll(pltpu.roll(face, tiles % 8, 0), lanes)
        return total

    def pack_z(r):
        for n, (row, h, k) in enumerate(((0, 0, 0), (7, 1, 7))):
            packed = jnp.zeros((8, 128), F32)
            for slot in range(16):
                i, half = slot // 2, slot % 2
                piece = summed[i, pl.ds(half * 64 + row, 8, stride=8), :]
                moved = lane_roll(piece, (slot // 8 - h) * 64 + slot % 8 - k)
                packed = jnp.where((lane_h == slot // 8) & (lane_k == slot % 8), moved, packed)
            zs[r, n] = packed_sum_y(packed)

    def pack_y(r):
        for n, (ey, j) in enumerate(((0, 0), (3, 7))):
            for g in range(4):
                packed = jnp.zeros((8, 128), F32)
                for slot in range(8):
                    row = (slot // 2) * 16 + START[ey]
                    piece = summed[2 * g + slot % 2, row : row + 8, :]
                    packed = jnp.where(lane_j == slot, lane_roll(piece, 8 * (slot - j)), packed)
                ys[r, n, 8 * g : 8 * g + 8] = packed

    def slot_of(r, g, d):
        n = GROUPS[g].index(d)
        return (xr.at[r, 0], xr.at[r, 1], yr.at[r], xyr.at[r], zer.at[r], zlr.at[r])[g].at[n]

    def message(r, g, d):
        dx, dy, dz = d
        if g < 2:
            src = summed.at[7 if dx > 0 else 0, pl.ds(64 * g, 64)]
        elif g == 2:
            src = ys.at[r, (dy + 1) // 2]
        elif g == 3:
            src = ys.at[r, (dy + 1) // 2, pl.ds(24 if dx > 0 else 0, 8)]
        else:
            src = zs.at[r, (dz + 1) // 2]
        n = sum(len(dirs) for dirs in GROUPS[:g]) + GROUPS[g].index(d)
        return pltpu.make_async_remote_copy(
            src_ref=src,
            dst_ref=slot_of(r, g, d),
            send_sem=send_sem.at[r, n],
            recv_sem=recv_sem.at[r, g],
            device_id=target(d),
            device_id_type=MESH,
        )

    def send(r, g, dirs=None):
        for d in dirs or GROUPS[g]:
            pl.when(to_there[d])(message(r, g, d).start)

    def fill_absent(r):
        for g in range(6):
            source = zero if g < 2 else zero.at[pl.ds(0, 32)] if g == 2 else zero.at[pl.ds(0, 8)]
            for d in GROUPS[g]:
                slot = slot_of(r, g, d)
                copy = pltpu.make_async_copy(source, slot, recv_sem.at[r, g])
                pl.when(jnp.logical_not(from_there(d)))(copy.start)

    def finish(r):
        for g in range(6):
            for d in GROUPS[g]:
                pl.when(to_there[d])(message(r, g, d).wait_send)

    def arrive(r, g):
        slots = (xr.at[r, 0], xr.at[r, 1], yr.at[r], xyr.at[r], zer.at[r], zlr.at[r])[g]
        pltpu.make_async_copy(slots, slots, recv_sem.at[r, g]).wait()

    def z_faces(slots, dirs):
        faces = []
        for dz in (-1, 1):
            face = None
            for n, d in enumerate(dirs):
                if d[2] != dz:
                    continue
                part = slots[n]
                dx, dy, _ = d
                wanted = None
                if dx != 0:
                    near = (lane_k < 2) if dx > 0 else (lane_k >= 6)
                    wanted = h_end[-dx] * fmask(near)
                if dy != 0:
                    mine = mask_of(0, 1 if dy > 0 else 0, 0 if dy > 0 else 7)
                    wanted = mine if wanted is None else wanted * mine
                    part = pltpu.roll(part, dy % 8, 0)
                part = lane_roll(part, -70 * dx - 56 * dy)
                if wanted is not None:
                    part = part * wanted
                face = part if face is None else face + part
            faces.append(face)
        return faces

    def add_z(faces, half):
        for dz, face in zip((-1, 1), faces):
            row, h, k = (0, 0, 0) if dz > 0 else (7, 1, 7)
            for i in range(8):
                slot = 2 * i + half
                where = pl.ds(half * 64 + row, 8, stride=8)
                moved = lane_roll(face, (h - slot // 8) * 64 + k - slot % 8)
                value[i, where, :] = value[i, where, :] + moved * z_end[-dz]

    def take_x(r, half):
        rows = slice(64 * half, 64 * half + 64)
        arrive(r, half)
        for n, d in enumerate(X_DIRS):
            i = 0 if d[0] > 0 else 7
            value[i, rows, :] = value[i, rows, :] + xr[r, half, n]

    def receive_early(r):
        arrive(r, 4)
        faces = z_faces(zer.at[r], Z_EARLY)
        take_x(r, 1)
        add_z(faces, 1)
        return faces

    def receive_late(r, faces):
        take_x(r, 0)
        arrive(r, 2)
        arrive(r, 3)
        for n, d in enumerate(Y_DIRS):
            dy = d[1]
            sides = [yr[r, n, 8 * g : 8 * g + 8] for g in range(4)]
            for dx in (-1, 1):
                edge = lane_roll(xyr[r, XY_DIRS.index((dx, dy, 0))], -8 * dx)
                g = 0 if dx > 0 else 3
                sides[g] = sides[g] + edge * fmask(lane_j % 2 == (0 if dx > 0 else 1))
            ey, j = (0, 0) if dy > 0 else (3, 7)
            for i in range(8):
                for f in range(4):
                    row = f * 16 + START[ey]
                    moved = lane_roll(sides[i // 2], 8 * (j - f * 2 - i % 2))
                    value[i, row : row + 8, :] = value[i, row : row + 8, :] + moved * j_end[-dy]
        arrive(r, 5)
        late = z_faces(zlr.at[r], Z_LATE)
        add_z([face + more for face, more in zip(faces, late)], 0)

    def brick():
        line_j = jnp.zeros((8, 128), F32)
        line_k = jnp.zeros((8, 128), F32)
        for n in range(8):
            line_j = jnp.where(lane_j == n, float(weights[n]), line_j)
            line_k = jnp.where(lane_k == n, float(weights[n]), line_k)
        plane = (line_j * line_k)[:1]
        return jnp.stack([plane * float(weights[n]) for n in range(8)])

    def gradients(block, exact):
        if exact:
            high = block.reshape(-1, 128).astype(BF16)
            left, table = jnp.concatenate([high, high], axis=1), forward[128:384, :]
        else:
            high, low = split(block.reshape(-1, 128))
            left, table = jnp.concatenate([high, low, high], axis=1), forward[...]
        yz = jnp.dot(left, table, preferred_element_type=F32)
        gx = jnp.stack(x_derivative([block[i] for i in range(8)], derivative))
        return gx, yz[:, :128].reshape(block.shape), yz[:, 128:].reshape(block.shape)

    def state_terms(half):
        rows = slice(16 * half, 16 * half + 16)
        moved = group(kept, half)[:, :3]
        gx, gy, gz = gradients(moved, True)
        shear = [gy[:, 0] + gx[:, 1], gz[:, 0] + gx[:, 2], gz[:, 1] + gy[:, 2]]
        normal = [gx[:, 0], gy[:, 1], gz[:, 2]]
        trace_sum = normal[0] + normal[1] + normal[2]
        stress = [lame_lambda * trace_sum + 2.0 * lame_mu * n for n in normal]
        stress += [lame_mu * s for s in shear]
        energy = stress[0] * normal[0] + stress[1] * normal[1] + stress[2] * normal[2]
        energy = 0.5 * (energy + stress[3] * shear[0] + stress[4] * shear[1] + stress[5] * shear[2])
        loading = keep[2, 0, rows, :][None]
        driving = (1.0 - loading) * keep[1, :, rows, :] + loading * energy
        intact = 1.0 - keep[0, :, rows, :]
        mass = brick()
        slope = -2.0 * intact * mass
        for n in range(6):
            state[n, :, rows, :] = slope * stress[n]
        state[6, :, rows, :] = lame_mu * mass * (intact * intact + residual_stiff)
        state[7, :, rows, :] = mass * (gc_inverse + 2.0 * driving)

    def apply_tile(half, tile, block):
        rows = slice(16 * half + 8 * tile, 16 * half + 8 * tile + 8)
        gx, gy, gz = gradients(block, False)
        scaled = [state[n, :, rows, :] for n in range(6)]
        stiff = state[6, :, rows, :]
        vd = block[:, 3]
        coupled = keep[2, 0, rows, :][None] * vd
        shear = [gy[:, 0] + gx[:, 1], gz[:, 0] + gx[:, 2], gz[:, 1] + gy[:, 2]]
        normal = [gx[:, 0], gy[:, 1], gz[:, 2]]
        trace_sum = 1.5 * (normal[0] + normal[1] + normal[2])
        tensor = [stiff * (trace_sum + 2.0 * normal[n]) + scaled[n] * coupled for n in range(3)]
        tensor += [stiff * shear[n] + scaled[n + 3] * coupled for n in range(3)]
        nodal = state[7, :, rows, :] * vd
        for n in range(3):
            nodal = nodal + scaled[n] * normal[n] + scaled[n + 3] * shear[n]
        flux = gc_length * brick()
        along_x = jnp.stack([tensor[0], tensor[3], tensor[4], flux * gx[:, 3]], axis=1)
        along_y = jnp.stack([tensor[3], tensor[1], tensor[5], flux * gy[:, 3]], axis=1)
        along_z = jnp.stack([tensor[4], tensor[5], tensor[2], flux * gz[:, 3]], axis=1)
        y_high, y_low = split(along_y.reshape(-1, 128))
        z_high, z_low = split(along_z.reshape(-1, 128))
        one = jnp.dot(
            jnp.concatenate([y_high, z_high], axis=1), back[...], preferred_element_type=F32
        )
        two = jnp.dot(
            jnp.concatenate([y_low, z_low], axis=1), back[:, :128], preferred_element_type=F32
        )
        total = (one[:, :128] + one[:, 128:] + two).reshape(block.shape)
        total = total + jnp.stack(x_derivative([along_x[i] for i in range(8)], derivative.T))
        result = group(load, half)[:, :, 8 * tile : 8 * tile + 8] - total
        return jnp.concatenate([result[:, :3], (result[:, 3] - nodal)[:, None]], axis=1)

    def apply_transposed(half, block):
        parts = [apply_tile(half, n, block[:, :, 8 * n : 8 * n + 8]) for n in range(2)]
        put_group(summed, half, jnp.concatenate(parts, axis=2))

    def ship(r):
        pack_z(r)
        for half in range(2):
            sum_z(half, 0, 1)
            sum_z(half, 7, 8)
        for e in range(3):
            sum_y(e, ((0, 1), (7, 8)))
        if r == 0:
            pl.semaphore_wait(barrier, neighbours)
        for d in Z_ORDER[:8]:
            send(r, 5, [d])
        send(r, 1)
        for d in Z_ORDER[8:]:
            send(r, 4 if d in Z_EARLY else 5, [d])
        for half in range(2):
            sum_z(half, 1, 7)
        pack_y(r)
        send(r, 3)
        send(r, 2)
        send(r, 0)
        for e in range(3):
            sum_y(e, ((1, 7),))
        value[...] = summed[...]

    copies[1].wait()
    copies[2].wait()
    put_fields(to_tiles([adjoint_b[f] for f in range(4)]), summed, 4)
    ship(0)

    zero[...] = jnp.zeros((64, 128), F32)
    fill_absent(0)

    copies[3].wait()
    copies[4].wait()
    copies[5].wait()
    copies[6].wait()
    tiles = to_tiles([displace_b[0], displace_b[1], displace_b[2], damage_b[...], history_b[...]])
    put_fields(tiles, kept, 3)
    put_single(tiles[12:16], 0)
    put_single(tiles[16:20], 1)
    copies[7].wait()
    frozen = 1.0 - jnp.sum(chosen * frozen_b[...].astype(F32), axis=1, keepdims=True)
    low_half = lax.broadcasted_iota(jnp.int32, (32, 128), 1) < 64
    keep[2, 0] = jnp.where(low_half, frozen[:32], frozen[32:])
    for half in range(2):
        state_terms(half)
    copies[8].wait()
    put_fields(to_tiles([load_b[f] for f in range(4)]), load, 4)
    copies[9].wait()

    def halved(condition, scalar):
        return 1.0 - 0.5 * fmask(condition) * scalar

    inv_z = halved(inner_z, 1.0) * halved(first_z & (sub > 0), 1.0) * halved(last_z & (sub < 7), 1.0)
    inv_z = inv_z * halved(first_z & (sub == 0), present[2][-1]) * halved(last_z & (sub == 7), present[2][1])

    def average(half):
        planes = []
        for ey in EY[half]:
            lower = 1.0 if ey > 0 else present[1][-1]
            upper = 1.0 if ey < 3 else present[1][1]
            planes.append(inv_z * halved(lane_j == 0, lower) * halved(lane_j == 7, upper))
        scale = jnp.concatenate(planes, axis=0)
        scales = [scale] * 8
        scales[0] = scale * (1.0 - 0.5 * present[0][-1])
        scales[7] = scale * (1.0 - 0.5 * present[0][1])
        block = group(value, half) * jnp.stack(scales)[:, None]
        put_group(kept, half, block)
        return block

    def relax(half):
        return group(kept, half) + relaxation * group(value, half)

    fill_absent(1)
    fill_absent(2)

    for r, ready in ((0, average), (1, relax)):
        finish(r)
        faces = receive_early(r)
        apply_transposed(1, ready(1))
        receive_late(r, faces)
        apply_transposed(0, ready(0))
        ship(r + 1)

    def emit(half):
        block = value[:, 64 * half : 64 * half + 64, :].reshape(4, 2, 4, 16, 128)
        sides = jnp.concatenate([block[:, 0], block[:, 1]], axis=3).reshape(256, 256)
        high, low = split(sides)
        moved = jnp.dot(
            jnp.concatenate([high, low], axis=0), swap[...], preferred_element_type=F32
        ).astype(BF16)
        rows = jnp.concatenate([chosen[16 * half : 16 * half + 16], chosen[32 + 16 * half : 48 + 16 * half]], axis=0)
        unpick = jnp.concatenate([rows, rows], axis=0).T.astype(BF16)
        for f in range(4):
            columns = []
            for a in range(4):
                parts = []
                for n in (a * 64 + f * 16, 256 + a * 64 + f * 16):
                    parts += [moved[n : n + 16, :128], moved[n : n + 16, 128:]]
                columns.append(jnp.concatenate(parts, axis=0))
            stacked = jnp.concatenate(columns, axis=1)
            out = jnp.dot(unpick, stacked, preferred_element_type=F32)
            out_ref[f] = out if half == 1 else out_ref[f] + out

    finish(2)
    faces = receive_early(2)
    emit(1)
    receive_late(2, faces)
    emit(0)


def shards(adjoint, load, displace, damage, history, frozen, order):
    forward, back, swap = (jnp.asarray(c) for c in constants())
    hbm = pl.BlockSpec(memory_space=pltpu.HBM)
    return pl.pallas_call(
        kernel,
        out_shape=pltpu.VMEM((4, 64, 512), F32),
        in_specs=[hbm] * 10,
        out_specs=pl.BlockSpec(memory_space=pltpu.VMEM),
        scratch_shapes=[
            pltpu.VMEM((4, 64, 512), BF16),
            pltpu.VMEM((4, 64, 512), BF16),
            pltpu.VMEM((3, 64, 512), BF16),
            pltpu.VMEM((64, 512), BF16),
            pltpu.VMEM((64, 512), BF16),
            pltpu.VMEM((1, 64), jnp.int32),
            pltpu.VMEM((1, 64), jnp.int32),
            pltpu.VMEM((384, 256), BF16),
            pltpu.VMEM((256, 256), BF16),
            pltpu.VMEM((256, 256), BF16),
            pltpu.VMEM((8, 128, 128), F32),
            pltpu.VMEM((8, 128, 128), F32),
            pltpu.VMEM((8, 128, 128), F32),
            pltpu.VMEM((8, 128, 128), F32),
            pltpu.VMEM((8, 8, 32, 128), F32),
            pltpu.VMEM((3, 8, 32, 128), F32),
            pltpu.VMEM((3, 2, 32, 128), F32),
            pltpu.VMEM((3, 2, 8, 128), F32),
            pltpu.VMEM((3, 2, 2, 64, 128), F32),
            pltpu.VMEM((3, 2, 32, 128), F32),
            pltpu.VMEM((3, 4, 8, 128), F32),
            pltpu.VMEM((3, 6, 8, 128), F32),
            pltpu.VMEM((3, 12, 8, 128), F32),
            pltpu.VMEM((64, 128), F32),
            pltpu.SemaphoreType.DMA((10,)),
            pltpu.SemaphoreType.DMA((3, 28)),
            pltpu.SemaphoreType.DMA((3, 6)),
        ],
        compiler_params=pltpu.CompilerParams(
            collective_id=0, has_side_effects=True, vmem_limit_bytes=56 * 1024 * 1024
        ),
    )(adjoint, load, displace, damage, history, frozen.reshape(1, 64), order, forward, back, swap)


def solution(mesh):
    in_specs = (
        P(None, ("gx", "gy", "gz"), None),
        P(None, ("gx", "gy", "gz"), None),
        P(None, ("gx", "gy", "gz"), None),
        P(("gx", "gy", "gz"), None),
        P(("gx", "gy", "gz"), None),
        P(("gx", "gy", "gz")),
        P(("gx", "gy", "gz"), None),
    )
    out_specs = P(None, ("gx", "gy", "gz"), None)
    return jax.shard_map(shards, mesh=mesh, in_specs=in_specs, out_specs=out_specs, check_vma=False)
```

```python
import jax
import jax.numpy as jnp
import ml_dtypes
import numpy as np
from jax import lax
from jax.experimental import pallas as pl
from jax.experimental.pallas import tpu as pltpu
from jax.sharding import PartitionSpec as P

F32 = jnp.float32
BF16 = jnp.bfloat16
MESH = pl.DeviceIdType.MESH

lame_lambda = 0.15
lame_mu = 0.1
gc_length = 0.3
gc_inverse = 40.0
residual_stiff = 0.001
relaxation = 0.5
gll_points = (
    -1.0,
    -0.8717401485096066,
    -0.5917001814331423,
    -0.2092992179024789,
    0.2092992179024789,
    0.5917001814331423,
    0.8717401485096066,
    1.0,
)

EY = ((3, 0), (1, 2))
START = {ey: 64 * half + 8 * tile for half in range(2) for tile, ey in enumerate(EY[half])}

DIRS = [
    (dx, dy, dz)
    for dx in (-1, 0, 1)
    for dy in (-1, 0, 1)
    for dz in (-1, 0, 1)
    if (dx, dy, dz) != (0, 0, 0)
]
X_DIRS = [d for d in DIRS if d[1] == 0 and d[2] == 0]
Y_DIRS = [d for d in DIRS if d[0] == 0 and d[1] != 0 and d[2] == 0]
XY_DIRS = [d for d in DIRS if d[0] != 0 and d[1] != 0 and d[2] == 0]
Z_DIRS = [d for d in DIRS if d[2] != 0]
Z_LATE = [d for d in Z_DIRS if d[1] != 0]
Z_EARLY = [d for d in Z_DIRS if d[1] == 0]
Z_ORDER = sorted(Z_DIRS, key=lambda d: -abs(d[0]) - abs(d[1]))
GROUPS = (X_DIRS, X_DIRS, Y_DIRS, XY_DIRS, Z_EARLY, Z_LATE)


def legendre_at(points, degree):
    values = []
    for point in points:
        previous = 1.0
        current = point
        for level in range(1, degree):
            following = ((2 * level + 1) * point * current - level * previous) / (level + 1)
            previous = current
            current = following
        values.append(current)
    return values


def gll_tables():
    degree = 7
    points = list(gll_points)
    legendre_vals = legendre_at(points, degree)
    weights = [2.0 / (degree * (degree + 1) * entry * entry) for entry in legendre_vals]
    derivative = []
    for row_index in range(degree + 1):
        row_vals = []
        for col_index in range(degree + 1):
            if row_index != col_index:
                row_vals.append(
                    legendre_vals[row_index]
                    / (legendre_vals[col_index] * (points[row_index] - points[col_index]))
                )
            else:
                row_vals.append(0.0)
        derivative.append(row_vals)
    derivative[0][0] = -degree * (degree + 1) / 4.0
    derivative[degree][degree] = degree * (degree + 1) / 4.0
    return (np.array(weights), np.array(derivative))


def split_np(matrix):
    high = matrix.astype(np.float32).astype(ml_dtypes.bfloat16)
    low = (matrix - high.astype(np.float64)).astype(np.float32).astype(ml_dtypes.bfloat16)
    return high, low


def constants():
    _, derivative = gll_tables()
    eye = np.eye
    forward_y = np.kron(eye(2), np.kron(derivative.T, eye(8)))
    forward_z = np.kron(eye(16), derivative.T)
    back_y = np.kron(eye(2), np.kron(derivative, eye(8)))
    back_z = np.kron(eye(16), derivative)
    f_high, f_low = split_np(np.concatenate([forward_y, forward_z], axis=1))
    forward = np.concatenate([f_high, f_high, f_low], axis=0)
    b_high, b_low = split_np(np.concatenate([back_y, back_z], axis=0))
    back = np.concatenate([b_high, b_low], axis=1)
    swap = np.zeros((2, 2, 64, 2, 2, 64))
    for h in range(2):
        for odd in range(2):
            swap[h, odd, :, odd, h, :] = eye(64)
    swap = swap.reshape(256, 256).astype(ml_dtypes.bfloat16)
    return forward, back, swap


def lane_roll(value, shift):
    shift = shift % 128
    if shift == 0:
        return value
    flat = value.reshape(-1, 128)
    return pltpu.roll(flat, shift, 1).reshape(value.shape)


def lane_swap(value, mask):
    flat = value.reshape(-1, 128)
    index = jnp.bitwise_xor(lax.broadcasted_iota(jnp.int32, flat.shape, 1), mask)
    return jnp.take_along_axis(flat, index, axis=1).reshape(value.shape)


def split(value):
    high = value.astype(BF16)
    low = (value - high.astype(F32)).astype(BF16)
    return high, low


def x_derivative(tiles, matrix):
    even_part = (matrix + matrix[:, ::-1]) / 2
    odd_part = (matrix - matrix[:, ::-1]) / 2
    even = [tiles[n] + tiles[7 - n] for n in range(4)]
    odd = [tiles[n] - tiles[7 - n] for n in range(4)]
    out = [None] * 8
    for n in range(4):
        first = float(even_part[n, 0]) * even[0]
        second = float(odd_part[n, 0]) * odd[0]
        for m in range(1, 4):
            first = first + float(even_part[n, m]) * even[m]
            second = second + float(odd_part[n, m]) * odd[m]
        out[n] = second + first
        out[7 - n] = second - first
    return out


def kernel(
    adjoint_h,
    load_h,
    displace_h,
    damage_h,
    history_h,
    frozen_h,
    order_h,
    forward_h,
    back_h,
    swap_h,
    out_ref,
    adjoint_b,
    load_b,
    displace_b,
    damage_b,
    history_b,
    frozen_b,
    order_b,
    forward,
    back,
    swap,
    value,
    kept,
    load,
    summed,
    state,
    keep,
    ys,
    zs,
    xr,
    yr,
    xyr,
    zer,
    zlr,
    zero,
    in_sem,
    send_sem,
    recv_sem,
):
    weights, derivative = gll_tables()
    px, py, pz = (lax.axis_index("gx"), lax.axis_index("gy"), lax.axis_index("gz"))
    sizes = (lax.axis_size("gx"), lax.axis_size("gy"), lax.axis_size("gz"))

    pairs = (
        (order_h, order_b),
        (adjoint_h, adjoint_b),
        (swap_h, swap),
        (displace_h, displace_b),
        (forward_h, forward),
        (damage_h, damage_b),
        (history_h, history_b),
        (frozen_h, frozen_b),
        (load_h, load_b),
        (back_h, back),
    )
    copies = [pltpu.make_async_copy(src, dst, in_sem.at[n]) for n, (src, dst) in enumerate(pairs)]
    for copy in copies[:3]:
        copy.start()

    along = [
        {
            -1: lax.rem(p + n - 1, n),
            0: p,
            1: lax.rem(p + 1, n),
        }
        for p, n in zip((px, py, pz), sizes)
    ]

    def target(d):
        return tuple(along[axis][d[axis]] for axis in range(3))

    has = [{-1: p > 0, 1: p < n - 1} for p, n in zip((px, py, pz), sizes)]
    present = [{s: side[s].astype(F32) for s in (-1, 1)} for side in has]

    def there(d):
        sides = [has[axis][d[axis]] for axis in range(3) if d[axis] != 0]
        found = sides[0]
        for side in sides[1:]:
            found = jnp.logical_and(found, side)
        return found

    to_there = {d: there(d) for d in DIRS}

    def from_there(d):
        return to_there[(-d[0], -d[1], -d[2])]

    barrier = pltpu.get_barrier_semaphore()
    for d in sorted(DIRS, key=lambda d: -abs(d[0]) - abs(d[1]) - abs(d[2])):

        @pl.when(to_there[d])
        def _(d=d):
            pl.semaphore_signal(barrier, inc=1, device_id=target(d), device_id_type=MESH)

    around = [1 + side[-1].astype(jnp.int32) + side[1].astype(jnp.int32) for side in has]
    neighbours = around[0] * around[1] * around[2] - 1
    for copy in copies[3:]:
        copy.start()

    lane = lax.broadcasted_iota(jnp.int32, (8, 128), 1)
    sub = lax.broadcasted_iota(jnp.int32, (8, 128), 0)
    lane_k = lane % 8
    lane_j = (lane // 8) % 8
    lane_h = lane // 64

    def fmask(condition):
        return jnp.where(condition, 1.0, 0.0).astype(F32)

    j_end = {-1: fmask(lane_j == 0), 1: fmask(lane_j == 7)}
    h_end = {-1: fmask(lane_h == 0), 1: fmask(lane_h == 1)}
    first_z = (lane_h == 0) & (lane_k == 0)
    last_z = (lane_h == 1) & (lane_k == 7)
    z_end = {-1: fmask(first_z), 1: fmask(last_z)}
    inner_z = ((lane_h == 0) & (lane_k == 7)) | ((lane_h == 1) & (lane_k == 0))
    z_here = fmask(inner_z | (last_z & (sub < 7)))
    z_next = fmask(first_z & (sub > 0))

    copies[0].wait()
    row_id = lax.broadcasted_iota(jnp.int32, (64, 64), 0)
    tile_id = (row_id // 8) % 4
    row_ey = (tile_id + 3) % 4
    place = row_ey * 16 + 2 * (row_id % 8) + row_id // 32
    chosen = fmask(place == order_b[...])
    pick = chosen.astype(BF16)

    def to_tiles(fields):
        sides = []
        for stored in fields:
            rows = jnp.dot(pick, stored, preferred_element_type=F32).astype(BF16)
            for n in range(0, 512, 128):
                sides.append(jnp.concatenate([rows[:32, n : n + 128], rows[32:, n : n + 128]], axis=1))
        tiles = jnp.dot(
            jnp.concatenate(sides, axis=0), swap[...], preferred_element_type=F32
        )
        return tiles.reshape(len(fields) * 4, 32, 256)

    def put_fields(tiles, ref, fields):
        for f in range(fields):
            for a in range(4):
                for half in range(2):
                    rows = slice(half * 64 + f * 16, half * 64 + f * 16 + 16)
                    both = tiles[4 * f + a, half * 16 : half * 16 + 16, :]
                    ref[2 * a, rows, :] = both[:, :128]
                    ref[2 * a + 1, rows, :] = both[:, 128:]

    def put_single(tiles, n):
        for a in range(4):
            keep[n, 2 * a] = tiles[a, :, :128]
            keep[n, 2 * a + 1] = tiles[a, :, 128:]

    def group(ref, half):
        return ref[:, half * 64 : half * 64 + 64, :].reshape(8, 4, 16, 128)

    def put_group(ref, half, block):
        ref[:, half * 64 : half * 64 + 64, :] = block.reshape(8, 64, 128)

    def sum_z(half, first, last):
        rows = slice(64 * half, 64 * half + 64)
        flat = summed[first:last, rows, :].reshape(-1, 8, 128)
        taken = lane_swap(jnp.where(first_z, pltpu.roll(flat, 7, 1), flat), 71)
        total = flat + z_here * taken + z_next * pltpu.roll(taken, 1, 1)
        summed[first:last, rows, :] = total.reshape(last - first, 64, 128)

    def sum_y(e, spans):
        for first, last in spans:
            for f in range(4):
                lower = slice(START[e] + f * 16, START[e] + f * 16 + 8)
                upper = slice(START[e + 1] + f * 16, START[e + 1] + f * 16 + 8)
                here, beyond = summed[first:last, lower, :], summed[first:last, upper, :]
                taken = lane_swap(jnp.where(lane_j == 7, here, beyond), 56)
                summed[first:last, lower, :] = here + j_end[1] * taken
                summed[first:last, upper, :] = beyond + j_end[-1] * taken

    def mask_of(half, tile, j):
        return fmask((lane_k % 2 == half) & (sub % 2 == tile) & (lane_j == j))

    packed_y = []
    for ey in range(3):
        half, tile = (START[ey] // 64, (START[ey] // 8) % 2)
        half_up, tile_up = (START[ey + 1] // 64, (START[ey + 1] // 8) % 2)
        packed_y += [
            (mask_of(half, tile, 7), tile - tile_up, 56 + half - half_up),
            (mask_of(half_up, tile_up, 0), tile_up - tile, half_up - half - 56),
        ]

    def packed_sum_y(face):
        total = face
        for wanted, tiles, lanes in packed_y:
            total = total + wanted * lane_roll(pltpu.roll(face, tiles % 8, 0), lanes)
        return total

    def pack_z(r):
        for n, (row, h, k) in enumerate(((0, 0, 0), (7, 1, 7))):
            packed = jnp.zeros((8, 128), F32)
            for slot in range(16):
                i, half = slot // 2, slot % 2
                piece = summed[i, pl.ds(half * 64 + row, 8, stride=8), :]
                moved = lane_roll(piece, (slot // 8 - h) * 64 + slot % 8 - k)
                packed = jnp.where((lane_h == slot // 8) & (lane_k == slot % 8), moved, packed)
            zs[r, n] = packed_sum_y(packed)

    def pack_y(r):
        for n, (ey, j) in enumerate(((0, 0), (3, 7))):
            for g in range(4):
                packed = jnp.zeros((8, 128), F32)
                for slot in range(8):
                    row = (slot // 2) * 16 + START[ey]
                    piece = summed[2 * g + slot % 2, row : row + 8, :]
                    packed = jnp.where(lane_j == slot, lane_roll(piece, 8 * (slot - j)), packed)
                ys[r, n, 8 * g : 8 * g + 8] = packed

    def slot_of(r, g, d):
        n = GROUPS[g].index(d)
        return (xr.at[r, 0], xr.at[r, 1], yr.at[r], xyr.at[r], zer.at[r], zlr.at[r])[g].at[n]

    def message(r, g, d):
        dx, dy, dz = d
        if g < 2:
            src = summed.at[7 if dx > 0 else 0, pl.ds(64 * g, 64)]
        elif g == 2:
            src = ys.at[r, (dy + 1) // 2]
        elif g == 3:
            src = ys.at[r, (dy + 1) // 2, pl.ds(24 if dx > 0 else 0, 8)]
        else:
            src = zs.at[r, (dz + 1) // 2]
        n = sum(len(dirs) for dirs in GROUPS[:g]) + GROUPS[g].index(d)
        return pltpu.make_async_remote_copy(
            src_ref=src,
            dst_ref=slot_of(r, g, d),
            send_sem=send_sem.at[r, n],
            recv_sem=recv_sem.at[r, g],
            device_id=target(d),
            device_id_type=MESH,
        )

    def send(r, g, dirs=None):
        for d in dirs or GROUPS[g]:
            pl.when(to_there[d])(message(r, g, d).start)

    def fill_absent(r):
        for g in range(6):
            source = zero if g < 2 else zero.at[pl.ds(0, 32)] if g == 2 else zero.at[pl.ds(0, 8)]
            for d in GROUPS[g]:
                slot = slot_of(r, g, d)
                copy = pltpu.make_async_copy(source, slot, recv_sem.at[r, g])
                pl.when(jnp.logical_not(from_there(d)))(copy.start)

    def finish(r):
        for g in range(6):
            for d in GROUPS[g]:
                pl.when(to_there[d])(message(r, g, d).wait_send)

    def arrive(r, g):
        slots = (xr.at[r, 0], xr.at[r, 1], yr.at[r], xyr.at[r], zer.at[r], zlr.at[r])[g]
        pltpu.make_async_copy(slots, slots, recv_sem.at[r, g]).wait()

    def z_faces(slots, dirs):
        faces = []
        for dz in (-1, 1):
            face = None
            for n, d in enumerate(dirs):
                if d[2] != dz:
                    continue
                part = slots[n]
                dx, dy, _ = d
                wanted = None
                if dx != 0:
                    near = (lane_k < 2) if dx > 0 else (lane_k >= 6)
                    wanted = h_end[-dx] * fmask(near)
                if dy != 0:
                    mine = mask_of(0, 1 if dy > 0 else 0, 0 if dy > 0 else 7)
                    wanted = mine if wanted is None else wanted * mine
                    part = pltpu.roll(part, dy % 8, 0)
                part = lane_roll(part, -70 * dx - 56 * dy)
                if wanted is not None:
                    part = part * wanted
                face = part if face is None else face + part
            faces.append(face)
        return faces

    def add_z(faces, half):
        for dz, face in zip((-1, 1), faces):
            row, h, k = (0, 0, 0) if dz > 0 else (7, 1, 7)
            for i in range(8):
                slot = 2 * i + half
                where = pl.ds(half * 64 + row, 8, stride=8)
                moved = lane_roll(face, (h - slot // 8) * 64 + k - slot % 8)
                value[i, where, :] = value[i, where, :] + moved * z_end[-dz]

    def take_x(r, half):
        rows = slice(64 * half, 64 * half + 64)
        for n, d in enumerate(X_DIRS):
            i = 0 if d[0] > 0 else 7
            value[i, rows, :] = value[i, rows, :] + xr[r, half, n]

    def receive_early(r):
        arrive(r, 4)
        faces = z_faces(zer.at[r], Z_EARLY)
        arrive(r, 1)
        take_x(r, 1)
        add_z(faces, 1)
        return faces

    def receive_late(r, faces):
        take_x(r, 0)
        for n, d in enumerate(Y_DIRS):
            dy = d[1]
            sides = [yr[r, n, 8 * g : 8 * g + 8] for g in range(4)]
            for dx in (-1, 1):
                edge = lane_roll(xyr[r, XY_DIRS.index((dx, dy, 0))], -8 * dx)
                g = 0 if dx > 0 else 3
                sides[g] = sides[g] + edge * fmask(lane_j % 2 == (0 if dx > 0 else 1))
            ey, j = (0, 0) if dy > 0 else (3, 7)
            for i in range(8):
                for f in range(4):
                    row = f * 16 + START[ey]
                    moved = lane_roll(sides[i // 2], 8 * (j - f * 2 - i % 2))
                    value[i, row : row + 8, :] = value[i, row : row + 8, :] + moved * j_end[-dy]
        late = z_faces(zlr.at[r], Z_LATE)
        add_z([face + more for face, more in zip(faces, late)], 0)

    def brick():
        line_j = jnp.zeros((8, 128), F32)
        line_k = jnp.zeros((8, 128), F32)
        for n in range(8):
            line_j = jnp.where(lane_j == n, float(weights[n]), line_j)
            line_k = jnp.where(lane_k == n, float(weights[n]), line_k)
        plane = (line_j * line_k)[:1]
        return jnp.stack([plane * float(weights[n]) for n in range(8)])

    def gradients(block, exact):
        if exact:
            high = block.reshape(-1, 128).astype(BF16)
            left, table = jnp.concatenate([high, high], axis=1), forward[128:384, :]
        else:
            high, low = split(block.reshape(-1, 128))
            left, table = jnp.concatenate([high, low, high], axis=1), forward[...]
        yz = jnp.dot(left, table, preferred_element_type=F32)
        gx = jnp.stack(x_derivative([block[i] for i in range(8)], derivative))
        return gx, yz[:, :128].reshape(block.shape), yz[:, 128:].reshape(block.shape)

    def state_terms(half):
        rows = slice(16 * half, 16 * half + 16)
        moved = group(kept, half)[:, :3]
        gx, gy, gz = gradients(moved, True)
        shear = [gy[:, 0] + gx[:, 1], gz[:, 0] + gx[:, 2], gz[:, 1] + gy[:, 2]]
        normal = [gx[:, 0], gy[:, 1], gz[:, 2]]
        trace_sum = normal[0] + normal[1] + normal[2]
        stress = [lame_lambda * trace_sum + 2.0 * lame_mu * n for n in normal]
        stress += [lame_mu * s for s in shear]
        energy = stress[0] * normal[0] + stress[1] * normal[1] + stress[2] * normal[2]
        energy = 0.5 * (energy + stress[3] * shear[0] + stress[4] * shear[1] + stress[5] * shear[2])
        loading = keep[2, 0, rows, :][None]
        driving = (1.0 - loading) * keep[1, :, rows, :] + loading * energy
        intact = 1.0 - keep[0, :, rows, :]
        mass = brick()
        slope = -2.0 * intact * mass
        for n in range(6):
            state[n, :, rows, :] = slope * stress[n]
        state[6, :, rows, :] = lame_mu * mass * (intact * intact + residual_stiff)
        state[7, :, rows, :] = mass * (gc_inverse + 2.0 * driving)

    def forward_tile(half, tile, block):
        rows = slice(16 * half + 8 * tile, 16 * half + 8 * tile + 8)
        gx, gy, gz = gradients(block, False)
        scaled = [state[n, :, rows, :] for n in range(6)]
        stiff = state[6, :, rows, :]
        vd = block[:, 3]
        coupled = keep[2, 0, rows, :][None] * vd
        shear = [gy[:, 0] + gx[:, 1], gz[:, 0] + gx[:, 2], gz[:, 1] + gy[:, 2]]
        normal = [gx[:, 0], gy[:, 1], gz[:, 2]]
        trace_sum = 1.5 * (normal[0] + normal[1] + normal[2])
        tensor = [stiff * (trace_sum + 2.0 * normal[n]) + scaled[n] * coupled for n in range(3)]
        tensor += [stiff * shear[n] + scaled[n + 3] * coupled for n in range(3)]
        nodal = state[7, :, rows, :] * vd
        for n in range(3):
            nodal = nodal + scaled[n] * normal[n] + scaled[n + 3] * shear[n]
        flux = gc_length * brick()
        along_x = jnp.stack([tensor[0], tensor[3], tensor[4], flux * gx[:, 3]], axis=1)
        along_y = jnp.stack([tensor[3], tensor[1], tensor[5], flux * gy[:, 3]], axis=1)
        along_z = jnp.stack([tensor[4], tensor[5], tensor[2], flux * gz[:, 3]], axis=1)
        y_high, y_low = split(along_y.reshape(-1, 128))
        z_high, z_low = split(along_z.reshape(-1, 128))
        return along_x, (y_high, y_low, z_high, z_low), nodal

    def backward_tile(half, tile, pieces):
        along_x, (y_high, y_low, z_high, z_low), nodal = pieces
        one = jnp.dot(
            jnp.concatenate([y_high, z_high], axis=1), back[...], preferred_element_type=F32
        )
        two = jnp.dot(
            jnp.concatenate([y_low, z_low], axis=1), back[:, :128], preferred_element_type=F32
        )
        total = (one[:, :128] + one[:, 128:] + two).reshape(along_x.shape)
        total = total + jnp.stack(x_derivative([along_x[i] for i in range(8)], derivative.T))
        result = group(load, half)[:, :, 8 * tile : 8 * tile + 8] - total
        return jnp.concatenate([result[:, :3], (result[:, 3] - nodal)[:, None]], axis=1)

    def forward_half(half, block):
        return [forward_tile(half, n, block[:, :, 8 * n : 8 * n + 8]) for n in range(2)]

    def backward_half(half, pieces):
        parts = [backward_tile(half, n, pieces[n]) for n in range(2)]
        put_group(summed, half, jnp.concatenate(parts, axis=2))

    def ship(r):
        pack_z(r)
        for half in range(2):
            sum_z(half, 0, 1)
            sum_z(half, 7, 8)
        for e in range(3):
            sum_y(e, ((0, 1), (7, 8)))
        if r == 0:
            pl.semaphore_wait(barrier, neighbours)
        for d in Z_ORDER[:8]:
            send(r, 5, [d])
        send(r, 1)
        for d in Z_ORDER[8:]:
            send(r, 4 if d in Z_EARLY else 5, [d])
        for half in range(2):
            sum_z(half, 1, 7)
        pack_y(r)
        send(r, 3)
        send(r, 2)
        send(r, 0)
        for e in range(3):
            sum_y(e, ((1, 7),))
        value[...] = summed[...]

    copies[1].wait()
    copies[2].wait()
    put_fields(to_tiles([adjoint_b[f] for f in range(4)]), summed, 4)
    ship(0)

    zero[...] = jnp.zeros((64, 128), F32)
    fill_absent(0)

    copies[3].wait()
    copies[4].wait()
    copies[5].wait()
    copies[6].wait()
    tiles = to_tiles([displace_b[0], displace_b[1], displace_b[2], damage_b[...], history_b[...]])
    put_fields(tiles, kept, 3)
    put_single(tiles[12:16], 0)
    put_single(tiles[16:20], 1)
    copies[7].wait()
    frozen = 1.0 - jnp.sum(chosen * frozen_b[...].astype(F32), axis=1, keepdims=True)
    low_half = lax.broadcasted_iota(jnp.int32, (32, 128), 1) < 64
    keep[2, 0] = jnp.where(low_half, frozen[:32], frozen[32:])
    for half in range(2):
        state_terms(half)
    copies[8].wait()
    put_fields(to_tiles([load_b[f] for f in range(4)]), load, 4)
    copies[9].wait()

    def halved(condition, scalar):
        return 1.0 - 0.5 * fmask(condition) * scalar

    inv_z = halved(inner_z, 1.0) * halved(first_z & (sub > 0), 1.0) * halved(last_z & (sub < 7), 1.0)
    inv_z = inv_z * halved(first_z & (sub == 0), present[2][-1]) * halved(last_z & (sub == 7), present[2][1])

    def average(half):
        planes = []
        for ey in EY[half]:
            lower = 1.0 if ey > 0 else present[1][-1]
            upper = 1.0 if ey < 3 else present[1][1]
            planes.append(inv_z * halved(lane_j == 0, lower) * halved(lane_j == 7, upper))
        scale = jnp.concatenate(planes, axis=0)
        scales = [scale] * 8
        scales[0] = scale * (1.0 - 0.5 * present[0][-1])
        scales[7] = scale * (1.0 - 0.5 * present[0][1])
        block = group(value, half) * jnp.stack(scales)[:, None]
        put_group(kept, half, block)
        return block

    def relax(half):
        return group(kept, half) + relaxation * group(value, half)

    fill_absent(1)
    fill_absent(2)

    for r, ready in ((0, average), (1, relax)):
        finish(r)
        faces = receive_early(r)
        pieces = forward_half(1, ready(1))
        for g in (0, 2, 3, 5):
            arrive(r, g)
        receive_late(r, faces)
        backward_half(1, pieces)
        backward_half(0, forward_half(0, ready(0)))
        ship(r + 1)

    def emit(half):
        block = value[:, 64 * half : 64 * half + 64, :].reshape(4, 2, 4, 16, 128)
        sides = jnp.concatenate([block[:, 0], block[:, 1]], axis=3).reshape(256, 256)
        high, low = split(sides)
        moved = jnp.dot(
            jnp.concatenate([high, low], axis=0), swap[...], preferred_element_type=F32
        ).astype(BF16)
        rows = jnp.concatenate([chosen[16 * half : 16 * half + 16], chosen[32 + 16 * half : 48 + 16 * half]], axis=0)
        unpick = jnp.concatenate([rows, rows], axis=0).T.astype(BF16)
        for f in range(4):
            columns = []
            for a in range(4):
                parts = []
                for n in (a * 64 + f * 16, 256 + a * 64 + f * 16):
                    parts += [moved[n : n + 16, :128], moved[n : n + 16, 128:]]
                columns.append(jnp.concatenate(parts, axis=0))
            stacked = jnp.concatenate(columns, axis=1)
            out = jnp.dot(unpick, stacked, preferred_element_type=F32)
            out_ref[f] = out if half == 1 else out_ref[f] + out

    finish(2)
    faces = receive_early(2)
    emit(1)
    for g in (0, 2, 3, 5):
        arrive(2, g)
    receive_late(2, faces)
    emit(0)


def shards(adjoint, load, displace, damage, history, frozen, order):
    forward, back, swap = (jnp.asarray(c) for c in constants())
    hbm = pl.BlockSpec(memory_space=pltpu.HBM)
    return pl.pallas_call(
        kernel,
        out_shape=pltpu.VMEM((4, 64, 512), F32),
        in_specs=[hbm] * 10,
        out_specs=pl.BlockSpec(memory_space=pltpu.VMEM),
        scratch_shapes=[
            pltpu.VMEM((4, 64, 512), BF16),
            pltpu.VMEM((4, 64, 512), BF16),
            pltpu.VMEM((3, 64, 512), BF16),
            pltpu.VMEM((64, 512), BF16),
            pltpu.VMEM((64, 512), BF16),
            pltpu.VMEM((1, 64), jnp.int32),
            pltpu.VMEM((1, 64), jnp.int32),
            pltpu.VMEM((384, 256), BF16),
            pltpu.VMEM((256, 256), BF16),
            pltpu.VMEM((256, 256), BF16),
            pltpu.VMEM((8, 128, 128), F32),
            pltpu.VMEM((8, 128, 128), F32),
            pltpu.VMEM((8, 128, 128), F32),
            pltpu.VMEM((8, 128, 128), F32),
            pltpu.VMEM((8, 8, 32, 128), F32),
            pltpu.VMEM((3, 8, 32, 128), F32),
            pltpu.VMEM((3, 2, 32, 128), F32),
            pltpu.VMEM((3, 2, 8, 128), F32),
            pltpu.VMEM((3, 2, 2, 64, 128), F32),
            pltpu.VMEM((3, 2, 32, 128), F32),
            pltpu.VMEM((3, 4, 8, 128), F32),
            pltpu.VMEM((3, 6, 8, 128), F32),
            pltpu.VMEM((3, 12, 8, 128), F32),
            pltpu.VMEM((64, 128), F32),
            pltpu.SemaphoreType.DMA((10,)),
            pltpu.SemaphoreType.DMA((3, 28)),
            pltpu.SemaphoreType.DMA((3, 6)),
        ],
        compiler_params=pltpu.CompilerParams(
            collective_id=0, has_side_effects=True, vmem_limit_bytes=56 * 1024 * 1024
        ),
    )(adjoint, load, displace, damage, history, frozen.reshape(1, 64), order, forward, back, swap)


def solution(mesh):
    in_specs = (
        P(None, ("gx", "gy", "gz"), None),
        P(None, ("gx", "gy", "gz"), None),
        P(None, ("gx", "gy", "gz"), None),
        P(("gx", "gy", "gz"), None),
        P(("gx", "gy", "gz"), None),
        P(("gx", "gy", "gz")),
        P(("gx", "gy", "gz"), None),
    )
    out_specs = P(None, ("gx", "gy", "gz"), None)
    return jax.shard_map(shards, mesh=mesh, in_specs=in_specs, out_specs=out_specs, check_vma=False)
```

```python
import jax
import jax.numpy as jnp
import ml_dtypes
import numpy as np
from jax import lax
from jax.experimental import pallas as pl
from jax.experimental.pallas import tpu as pltpu
from jax.sharding import PartitionSpec as P

F32 = jnp.float32
BF16 = jnp.bfloat16
MESH = pl.DeviceIdType.MESH

lame_lambda = 0.15
lame_mu = 0.1
gc_length = 0.3
gc_inverse = 40.0
residual_stiff = 0.001
relaxation = 0.5
gll_points = (
    -1.0,
    -0.8717401485096066,
    -0.5917001814331423,
    -0.2092992179024789,
    0.2092992179024789,
    0.5917001814331423,
    0.8717401485096066,
    1.0,
)

EY = ((3, 0), (1, 2))
START = {ey: 64 * half + 8 * tile for half in range(2) for tile, ey in enumerate(EY[half])}

DIRS = [
    (dx, dy, dz)
    for dx in (-1, 0, 1)
    for dy in (-1, 0, 1)
    for dz in (-1, 0, 1)
    if (dx, dy, dz) != (0, 0, 0)
]
X_DIRS = [d for d in DIRS if d[1] == 0 and d[2] == 0]
Y_DIRS = [d for d in DIRS if d[0] == 0 and d[1] != 0 and d[2] == 0]
XY_DIRS = [d for d in DIRS if d[0] != 0 and d[1] != 0 and d[2] == 0]
Z_DIRS = [d for d in DIRS if d[2] != 0]
Z_LATE = [d for d in Z_DIRS if d[1] != 0]
Z_EARLY = [d for d in Z_DIRS if d[1] == 0]
Z_ORDER = sorted(Z_DIRS, key=lambda d: -abs(d[0]) - abs(d[1]))
GROUPS = (X_DIRS, X_DIRS, Y_DIRS, XY_DIRS, Z_EARLY, Z_LATE)


def legendre_at(points, degree):
    values = []
    for point in points:
        previous = 1.0
        current = point
        for level in range(1, degree):
            following = ((2 * level + 1) * point * current - level * previous) / (level + 1)
            previous = current
            current = following
        values.append(current)
    return values


def gll_tables():
    degree = 7
    points = list(gll_points)
    legendre_vals = legendre_at(points, degree)
    weights = [2.0 / (degree * (degree + 1) * entry * entry) for entry in legendre_vals]
    derivative = []
    for row_index in range(degree + 1):
        row_vals = []
        for col_index in range(degree + 1):
            if row_index != col_index:
                row_vals.append(
                    legendre_vals[row_index]
                    / (legendre_vals[col_index] * (points[row_index] - points[col_index]))
                )
            else:
                row_vals.append(0.0)
        derivative.append(row_vals)
    derivative[0][0] = -degree * (degree + 1) / 4.0
    derivative[degree][degree] = degree * (degree + 1) / 4.0
    return (np.array(weights), np.array(derivative))


def split_np(matrix):
    high = matrix.astype(np.float32).astype(ml_dtypes.bfloat16)
    low = (matrix - high.astype(np.float64)).astype(np.float32).astype(ml_dtypes.bfloat16)
    return high, low


def constants():
    _, derivative = gll_tables()
    eye = np.eye
    forward_y = np.kron(eye(2), np.kron(derivative.T, eye(8)))
    forward_z = np.kron(eye(16), derivative.T)
    back_y = np.kron(eye(2), np.kron(derivative, eye(8)))
    back_z = np.kron(eye(16), derivative)
    f_high, f_low = split_np(np.concatenate([forward_y, forward_z], axis=1))
    forward = np.concatenate([f_high, f_high, f_low], axis=0)
    b_high, b_low = split_np(np.concatenate([back_y, back_z], axis=0))
    back = np.concatenate([b_high, b_low], axis=1)
    swap = np.zeros((2, 2, 64, 2, 2, 64))
    for h in range(2):
        for odd in range(2):
            swap[h, odd, :, odd, h, :] = eye(64)
    swap = swap.reshape(256, 256).astype(ml_dtypes.bfloat16)
    return forward, back, swap


def lane_roll(value, shift):
    shift = shift % 128
    if shift == 0:
        return value
    flat = value.reshape(-1, 128)
    return pltpu.roll(flat, shift, 1).reshape(value.shape)


def lane_swap(value, mask):
    flat = value.reshape(-1, 128)
    index = jnp.bitwise_xor(lax.broadcasted_iota(jnp.int32, flat.shape, 1), mask)
    return jnp.take_along_axis(flat, index, axis=1).reshape(value.shape)


def split(value):
    high = value.astype(BF16)
    low = (value - high.astype(F32)).astype(BF16)
    return high, low


def x_derivative(tiles, matrix):
    even_part = (matrix + matrix[:, ::-1]) / 2
    odd_part = (matrix - matrix[:, ::-1]) / 2
    even = [tiles[n] + tiles[7 - n] for n in range(4)]
    odd = [tiles[n] - tiles[7 - n] for n in range(4)]
    out = [None] * 8
    for n in range(4):
        first = float(even_part[n, 0]) * even[0]
        second = float(odd_part[n, 0]) * odd[0]
        for m in range(1, 4):
            first = first + float(even_part[n, m]) * even[m]
            second = second + float(odd_part[n, m]) * odd[m]
        out[n] = second + first
        out[7 - n] = second - first
    return out


def kernel(
    adjoint_h,
    load_h,
    displace_h,
    damage_h,
    history_h,
    frozen_h,
    order_h,
    forward_h,
    back_h,
    swap_h,
    out_ref,
    adjoint_b,
    load_b,
    displace_b,
    damage_b,
    history_b,
    frozen_b,
    order_b,
    forward,
    back,
    swap,
    value,
    kept,
    load,
    summed,
    state,
    keep,
    ys,
    zs,
    xr,
    yr,
    xyr,
    zer,
    zlr,
    zero,
    in_sem,
    send_sem,
    recv_sem,
):
    weights, derivative = gll_tables()
    px, py, pz = (lax.axis_index("gx"), lax.axis_index("gy"), lax.axis_index("gz"))
    sizes = (lax.axis_size("gx"), lax.axis_size("gy"), lax.axis_size("gz"))

    pairs = (
        (order_h, order_b),
        (adjoint_h, adjoint_b),
        (swap_h, swap),
        (displace_h, displace_b),
        (forward_h, forward),
        (damage_h, damage_b),
        (history_h, history_b),
        (frozen_h, frozen_b),
        (load_h, load_b),
        (back_h, back),
    )
    copies = [pltpu.make_async_copy(src, dst, in_sem.at[n]) for n, (src, dst) in enumerate(pairs)]
    for copy in copies[:3]:
        copy.start()

    along = [
        {
            -1: lax.rem(p + n - 1, n),
            0: p,
            1: lax.rem(p + 1, n),
        }
        for p, n in zip((px, py, pz), sizes)
    ]

    def target(d):
        return tuple(along[axis][d[axis]] for axis in range(3))

    has = [{-1: p > 0, 1: p < n - 1} for p, n in zip((px, py, pz), sizes)]
    present = [{s: side[s].astype(F32) for s in (-1, 1)} for side in has]

    def there(d):
        sides = [has[axis][d[axis]] for axis in range(3) if d[axis] != 0]
        found = sides[0]
        for side in sides[1:]:
            found = jnp.logical_and(found, side)
        return found

    to_there = {d: there(d) for d in DIRS}

    def from_there(d):
        return to_there[(-d[0], -d[1], -d[2])]

    barrier = pltpu.get_barrier_semaphore()
    for d in sorted(DIRS, key=lambda d: -abs(d[0]) - abs(d[1]) - abs(d[2])):

        @pl.when(to_there[d])
        def _(d=d):
            pl.semaphore_signal(barrier, inc=1, device_id=target(d), device_id_type=MESH)

    around = [1 + side[-1].astype(jnp.int32) + side[1].astype(jnp.int32) for side in has]
    neighbours = around[0] * around[1] * around[2] - 1
    for copy in copies[3:]:
        copy.start()

    lane = lax.broadcasted_iota(jnp.int32, (8, 128), 1)
    sub = lax.broadcasted_iota(jnp.int32, (8, 128), 0)
    lane_k = lane % 8
    lane_j = (lane // 8) % 8
    lane_h = lane // 64

    def fmask(condition):
        return jnp.where(condition, 1.0, 0.0).astype(F32)

    j_end = {-1: fmask(lane_j == 0), 1: fmask(lane_j == 7)}
    h_end = {-1: fmask(lane_h == 0), 1: fmask(lane_h == 1)}
    first_z = (lane_h == 0) & (lane_k == 0)
    last_z = (lane_h == 1) & (lane_k == 7)
    z_end = {-1: fmask(first_z), 1: fmask(last_z)}
    inner_z = ((lane_h == 0) & (lane_k == 7)) | ((lane_h == 1) & (lane_k == 0))
    z_here = fmask(inner_z | (last_z & (sub < 7)))
    z_next = fmask(first_z & (sub > 0))

    copies[0].wait()
    row_id = lax.broadcasted_iota(jnp.int32, (64, 64), 0)
    tile_id = (row_id // 8) % 4
    row_ey = (tile_id + 3) % 4
    place = row_ey * 16 + 2 * (row_id % 8) + row_id // 32
    chosen = fmask(place == order_b[...])
    pick = chosen.astype(BF16)

    def to_tiles(fields):
        sides = []
        for stored in fields:
            rows = jnp.dot(pick, stored, preferred_element_type=F32).astype(BF16)
            for n in range(0, 512, 128):
                sides.append(jnp.concatenate([rows[:32, n : n + 128], rows[32:, n : n + 128]], axis=1))
        tiles = jnp.dot(
            jnp.concatenate(sides, axis=0), swap[...], preferred_element_type=F32
        )
        return tiles.reshape(len(fields) * 4, 32, 256)

    def put_fields(tiles, ref, fields):
        for f in range(fields):
            for a in range(4):
                for half in range(2):
                    rows = slice(half * 64 + f * 16, half * 64 + f * 16 + 16)
                    both = tiles[4 * f + a, half * 16 : half * 16 + 16, :]
                    ref[2 * a, rows, :] = both[:, :128]
                    ref[2 * a + 1, rows, :] = both[:, 128:]

    def put_single(tiles, n):
        for a in range(4):
            keep[n, 2 * a] = tiles[a, :, :128]
            keep[n, 2 * a + 1] = tiles[a, :, 128:]

    def group(ref, half):
        return ref[:, half * 64 : half * 64 + 64, :].reshape(8, 4, 16, 128)

    def put_group(ref, half, block):
        ref[:, half * 64 : half * 64 + 64, :] = block.reshape(8, 64, 128)

    def sum_z(half, first, last):
        rows = slice(64 * half, 64 * half + 64)
        flat = summed[first:last, rows, :].reshape(-1, 8, 128)
        taken = lane_swap(jnp.where(first_z, pltpu.roll(flat, 7, 1), flat), 71)
        total = flat + z_here * taken + z_next * pltpu.roll(taken, 1, 1)
        summed[first:last, rows, :] = total.reshape(last - first, 64, 128)

    def sum_y(e, spans):
        for first, last in spans:
            for f in range(4):
                lower = slice(START[e] + f * 16, START[e] + f * 16 + 8)
                upper = slice(START[e + 1] + f * 16, START[e + 1] + f * 16 + 8)
                here, beyond = summed[first:last, lower, :], summed[first:last, upper, :]
                taken = lane_swap(jnp.where(lane_j == 7, here, beyond), 56)
                summed[first:last, lower, :] = here + j_end[1] * taken
                summed[first:last, upper, :] = beyond + j_end[-1] * taken

    def mask_of(half, tile, j):
        return fmask((lane_k % 2 == half) & (sub % 2 == tile) & (lane_j == j))

    packed_y = []
    for ey in range(3):
        half, tile = (START[ey] // 64, (START[ey] // 8) % 2)
        half_up, tile_up = (START[ey + 1] // 64, (START[ey + 1] // 8) % 2)
        packed_y += [
            (mask_of(half, tile, 7), tile - tile_up, 56 + half - half_up),
            (mask_of(half_up, tile_up, 0), tile_up - tile, half_up - half - 56),
        ]

    def packed_sum_y(face):
        total = face
        for wanted, tiles, lanes in packed_y:
            total = total + wanted * lane_roll(pltpu.roll(face, tiles % 8, 0), lanes)
        return total

    def pack_z(r):
        for n, (row, h, k) in enumerate(((0, 0, 0), (7, 1, 7))):
            packed = jnp.zeros((8, 128), F32)
            for slot in range(16):
                i, half = slot // 2, slot % 2
                piece = summed[i, pl.ds(half * 64 + row, 8, stride=8), :]
                moved = lane_roll(piece, (slot // 8 - h) * 64 + slot % 8 - k)
                packed = jnp.where((lane_h == slot // 8) & (lane_k == slot % 8), moved, packed)
            zs[r, n] = packed_sum_y(packed)

    def pack_y(r):
        for n, (ey, j) in enumerate(((0, 0), (3, 7))):
            for g in range(4):
                packed = jnp.zeros((8, 128), F32)
                for slot in range(8):
                    row = (slot // 2) * 16 + START[ey]
                    piece = summed[2 * g + slot % 2, row : row + 8, :]
                    packed = jnp.where(lane_j == slot, lane_roll(piece, 8 * (slot - j)), packed)
                ys[r, n, 8 * g : 8 * g + 8] = packed

    def slot_of(r, g, d):
        n = GROUPS[g].index(d)
        return (xr.at[r, 0], xr.at[r, 1], yr.at[r], xyr.at[r], zer.at[r], zlr.at[r])[g].at[n]

    def message(r, g, d):
        dx, dy, dz = d
        if g < 2:
            src = summed.at[7 if dx > 0 else 0, pl.ds(64 * g, 64)]
        elif g == 2:
            src = ys.at[r, (dy + 1) // 2]
        elif g == 3:
            src = ys.at[r, (dy + 1) // 2, pl.ds(24 if dx > 0 else 0, 8)]
        else:
            src = zs.at[r, (dz + 1) // 2]
        n = sum(len(dirs) for dirs in GROUPS[:g]) + GROUPS[g].index(d)
        return pltpu.make_async_remote_copy(
            src_ref=src,
            dst_ref=slot_of(r, g, d),
            send_sem=send_sem.at[r, n],
            recv_sem=recv_sem.at[r, g],
            device_id=target(d),
            device_id_type=MESH,
        )

    def send(r, g, dirs=None):
        for d in dirs or GROUPS[g]:
            pl.when(to_there[d])(message(r, g, d).start)

    def fill_absent(r):
        for g in range(6):
            source = zero if g < 2 else zero.at[pl.ds(0, 32)] if g == 2 else zero.at[pl.ds(0, 8)]
            for d in GROUPS[g]:
                slot = slot_of(r, g, d)
                copy = pltpu.make_async_copy(source, slot, recv_sem.at[r, g])
                pl.when(jnp.logical_not(from_there(d)))(copy.start)

    def finish(r):
        for g in range(6):
            for d in GROUPS[g]:
                pl.when(to_there[d])(message(r, g, d).wait_send)

    def arrive(r, g):
        slots = (xr.at[r, 0], xr.at[r, 1], yr.at[r], xyr.at[r], zer.at[r], zlr.at[r])[g]
        pltpu.make_async_copy(slots, slots, recv_sem.at[r, g]).wait()

    def z_faces(slots, dirs):
        faces = []
        for dz in (-1, 1):
            face = None
            for n, d in enumerate(dirs):
                if d[2] != dz:
                    continue
                part = slots[n]
                dx, dy, _ = d
                wanted = None
                if dx != 0:
                    near = (lane_k < 2) if dx > 0 else (lane_k >= 6)
                    wanted = h_end[-dx] * fmask(near)
                if dy != 0:
                    mine = mask_of(0, 1 if dy > 0 else 0, 0 if dy > 0 else 7)
                    wanted = mine if wanted is None else wanted * mine
                    part = pltpu.roll(part, dy % 8, 0)
                part = lane_roll(part, -70 * dx - 56 * dy)
                if wanted is not None:
                    part = part * wanted
                face = part if face is None else face + part
            faces.append(face)
        return faces

    def add_z(faces, half):
        for dz, face in zip((-1, 1), faces):
            row, h, k = (0, 0, 0) if dz > 0 else (7, 1, 7)
            for i in range(8):
                slot = 2 * i + half
                where = pl.ds(half * 64 + row, 8, stride=8)
                moved = lane_roll(face, (h - slot // 8) * 64 + k - slot % 8)
                value[i, where, :] = value[i, where, :] + moved * z_end[-dz]

    def take_x(r, half):
        rows = slice(64 * half, 64 * half + 64)
        for n, d in enumerate(X_DIRS):
            i = 0 if d[0] > 0 else 7
            value[i, rows, :] = value[i, rows, :] + xr[r, half, n]

    def receive_early(r):
        arrive(r, 4)
        faces = z_faces(zer.at[r], Z_EARLY)
        arrive(r, 1)
        take_x(r, 1)
        add_z(faces, 1)
        return faces

    def receive_late(r, faces):
        take_x(r, 0)
        for n, d in enumerate(Y_DIRS):
            dy = d[1]
            sides = [yr[r, n, 8 * g : 8 * g + 8] for g in range(4)]
            for dx in (-1, 1):
                edge = lane_roll(xyr[r, XY_DIRS.index((dx, dy, 0))], -8 * dx)
                g = 0 if dx > 0 else 3
                sides[g] = sides[g] + edge * fmask(lane_j % 2 == (0 if dx > 0 else 1))
            ey, j = (0, 0) if dy > 0 else (3, 7)
            for i in range(8):
                for f in range(4):
                    row = f * 16 + START[ey]
                    moved = lane_roll(sides[i // 2], 8 * (j - f * 2 - i % 2))
                    value[i, row : row + 8, :] = value[i, row : row + 8, :] + moved * j_end[-dy]
        late = z_faces(zlr.at[r], Z_LATE)
        add_z([face + more for face, more in zip(faces, late)], 0)

    def brick():
        line_j = jnp.zeros((8, 128), F32)
        line_k = jnp.zeros((8, 128), F32)
        for n in range(8):
            line_j = jnp.where(lane_j == n, float(weights[n]), line_j)
            line_k = jnp.where(lane_k == n, float(weights[n]), line_k)
        plane = (line_j * line_k)[:1]
        return jnp.stack([plane * float(weights[n]) for n in range(8)])

    def gradients(block, exact):
        if exact:
            high = block.reshape(-1, 128).astype(BF16)
            left, table = jnp.concatenate([high, high], axis=1), forward[128:384, :]
        else:
            high, low = split(block.reshape(-1, 128))
            left, table = jnp.concatenate([high, low, high], axis=1), forward[...]
        yz = jnp.dot(left, table, preferred_element_type=F32)
        gx = jnp.stack(x_derivative([block[i] for i in range(8)], derivative))
        return gx, yz[:, :128].reshape(block.shape), yz[:, 128:].reshape(block.shape)

    def state_terms(half):
        rows = slice(16 * half, 16 * half + 16)
        moved = group(kept, half)[:, :3]
        gx, gy, gz = gradients(moved, True)
        shear = [gy[:, 0] + gx[:, 1], gz[:, 0] + gx[:, 2], gz[:, 1] + gy[:, 2]]
        normal = [gx[:, 0], gy[:, 1], gz[:, 2]]
        trace_sum = normal[0] + normal[1] + normal[2]
        stress = [lame_lambda * trace_sum + 2.0 * lame_mu * n for n in normal]
        stress += [lame_mu * s for s in shear]
        energy = stress[0] * normal[0] + stress[1] * normal[1] + stress[2] * normal[2]
        energy = 0.5 * (energy + stress[3] * shear[0] + stress[4] * shear[1] + stress[5] * shear[2])
        loading = keep[2, 0, rows, :][None]
        driving = (1.0 - loading) * keep[1, :, rows, :] + loading * energy
        intact = 1.0 - keep[0, :, rows, :]
        mass = brick()
        slope = -2.0 * intact * mass
        for n in range(6):
            state[n, :, rows, :] = slope * stress[n]
        state[6, :, rows, :] = lame_mu * mass * (intact * intact + residual_stiff)
        state[7, :, rows, :] = mass * (gc_inverse + 2.0 * driving)

    def forward_tile(half, tile, block):
        rows = slice(16 * half + 8 * tile, 16 * half + 8 * tile + 8)
        gx, gy, gz = gradients(block, False)
        scaled = [state[n, :, rows, :] for n in range(6)]
        stiff = state[6, :, rows, :]
        vd = block[:, 3]
        coupled = keep[2, 0, rows, :][None] * vd
        shear = [gy[:, 0] + gx[:, 1], gz[:, 0] + gx[:, 2], gz[:, 1] + gy[:, 2]]
        normal = [gx[:, 0], gy[:, 1], gz[:, 2]]
        trace_sum = 1.5 * (normal[0] + normal[1] + normal[2])
        tensor = [stiff * (trace_sum + 2.0 * normal[n]) + scaled[n] * coupled for n in range(3)]
        tensor += [stiff * shear[n] + scaled[n + 3] * coupled for n in range(3)]
        nodal = state[7, :, rows, :] * vd
        for n in range(3):
            nodal = nodal + scaled[n] * normal[n] + scaled[n + 3] * shear[n]
        flux = gc_length * brick()
        along_x = jnp.stack([tensor[0], tensor[3], tensor[4], flux * gx[:, 3]], axis=1)
        along_y = jnp.stack([tensor[3], tensor[1], tensor[5], flux * gy[:, 3]], axis=1)
        along_z = jnp.stack([tensor[4], tensor[5], tensor[2], flux * gz[:, 3]], axis=1)
        y_high, y_low = split(along_y.reshape(-1, 128))
        z_high, z_low = split(along_z.reshape(-1, 128))
        return along_x, (y_high, y_low, z_high, z_low), nodal

    def backward_tile(half, tile, pieces):
        along_x, (y_high, y_low, z_high, z_low), nodal = pieces
        one = jnp.dot(
            jnp.concatenate([y_high, z_high], axis=1), back[...], preferred_element_type=F32
        )
        two = jnp.dot(
            jnp.concatenate([y_low, z_low], axis=1), back[:, :128], preferred_element_type=F32
        )
        total = (one[:, :128] + one[:, 128:] + two).reshape(along_x.shape)
        total = total + jnp.stack(x_derivative([along_x[i] for i in range(8)], derivative.T))
        result = group(load, half)[:, :, 8 * tile : 8 * tile + 8] - total
        return jnp.concatenate([result[:, :3], (result[:, 3] - nodal)[:, None]], axis=1)

    def forward_half(half, block):
        return [forward_tile(half, n, block[:, :, 8 * n : 8 * n + 8]) for n in range(2)]

    def backward_half(half, pieces):
        parts = [backward_tile(half, n, pieces[n]) for n in range(2)]
        put_group(summed, half, jnp.concatenate(parts, axis=2))

    def ship(r):
        pack_z(r)
        if r == 0:
            pl.semaphore_wait(barrier, neighbours)
        for d in Z_ORDER[:8]:
            send(r, 5, [d])
        for half in range(2):
            sum_z(half, 0, 1)
            sum_z(half, 7, 8)
        for e in (0, 2, 1):
            sum_y(e, ((0, 1), (7, 8)))
        send(r, 1)
        for d in Z_ORDER[8:]:
            send(r, 4 if d in Z_EARLY else 5, [d])
        for half in range(2):
            sum_z(half, 1, 7)
        pack_y(r)
        send(r, 3)
        send(r, 2)
        send(r, 0)
        for e in (0, 2, 1):
            sum_y(e, ((1, 7),))
        value[...] = summed[...]

    copies[1].wait()
    copies[2].wait()
    put_fields(to_tiles([adjoint_b[f] for f in range(4)]), summed, 4)
    ship(0)

    zero[...] = jnp.zeros((64, 128), F32)
    fill_absent(0)

    copies[3].wait()
    copies[4].wait()
    copies[5].wait()
    copies[6].wait()
    tiles = to_tiles([displace_b[0], displace_b[1], displace_b[2], damage_b[...], history_b[...]])
    put_fields(tiles, kept, 3)
    put_single(tiles[12:16], 0)
    put_single(tiles[16:20], 1)
    copies[7].wait()
    frozen = 1.0 - jnp.sum(chosen * frozen_b[...].astype(F32), axis=1, keepdims=True)
    low_half = lax.broadcasted_iota(jnp.int32, (32, 128), 1) < 64
    keep[2, 0] = jnp.where(low_half, frozen[:32], frozen[32:])
    for half in range(2):
        state_terms(half)
    copies[8].wait()
    put_fields(to_tiles([load_b[f] for f in range(4)]), load, 4)
    copies[9].wait()

    def halved(condition, scalar):
        return 1.0 - 0.5 * fmask(condition) * scalar

    inv_z = halved(inner_z, 1.0) * halved(first_z & (sub > 0), 1.0) * halved(last_z & (sub < 7), 1.0)
    inv_z = inv_z * halved(first_z & (sub == 0), present[2][-1]) * halved(last_z & (sub == 7), present[2][1])

    def average(half):
        planes = []
        for ey in EY[half]:
            lower = 1.0 if ey > 0 else present[1][-1]
            upper = 1.0 if ey < 3 else present[1][1]
            planes.append(inv_z * halved(lane_j == 0, lower) * halved(lane_j == 7, upper))
        scale = jnp.concatenate(planes, axis=0)
        scales = [scale] * 8
        scales[0] = scale * (1.0 - 0.5 * present[0][-1])
        scales[7] = scale * (1.0 - 0.5 * present[0][1])
        block = group(value, half) * jnp.stack(scales)[:, None]
        put_group(kept, half, block)
        return block

    def relax(half):
        return group(kept, half) + relaxation * group(value, half)

    fill_absent(1)
    fill_absent(2)

    for r, ready in ((0, average), (1, relax)):
        finish(r)
        faces = receive_early(r)
        pieces = forward_half(1, ready(1))
        for g in (0, 2, 3, 5):
            arrive(r, g)
        receive_late(r, faces)
        backward_half(1, pieces)
        backward_half(0, forward_half(0, ready(0)))
        ship(r + 1)

    def emit(half):
        block = value[:, 64 * half : 64 * half + 64, :].reshape(4, 2, 4, 16, 128)
        sides = jnp.concatenate([block[:, 0], block[:, 1]], axis=3).reshape(256, 256)
        high, low = split(sides)
        moved = jnp.dot(
            jnp.concatenate([high, low], axis=0), swap[...], preferred_element_type=F32
        ).astype(BF16)
        rows = jnp.concatenate([chosen[16 * half : 16 * half + 16], chosen[32 + 16 * half : 48 + 16 * half]], axis=0)
        unpick = jnp.concatenate([rows, rows], axis=0).T.astype(BF16)
        for f in range(4):
            columns = []
            for a in range(4):
                parts = []
                for n in (a * 64 + f * 16, 256 + a * 64 + f * 16):
                    parts += [moved[n : n + 16, :128], moved[n : n + 16, 128:]]
                columns.append(jnp.concatenate(parts, axis=0))
            stacked = jnp.concatenate(columns, axis=1)
            out = jnp.dot(unpick, stacked, preferred_element_type=F32)
            out_ref[f] = out if half == 1 else out_ref[f] + out

    finish(2)
    faces = receive_early(2)
    emit(1)
    for g in (0, 2, 3, 5):
        arrive(2, g)
    receive_late(2, faces)
    emit(0)


def shards(adjoint, load, displace, damage, history, frozen, order):
    forward, back, swap = (jnp.asarray(c) for c in constants())
    hbm = pl.BlockSpec(memory_space=pltpu.HBM)
    return pl.pallas_call(
        kernel,
        out_shape=pltpu.VMEM((4, 64, 512), F32),
        in_specs=[hbm] * 10,
        out_specs=pl.BlockSpec(memory_space=pltpu.VMEM),
        scratch_shapes=[
            pltpu.VMEM((4, 64, 512), BF16),
            pltpu.VMEM((4, 64, 512), BF16),
            pltpu.VMEM((3, 64, 512), BF16),
            pltpu.VMEM((64, 512), BF16),
            pltpu.VMEM((64, 512), BF16),
            pltpu.VMEM((1, 64), jnp.int32),
            pltpu.VMEM((1, 64), jnp.int32),
            pltpu.VMEM((384, 256), BF16),
            pltpu.VMEM((256, 256), BF16),
            pltpu.VMEM((256, 256), BF16),
            pltpu.VMEM((8, 128, 128), F32),
            pltpu.VMEM((8, 128, 128), F32),
            pltpu.VMEM((8, 128, 128), F32),
            pltpu.VMEM((8, 128, 128), F32),
            pltpu.VMEM((8, 8, 32, 128), F32),
            pltpu.VMEM((3, 8, 32, 128), F32),
            pltpu.VMEM((3, 2, 32, 128), F32),
            pltpu.VMEM((3, 2, 8, 128), F32),
            pltpu.VMEM((3, 2, 2, 64, 128), F32),
            pltpu.VMEM((3, 2, 32, 128), F32),
            pltpu.VMEM((3, 4, 8, 128), F32),
            pltpu.VMEM((3, 6, 8, 128), F32),
            pltpu.VMEM((3, 12, 8, 128), F32),
            pltpu.VMEM((64, 128), F32),
            pltpu.SemaphoreType.DMA((10,)),
            pltpu.SemaphoreType.DMA((3, 28)),
            pltpu.SemaphoreType.DMA((3, 6)),
        ],
        compiler_params=pltpu.CompilerParams(
            collective_id=0, has_side_effects=True, vmem_limit_bytes=56 * 1024 * 1024
        ),
    )(adjoint, load, displace, damage, history, frozen.reshape(1, 64), order, forward, back, swap)


def solution(mesh):
    in_specs = (
        P(None, ("gx", "gy", "gz"), None),
        P(None, ("gx", "gy", "gz"), None),
        P(None, ("gx", "gy", "gz"), None),
        P(("gx", "gy", "gz"), None),
        P(("gx", "gy", "gz"), None),
        P(("gx", "gy", "gz")),
        P(("gx", "gy", "gz"), None),
    )
    out_specs = P(None, ("gx", "gy", "gz"), None)
    return jax.shard_map(shards, mesh=mesh, in_specs=in_specs, out_specs=out_specs, check_vma=False)
```
